32 devices in a mesh: dp: 4 (over z), mp: 4 (over y, x), phase: 2 (over core).
Axes of the slice: x: 2, y: 2, z: 4, core: 2. Of those that a mesh axis runs over, the one named last changes fastest.
Arguments:
- item_owner: int32 [2048, 1], P('dp'), may hold values from 0 to 3; in each aligned block of 512 rows (0 to 511, 512 to 1023, ...) at most 224 rows name the same one
- item_row: int32 [2048], P('dp'), may hold values from 0 to 1023
- segments: int32 [4, 2, 256], P('dp'), may hold values from 0 to 31, never falling along the last dimension, each value on 1 to 128 neighbouring positions
- neighbors: int32 [4, 2, 256, 8], P('dp'), may hold values from 0 to 255
- table: bfloat16 [4096, 1024], P('dp'), may hold values from -6 to 6
- gains: bfloat16 [2, 1024], P('phase'), may hold values from 0.099609375 to 1.8984375
- w_in: bfloat16 [2, 1024, 4, 1024], P('phase', None, None, 'mp'), may hold values from -0.1875 to 0.1875
- w_out: bfloat16 [2, 1024, 1024], P('phase', 'mp'), may hold values from -0.1875 to 0.1875
- w_ctx: bfloat16 [1024, 1024], P(None, 'mp'), may hold values from -0.1875 to 0.1875
- ctx_bias: bfloat16 [1024], P('mp'), may hold values from -3 to 3
Outputs:
- user_states: bfloat16 [4, 2, 256, 1024], P('dp', 'phase')
- impression_context: bfloat16 [4, 2, 256, 1024], P('dp', 'phase', None, 'mp')
The draws below stay inside these ranges and needn't reach their ends.
Inputs may be any that keep to these rules, and one draw needn't show every extreme that they name: `item_owner`: among the rows of one index of dp, at most 224 name the same owner.
All inputs are finite; a program needn't handle non-finite values.
Results may differ from the reference program's by a relative error of at most 0.02.
Values may be sent and summed in bfloat16 or wider, within the bound.
No kernel may reach another device: no remote copies, remote signals or barrier semaphores. Data moves between devices by JAX's collectives and lax.ppermute only.
A program may use at most 64 MiB of HBM per device.

```python
import math
import jax
import jax.numpy as jnp
import numpy as np
from jax import lax

D = 1024
H = 8
HD = 128
NBR = 8
MBS = 2
MB_ROWS = 256
IMP = 256
TABLE_DEV = 1024
ROWS_DEV = 512
CAP = 224
N_DP = 4
N_MP = 4


def plant(values, rng, smallest, largest):
    longest = values.shape.index(max(values.shape))
    spots = []
    for shift in (0, 1):
        where = [jax.random.randint(jax.random.fold_in(rng, axis), (), 0, length) for axis, length in enumerate(values.shape)]
        where[longest] = (where[longest] + shift) % values.shape[longest]
        spots.append(tuple(where))
    return values.at[spots[0]].set(smallest).at[spots[1]].set(largest)


def levels(rng, dims, shards, smallest, top_value):
    factor_of, own = 1.0, jax.random.fold_in(rng, 6)
    for axis_at, parts in shards:
        draws = jnp.exp(jax.random.uniform(jax.random.fold_in(own, axis_at), (parts,), jnp.float32, smallest / len(shards), top_value / len(shards)))
        factor_of = factor_of * jnp.repeat(draws, dims[axis_at] // parts).reshape([-1 if axis == axis_at else 1 for axis in range(len(dims))])
    return factor_of


def split_up(amount, total, bound, slope):
    loads = [(1 << 20) // math.isqrt(grade ** slope) + 1 for grade in range(2, amount + 1)]
    spare, holding = total - bound - (amount - 1), [1] * (amount - 1)
    while spare > 0:
        movable = [i for i in range(amount - 1) if holding[i] < bound]
        whole, left = sum([loads[i] for i in movable]), spare
        for i in movable:
            more = min(bound - holding[i], max(1, left * loads[i] // whole), spare)
            holding[i] = holding[i] + more
            spare = spare - more
    return np.array([bound] + holding)


def uneven_parts(rng, number_of, total, bound, slope):
    if number_of == 2:
        one = jax.random.randint(rng, (), max(1, total - bound), min(bound, total - 1) + 1)
        return jnp.stack([one, total - one])
    lengths = jnp.asarray(split_up(number_of, total, bound, slope), jnp.int32)
    pairs = (number_of - 1) // 2
    source_of, sink = lengths[1:1 + 2 * pairs:2], lengths[2:2 + 2 * pairs:2]
    room = jnp.minimum(source_of - 1, bound - sink)
    shifted = jax.random.randint(jax.random.fold_in(rng, 1), (pairs,), 0, 1 << 20) % (room + 1)
    lengths = lengths.at[1:1 + 2 * pairs:2].set(source_of - shifted).at[2:2 + 2 * pairs:2].set(sink + shifted)
    return lengths[jax.random.permutation(jax.random.fold_in(rng, 2), number_of)]


def routed_block(stream_key, own, number, rows, count, top, most, slope):
    ranking = jax.random.permutation(stream_key, count)
    crowded, common = shares(count, rows * top, most, slope, True), shares(count, rows * top, most, slope, False)
    places = jnp.arange(count)

    def named(lengths, rotation):
        used = int((lengths > 0).sum())
        fixed = max(1, used // 4)
        passed = fixed + (places - fixed + rotation * (used - fixed)) % max(1, count - fixed)
        return jnp.zeros((count,), jnp.int32).at[ranking[jnp.where(places < fixed, places, passed)]].set(jnp.asarray(lengths, jnp.int32))

    lengths = jnp.where(number % 4 == 0, named(crowded, number // 4), named(common, number - number // 4 - 1))
    mixed = jax.random.permutation(jax.random.fold_in(own, 3), count)
    giver, receiver = mixed[0:count // 2 * 2:2], mixed[1:count // 2 * 2:2]
    margin = jnp.minimum(lengths[giver] - 1, most - lengths[receiver]) // 2
    margin = jnp.where((giver == ranking[0]) | (receiver == ranking[0]) | (lengths[receiver] == 0), 0, jnp.maximum(margin, 0))
    passed = jax.random.randint(jax.random.fold_in(own, 4), (count // 2,), 0, 1 << 20) % (margin + 1)
    lengths = lengths.at[giver].add(-passed).at[receiver].add(passed)
    labels = jnp.searchsorted(jnp.cumsum(lengths), jnp.arange(rows * top), side="right").astype(jnp.int32)
    table = labels.reshape(top, rows).T
    table = table[jax.random.permutation(jax.random.fold_in(own, 1), rows)]
    rotation = jax.random.randint(jax.random.fold_in(own, 2), (rows, 1), 0, top)
    return jnp.take_along_axis(table, (jnp.arange(top)[None, :] + rotation) % top, axis=1)


def shares(amount, total, limit, lean, full):
    weights = [(1 << 20) // math.isqrt(grade ** lean) + 1 for grade in range(1, amount + 1)]
    largest = limit if full else min(limit, max(-(-total // amount), total * weights[0] // sum(weights)))
    least = 1 if total - largest >= amount - 1 else 0
    given, spare = [largest] + [least] * (amount - 1), total - largest - least * (amount - 1)
    while spare > 0:
        free = [i for i in range(1, amount) if given[i] < largest] or [i for i in range(1, amount) if given[i] < limit]
        pool, left = sum([weights[i] for i in free]), spare
        for i in free:
            more = min(limit - given[i], max(1, left * weights[i] // pool), spare)
            given[i] = given[i] + more
            spare = spare - more
    return np.array(given)


def noise(rng, extent, spread, limit, cuts=(), kind=jnp.bfloat16):
    values = jax.random.normal(rng, extent, jnp.float32) * spread
    if len(cuts) > 0:
        values = levels(rng, extent, cuts, -0.22, 0.18) * values
    return jnp.clip(values, min=-limit, max=limit).astype(kind)


def setup_inputs(seed: int = 0) -> dict:
    splits = jax.random.split(jax.random.key(seed), 11)
    item_owner_keys = jax.random.split(jax.random.fold_in(splits[0], 1), (N_DP * ROWS_DEV) // ROWS_DEV)
    item_owner_turns = jax.random.permutation(jax.random.fold_in(splits[0], 3), (N_DP * ROWS_DEV) // ROWS_DEV)
    item_owner = jax.vmap(lambda own, number: routed_block(jax.random.fold_in(splits[0], 2), own, number, ROWS_DEV, N_DP, 1, CAP, 2))(item_owner_keys, item_owner_turns).reshape((N_DP * ROWS_DEV, 1))
    item_row = plant(jax.random.randint(splits[1], (N_DP * ROWS_DEV,), 0, TABLE_DEV), jax.random.fold_in(splits[1], 1), 0, TABLE_DEV - 1).astype(jnp.int32)
    segments = jax.vmap(lambda own: jnp.searchsorted(jnp.cumsum(uneven_parts(own, MB_ROWS // 8, MB_ROWS, MB_ROWS // 2, 2)), jnp.arange(MB_ROWS), side="right"))(jax.random.split(splits[2], N_DP * MBS)).reshape((N_DP, MBS, MB_ROWS)).astype(jnp.int32)
    neighbors = plant(jax.random.randint(splits[3], (N_DP, MBS, IMP, NBR), 0, MB_ROWS), jax.random.fold_in(splits[3], 1), 0, MB_ROWS - 1).astype(jnp.int32)
    table = noise(splits[4], (N_DP * TABLE_DEV, D), 1.0, 6.0, ((0, 4),))
    gains = jnp.clip(1.0 + 0.18 * jax.random.normal(splits[5], (2, D), jnp.float32), 0.099609375, 1.8984375).astype(jnp.bfloat16)
    w_in = noise(splits[6], (2, D, 4, H * HD), D ** -0.5, 0.1875, ((0, 2), (3, 4)))
    w_out = noise(splits[7], (2, H * HD, D), (H * HD) ** -0.5, 0.1875, ((0, 2), (1, 4)))
    w_ctx = noise(splits[8], (D, D), D ** -0.5, 0.1875, ((1, 4),))
    ctx_bias = noise(splits[9], (D,), 0.5, 3.0, ((0, 4),))
    return {"item_owner": item_owner, "item_row": item_row, "segments": segments, "neighbors": neighbors, "table": table, "gains": gains, "w_in": w_in, "w_out": w_out, "w_ctx": w_ctx, "ctx_bias": ctx_bias}


norm_eps = 1e-06

def hstu_layer(acts, seg_ids, gain, w_proj, w_back):
    rows_n = acts.shape[0]
    acts_f = acts.astype(jnp.float32)
    inv_rms = lax.rsqrt(lax.optimization_barrier(jnp.mean(acts_f * acts_f, axis=-1, keepdims=True)) + norm_eps)
    normed = (acts_f * inv_rms * gain.astype(jnp.float32)).astype(jnp.bfloat16)
    projected = jnp.dot(normed, w_proj.reshape(D, 4 * H * HD), preferred_element_type=jnp.float32)
    projected = jax.nn.silu(projected).astype(jnp.bfloat16).reshape(rows_n, 4, H, HD)
    gates_u = projected[:, 0].astype(jnp.float32)
    values_h = projected[:, 1].astype(jnp.float32)
    queries = projected[:, 2].astype(jnp.float32)
    keys_h = projected[:, 3].astype(jnp.float32)
    scores = jnp.einsum('qhd,khd->hqk', queries, keys_h) * HD ** (-0.5)
    position = jnp.arange(rows_n)
    allowed = (position[None, :] <= position[:, None]) & (seg_ids[:, None] == seg_ids[None, :])
    weights = (jnp.where(allowed[None], jax.nn.silu(scores), 0.0) / MB_ROWS).astype(jnp.bfloat16)
    mixed = jnp.einsum('hqk,khd->qhd', weights.astype(jnp.float32), values_h)
    mixed = mixed * lax.rsqrt(lax.optimization_barrier(jnp.mean(mixed * mixed, axis=-1, keepdims=True)) + norm_eps)
    group_cols = H * HD // N_MP
    gated = (mixed * gates_u).astype(jnp.bfloat16).reshape(rows_n, N_MP, group_cols).astype(jnp.float32)
    partial_terms = jnp.einsum('rjc,jcd->jrd', gated, w_back.reshape(N_MP, group_cols, D).astype(jnp.float32))
    partial_terms = lax.optimization_barrier(partial_terms.astype(jnp.bfloat16)).astype(jnp.float32)
    return (acts_f + lax.optimization_barrier(jnp.sum(partial_terms, axis=0))).astype(jnp.bfloat16)

def context_score(states, neigh_rows, w_ctx, ctx_bias):
    picked = jnp.take(states, neigh_rows.reshape(-1), axis=0).astype(jnp.float32)
    context = lax.optimization_barrier(jnp.mean(picked.reshape(neigh_rows.shape[0], NBR, D), axis=1)).astype(jnp.bfloat16)
    summed = jnp.dot(context, w_ctx, preferred_element_type=jnp.float32) + ctx_bias.astype(jnp.float32)
    return jax.nn.silu(summed).astype(jnp.bfloat16)

def reference(item_owner, item_row, segments, neighbors, table, gains, w_in, w_out, w_ctx, ctx_bias):
    item_ids = (item_owner[:, 0] * TABLE_DEV + item_row).astype(jnp.int32)
    acts_all = jnp.take(table, item_ids, axis=0).reshape(N_DP, MBS, MB_ROWS, D)

    def one_batch(packed):
        acts_m, seg_m, neigh_m = packed
        first = hstu_layer(acts_m, seg_m, gains[0], w_in[0], w_out[0])
        second = hstu_layer(first, seg_m, gains[1], w_in[1], w_out[1])
        return (second, context_score(second, neigh_m, w_ctx, ctx_bias))

    def one_group(packed):
        return lax.map(one_batch, packed)
    return lax.map(one_group, (acts_all, segments, neighbors))
```

```python
import functools

import jax
import jax.numpy as jnp
from jax import lax
from jax.experimental import pallas as pl
from jax.experimental.pallas import tpu as pltpu
from jax.sharding import PartitionSpec as P

HD = 128
NBR = 8
LANES = 128
EPS = 1e-06
VMEM_LIMIT = 48 * 1024 * 1024
VMEM = pl.BlockSpec(memory_space=pltpu.VMEM)
ANY = pl.BlockSpec(memory_space=pl.ANY)
SMEM = pl.BlockSpec(memory_space=pltpu.SMEM)
F32 = jnp.float32
BF16 = jnp.bfloat16


def params():
    return pltpu.CompilerParams(vmem_limit_bytes=VMEM_LIMIT)


def is_pow2(n):
    return n & (n - 1) == 0


def source_of(me, k, n):
    return me ^ k if is_pow2(n) else lax.rem(me + n - k, n)


def exchange(value, axis, k):
    n = lax.axis_size(axis)
    pairs = [(i, i ^ k if is_pow2(n) else (i + k) % n) for i in range(n)]
    return lax.ppermute(value, axis, pairs)


def spread(value, axis):
    return [value] + [exchange(value, axis, k) for k in range(1, lax.axis_size(axis))]


def columns_of(row, count):
    return jnp.transpose(jnp.broadcast_to(row, (count, row.shape[1])))


def fetch_kernel(steps, pos_ref, *refs):
    idx_refs, table_ref = refs[:steps], refs[steps]
    out_refs = refs[steps + 1 : 2 * steps + 1]
    tab, sem = refs[2 * steps + 1 :]
    width = tab.shape[1]
    copy = pltpu.make_async_copy(
        table_ref.at[:, pl.ds(pl.multiple_of(pos_ref[1] * width, width), width)], tab, sem
    )
    copy.start()
    first = pos_ref[0] * tab.shape[0]
    hots = []
    for idx_ref in idx_refs:
        cols = columns_of(idx_ref[...] - first, LANES)
        lane = lax.broadcasted_iota(jnp.int32, cols.shape, 1)
        hots.append(
            jnp.concatenate(
                [
                    jnp.where(cols == lane + c, 1.0, 0.0).astype(BF16)
                    for c in range(0, tab.shape[0], LANES)
                ],
                axis=1,
            )
        )
    copy.wait()
    for hot, out_ref in zip(hots, out_refs):
        out_ref[...] = jnp.dot(hot, tab[...], preferred_element_type=F32).astype(BF16)


def fetch(pos, idx_rows, table, width):
    steps = len(idx_rows)
    rows = idx_rows[0].shape[1]
    return pl.pallas_call(
        functools.partial(fetch_kernel, steps),
        out_shape=[jax.ShapeDtypeStruct((rows, width), BF16)] * steps,
        in_specs=[SMEM] + [VMEM] * steps + [ANY],
        out_specs=[VMEM] * steps,
        scratch_shapes=[pltpu.VMEM((table.shape[0], width), BF16), pltpu.SemaphoreType.DMA],
        compiler_params=params(),
        cost_estimate=pl.CostEstimate(
            flops=2 * steps * rows * width * table.shape[0],
            bytes_accessed=2 * width * table.shape[0],
            transcendentals=0,
        ),
        name="fetch",
    )(pos, *idx_rows, table)


def silu(x):
    return x * jax.nn.sigmoid(x)


def start_picked(section, phase, own, other, dst, sem):
    @pl.when(phase == section)
    def _():
        pltpu.make_async_copy(own, dst, sem).start()

    @pl.when(phase != section)
    def _():
        pltpu.make_async_copy(other, dst, sem).start()


def wait_picked(own, dst, sem):
    pltpu.make_async_copy(own, dst, sem).wait()


def front(x, gain, seg, w_own, w_buf, w_sem, gated_ref):
    rows, local_cols = x.shape[0], w_buf.shape[2]
    inv = lax.rsqrt(jnp.mean(x * x, axis=-1, keepdims=True) + EPS)
    normed = (x * inv * gain.astype(F32)).astype(BF16)
    proj = []
    for g in range(4):
        wait_picked(w_own.at[g], w_buf.at[g], w_sem.at[g])
        proj.append(
            silu(jnp.dot(normed, w_buf[g], preferred_element_type=F32)).astype(BF16)
        )
    gates, values, queries, keys = proj
    seg_cols = columns_of(seg, rows)
    at_row = lax.broadcasted_iota(jnp.int32, (rows, rows), 0)
    at_col = lax.broadcasted_iota(jnp.int32, (rows, rows), 1)
    allowed = (at_col <= at_row) & (seg_cols == seg)
    for h in range(0, local_cols, HD):
        head = slice(h, h + HD)
        scores = lax.dot_general(
            queries[:, head], keys[:, head], (((1,), (1,)), ((), ())), preferred_element_type=F32
        ) * HD ** (-0.5)
        weights = (jnp.where(allowed, silu(scores), 0.0) / rows).astype(BF16)
        mixed = jnp.dot(weights, values[:, head], preferred_element_type=F32)
        mixed = mixed * lax.rsqrt(jnp.mean(mixed * mixed, axis=-1, keepdims=True) + EPS)
        gated_ref[:, head] = (mixed * gates[:, head].astype(F32)).astype(BF16)


def back(x, gated_refs, o_own, o_buf, o_sem):
    total = x.astype(F32)
    for k, gated_ref in enumerate(gated_refs):
        wait_picked(o_own[k], o_buf.at[k], o_sem.at[k])
        part = jnp.dot(gated_ref[...], o_buf[k], preferred_element_type=F32)
        total = total + part.astype(BF16).astype(F32)
    return total.astype(BF16)


def first_kernel(steps, pos_ref, *refs):
    x_refs = refs[:steps]
    gain_ref, seg_ref, w_own, w_other, gated_ref, x_ref, w_buf, w_sem = refs[steps:]
    for g in range(4):
        start_picked(0, pos_ref[2], w_own.at[g], w_other.at[g], w_buf.at[g], w_sem.at[g])
    width = x_refs[0].shape[1]
    for k, piece in enumerate(x_refs):
        at = pl.multiple_of(source_of(pos_ref[1], k, steps) * width, width)
        x_ref[:, pl.ds(at, width)] = piece[...]
    front(x_ref[...].astype(F32), gain_ref[...], seg_ref[...], w_own, w_buf, w_sem, gated_ref)


def middle_kernel(steps, pos_ref, *refs):
    gated_refs, o_own, o_other = refs[:steps], refs[steps : 2 * steps], refs[2 * steps : 3 * steps]
    x_ref, gain_ref, seg_ref, w_own, w_other, gated_ref, x1_ref = refs[3 * steps : 3 * steps + 7]
    o_buf, o_sem, w_buf, w_sem = refs[3 * steps + 7 :]
    for k in range(steps):
        start_picked(0, pos_ref[2], o_own[k], o_other[k], o_buf.at[k], o_sem.at[k])
    for g in range(4):
        start_picked(1, pos_ref[2], w_own.at[g], w_other.at[g], w_buf.at[g], w_sem.at[g])
    x1 = back(x_ref[...], gated_refs, o_own, o_buf, o_sem)
    x1_ref[...] = x1
    front(x1.astype(F32), gain_ref[...], seg_ref[...], w_own, w_buf, w_sem, gated_ref)


def last_kernel(steps, pos_ref, *refs):
    gated_refs, o_own, o_other = refs[:steps], refs[steps : 2 * steps], refs[2 * steps : 3 * steps]
    x_ref, neigh_ref, w_ref, bias_ref, states_ref, ctx_ref = refs[3 * steps : 3 * steps + 6]
    o_buf, o_sem = refs[3 * steps + 6 :]
    for k in range(steps):
        start_picked(1, pos_ref[2], o_own[k], o_other[k], o_buf.at[k], o_sem.at[k])
    rows, imps = x_ref.shape[0], neigh_ref.shape[0]
    lane = lax.broadcasted_iota(jnp.int32, (imps, rows), 1)
    share = jnp.zeros((imps, rows), F32)
    for n in range(NBR):
        share = share + jnp.where(neigh_ref[:, n : n + 1] == lane, 1.0 / NBR, 0.0)
    states = back(x_ref[...], gated_refs, o_own, o_buf, o_sem)
    states_ref[...] = states
    context = jnp.dot(share.astype(BF16), states, preferred_element_type=F32).astype(BF16)
    summed = jnp.dot(context, w_ref[...], preferred_element_type=F32) + bias_ref[...].astype(F32)
    ctx_ref[...] = silu(summed).astype(BF16)


def section_flops(rows, width, local_cols):
    return 2 * rows * (width * 4 * local_cols + 2 * rows * local_cols)


def fetch_rows_padded(owners, item_row, table, width):
    dp_count = lax.axis_size("dp")
    row_total = item_row.shape[0]
    capacity = max(2, 7 * row_total // (4 * dp_count))
    hits = (owners[:, None] == jnp.arange(dp_count, dtype=jnp.int32)[None, :]).astype(jnp.int32)
    rank = jnp.sum((jnp.cumsum(hits, axis=0) - 1) * hits, axis=1)
    slot = owners * capacity + rank
    requests = jnp.full((dp_count * capacity,), -1, jnp.int32).at[slot].set(item_row)
    requests = requests.reshape(dp_count, capacity)
    asked = lax.all_to_all(requests, "dp", split_axis=0, concat_axis=0, tiled=True)
    part = lax.dynamic_slice_in_dim(table, lax.axis_index("mp") * width, width, 1)
    found = jnp.take(part, jnp.maximum(asked, 0), axis=0)
    fetched = lax.all_to_all(found, "dp", split_axis=0, concat_axis=0, tiled=True)
    return fetched.reshape(dp_count * capacity, width)[slot]


def on_device(
    item_owner, item_row, segments, neighbors, table, gains, w_in, w_out, w_ctx, ctx_bias
):
    dp_count, mp_count = lax.axis_size("dp"), lax.axis_size("mp")
    dp_at, mp_at, phase = lax.axis_index("dp"), lax.axis_index("mp"), lax.axis_index("phase")
    pos = jnp.stack([dp_at, mp_at, phase]).astype(jnp.int32)
    table_rows, width = table.shape
    batches, rows = segments.shape[1], segments.shape[2]
    imps = neighbors.shape[2]
    local_cols = w_out.shape[1]
    part = width // mp_count

    w_own = jnp.transpose(w_in[0], (1, 0, 2))
    w_other = exchange(w_own, "phase", 1)
    o_own = spread(w_out[0], "mp")
    o_other = [exchange(piece, "phase", 1) for piece in o_own]
    gain_other = exchange(gains, "phase", 1)
    gain0 = jnp.where(phase == 0, gains, gain_other)
    gain1 = jnp.where(phase == 0, gain_other, gains)
    seg = lax.dynamic_index_in_dim(segments[0], phase, 0, keepdims=True)
    neigh = lax.dynamic_index_in_dim(neighbors[0], phase, 0, keepdims=False)

    if is_pow2(dp_count) and dp_count <= 8:
        wanted = (item_owner[:, 0] * table_rows + item_row).reshape(batches, rows)
        wanted = lax.dynamic_index_in_dim(wanted, phase, 0, keepdims=True)
        found = fetch(pos, spread(wanted, "dp"), table, part)
        piece = found[0]
        for k in range(1, dp_count):
            piece = piece + exchange(found[k], "dp", k)
    else:
        piece = fetch_rows_padded(item_owner[:, 0], item_row, table, part)
        piece = lax.dynamic_index_in_dim(
            piece.reshape(batches, rows, part), phase, 0, keepdims=False
        )
    x_pieces = spread(piece, "mp")

    sem4 = pltpu.SemaphoreType.DMA((4,))
    semk = pltpu.SemaphoreType.DMA((mp_count,))
    w_buf = pltpu.VMEM((4, width, local_cols), BF16)
    o_buf = pltpu.VMEM((mp_count, local_cols, width), BF16)
    x_shape = jax.ShapeDtypeStruct((rows, width), BF16)
    gated_shape = jax.ShapeDtypeStruct((rows, local_cols), BF16)
    front_flops = section_flops(rows, width, local_cols)
    back_flops = 2 * rows * width * local_cols * mp_count

    gated, x0 = pl.pallas_call(
        functools.partial(first_kernel, mp_count),
        out_shape=[gated_shape, x_shape],
        in_specs=[SMEM] + [VMEM] * (mp_count + 2) + [ANY] * 2,
        out_specs=[VMEM] * 2,
        scratch_shapes=[w_buf, sem4],
        compiler_params=params(),
        cost_estimate=pl.CostEstimate(
            flops=front_flops, bytes_accessed=8 * width * local_cols, transcendentals=0
        ),
        name="section0_front",
    )(pos, *x_pieces, gain0, seg, w_own, w_other)

    gated, x1 = pl.pallas_call(
        functools.partial(middle_kernel, mp_count),
        out_shape=[gated_shape, x_shape],
        in_specs=[SMEM] + [VMEM] * mp_count + [ANY] * (2 * mp_count) + [VMEM] * 3 + [ANY] * 2,
        out_specs=[VMEM] * 2,
        scratch_shapes=[o_buf, semk, w_buf, sem4],
        compiler_params=params(),
        cost_estimate=pl.CostEstimate(
            flops=front_flops + back_flops,
            bytes_accessed=(8 + 2 * mp_count) * width * local_cols,
            transcendentals=0,
        ),
        name="section0_back_section1_front",
    )(pos, *spread(gated, "mp"), *o_own, *o_other, x0, gain1, seg, w_own, w_other)

    states, ctx = pl.pallas_call(
        functools.partial(last_kernel, mp_count),
        out_shape=[x_shape, jax.ShapeDtypeStruct((imps, w_ctx.shape[1]), BF16)],
        in_specs=[SMEM] + [VMEM] * mp_count + [ANY] * (2 * mp_count) + [VMEM] * 4,
        out_specs=[VMEM] * 2,
        scratch_shapes=[o_buf, semk],
        compiler_params=params(),
        cost_estimate=pl.CostEstimate(
            flops=back_flops + 2 * imps * width * (rows + w_ctx.shape[1]),
            bytes_accessed=2 * mp_count * width * local_cols,
            transcendentals=0,
        ),
        name="section1_back_context",
    )(pos, *spread(gated, "mp"), *o_own, *o_other, x1, neigh, w_ctx, ctx_bias[None])

    return (
        states.reshape(1, 1, rows, width),
        ctx.reshape(1, 1, imps, w_ctx.shape[1]),
    )


def solution(mesh):
    in_specs = (
        P("dp", None),
        P("dp"),
        P("dp", None, None),
        P("dp", None, None, None),
        P("dp", None),
        P("phase", None),
        P("phase", None, None, "mp"),
        P("phase", "mp", None),
        P(None, "mp"),
        P("mp"),
    )
    out_specs = (P("dp", "phase", None, None), P("dp", "phase", None, "mp"))
    return jax.shard_map(
        on_device, mesh=mesh, in_specs=in_specs, out_specs=out_specs, check_vma=False
    )
```

```python
import functools

import jax
import jax.numpy as jnp
from jax import lax
from jax.experimental import pallas as pl
from jax.experimental.pallas import tpu as pltpu
from jax.sharding import PartitionSpec as P

HD = 128
NBR = 8
LANES = 128
EPS = 1e-06
VMEM_LIMIT = 20 * 1024 * 1024
VMEM = pl.BlockSpec(memory_space=pltpu.VMEM)
HBM = pl.BlockSpec(memory_space=pltpu.HBM)
F32 = jnp.float32
BF16 = jnp.bfloat16


def params():
    return pltpu.CompilerParams(vmem_limit_bytes=VMEM_LIMIT)


def is_pow2(n):
    return n & (n - 1) == 0


def source_of(me, k, n):
    return me ^ k if is_pow2(n) else lax.rem(me + n - k, n)


def exchange(value, axis, k):
    n = lax.axis_size(axis)
    pairs = [(i, i ^ k if is_pow2(n) else (i + k) % n) for i in range(n)]
    return lax.ppermute(value, axis, pairs)


def spread(value, axis):
    return [value] + [exchange(value, axis, k) for k in range(1, lax.axis_size(axis))]


def columns_of(row, count):
    return jnp.transpose(jnp.broadcast_to(row, (count, row.shape[1])))


def fetch_kernel(steps, *refs):
    idx_refs, table_ref = refs[:steps], refs[steps]
    out_refs = refs[steps + 1 : 2 * steps + 1]
    tab, sem = refs[2 * steps + 1 :]
    width = tab.shape[1]
    at = pl.multiple_of(lax.axis_index("mp") * width, width)
    copy = pltpu.make_async_copy(table_ref.at[:, pl.ds(at, width)], tab, sem)
    copy.start()
    first = lax.axis_index("dp") * tab.shape[0]
    hots = []
    for idx_ref in idx_refs:
        cols = columns_of(idx_ref[...] - first, LANES)
        lane = lax.broadcasted_iota(jnp.int32, cols.shape, 1)
        hots.append(
            jnp.concatenate(
                [
                    jnp.where(cols == lane + c, 1.0, 0.0).astype(BF16)
                    for c in range(0, tab.shape[0], LANES)
                ],
                axis=1,
            )
        )
    copy.wait()
    for hot, out_ref in zip(hots, out_refs):
        out_ref[...] = jnp.dot(hot, tab[...], preferred_element_type=F32).astype(BF16)


def fetch(idx_rows, table, width):
    steps = len(idx_rows)
    rows = idx_rows[0].shape[1]
    return pl.pallas_call(
        functools.partial(fetch_kernel, steps),
        out_shape=[jax.ShapeDtypeStruct((rows, width), BF16)] * steps,
        in_specs=[VMEM] * steps + [HBM],
        out_specs=[VMEM] * steps,
        scratch_shapes=[pltpu.VMEM((table.shape[0], width), BF16), pltpu.SemaphoreType.DMA],
        compiler_params=params(),
        cost_estimate=pl.CostEstimate(
            flops=2 * steps * rows * width * table.shape[0],
            bytes_accessed=2 * width * table.shape[0],
            transcendentals=0,
        ),
        name="fetch",
    )(*idx_rows, table)


def silu(x):
    return x * jax.nn.sigmoid(x)


def start_picked(section, own, other, dst, sem):
    phase = lax.axis_index("phase")

    @pl.when(phase == section)
    def _():
        pltpu.make_async_copy(own, dst, sem).start()

    @pl.when(phase != section)
    def _():
        pltpu.make_async_copy(other, dst, sem).start()


def wait_picked(own, dst, sem):
    pltpu.make_async_copy(own, dst, sem).wait()


def back_copy(section, k, steps, o_all, o_buf, o_sem):
    cols = o_buf.shape[1]
    at = (section * steps + source_of(lax.axis_index("mp"), k, steps)) * cols
    return pltpu.make_async_copy(
        o_all.at[pl.ds(pl.multiple_of(at, cols), cols), :], o_buf.at[k], o_sem.at[k]
    )


def front(x, gain, seg, w_own, w_buf, w_sem, gated_ref):
    rows, local_cols = x.shape[0], w_buf.shape[2]
    inv = lax.rsqrt(jnp.mean(x * x, axis=-1, keepdims=True) + EPS)
    normed = (x * inv * gain.astype(F32)).astype(BF16)
    proj = []
    for g in range(4):
        wait_picked(w_own.at[g], w_buf.at[g], w_sem.at[g])
        proj.append(
            silu(jnp.dot(normed, w_buf[g], preferred_element_type=F32)).astype(BF16)
        )
    gates, values, queries, keys = proj
    seg_cols = columns_of(seg, rows)
    at_row = lax.broadcasted_iota(jnp.int32, (rows, rows), 0)
    at_col = lax.broadcasted_iota(jnp.int32, (rows, rows), 1)
    allowed = (at_col <= at_row) & (seg_cols == seg)
    for h in range(0, local_cols, HD):
        head = slice(h, h + HD)
        scores = lax.dot_general(
            queries[:, head], keys[:, head], (((1,), (1,)), ((), ())), preferred_element_type=F32
        ) * HD ** (-0.5)
        weights = (jnp.where(allowed, silu(scores), 0.0) / rows).astype(BF16)
        mixed = jnp.dot(weights, values[:, head], preferred_element_type=F32)
        mixed = mixed * lax.rsqrt(jnp.mean(mixed * mixed, axis=-1, keepdims=True) + EPS)
        gated_ref[:, head] = (mixed * gates[:, head].astype(F32)).astype(BF16)


def back(x, section, gated_refs, o_all, o_buf, o_sem):
    total = x.astype(F32)
    for k, gated_ref in enumerate(gated_refs):
        back_copy(section, k, len(gated_refs), o_all, o_buf, o_sem).wait()
        part = jnp.dot(gated_ref[...], o_buf[k], preferred_element_type=F32)
        total = total + part.astype(BF16).astype(F32)
    return total.astype(BF16)


def first_kernel(steps, *refs):
    x_refs = refs[:steps]
    gain_ref, seg_ref, w_own, w_other, gated_ref, x_ref, w_buf, w_sem = refs[steps:]
    for g in range(4):
        start_picked(0, w_own.at[g], w_other.at[g], w_buf.at[g], w_sem.at[g])
    width = x_refs[0].shape[1]
    for k, piece in enumerate(x_refs):
        at = pl.multiple_of(source_of(lax.axis_index("mp"), k, steps) * width, width)
        x_ref[:, pl.ds(at, width)] = piece[...]
    front(x_ref[...].astype(F32), gain_ref[...], seg_ref[...], w_own, w_buf, w_sem, gated_ref)


def middle_kernel(steps, *refs):
    gated_refs = refs[:steps]
    o_all, x_ref, gain_ref, seg_ref, w_own, w_other, gated_ref, x1_ref = refs[steps : steps + 8]
    o_buf, o_sem, w_buf, w_sem = refs[steps + 8 :]
    for k in range(steps):
        back_copy(0, k, steps, o_all, o_buf, o_sem).start()
    for g in range(4):
        start_picked(1, w_own.at[g], w_other.at[g], w_buf.at[g], w_sem.at[g])
    x1 = back(x_ref[...], 0, gated_refs, o_all, o_buf, o_sem)
    x1_ref[...] = x1
    front(x1.astype(F32), gain_ref[...], seg_ref[...], w_own, w_buf, w_sem, gated_ref)


def last_kernel(steps, *refs):
    gated_refs = refs[:steps]
    o_all, x_ref, neigh_ref, w_ref, bias_ref, states_ref, ctx_ref = refs[steps : steps + 7]
    o_buf, o_sem = refs[steps + 7 :]
    for k in range(steps):
        back_copy(1, k, steps, o_all, o_buf, o_sem).start()
    rows, imps = x_ref.shape[0], neigh_ref.shape[0]
    lane = lax.broadcasted_iota(jnp.int32, (imps, rows), 1)
    share = jnp.zeros((imps, rows), F32)
    for n in range(NBR):
        share = share + jnp.where(neigh_ref[:, n : n + 1] == lane, 1.0 / NBR, 0.0)
    states = back(x_ref[...], 1, gated_refs, o_all, o_buf, o_sem)
    states_ref[...] = states
    context = jnp.dot(share.astype(BF16), states, preferred_element_type=F32).astype(BF16)
    summed = jnp.dot(context, w_ref[...], preferred_element_type=F32) + bias_ref[...].astype(F32)
    ctx_ref[...] = silu(summed).astype(BF16)


def section_flops(rows, width, local_cols):
    return 2 * rows * (width * 4 * local_cols + 2 * rows * local_cols)


def fetch_rows_padded(owners, item_row, table, width):
    dp_count = lax.axis_size("dp")
    row_total = item_row.shape[0]
    capacity = max(2, 7 * row_total // (4 * dp_count))
    hits = (owners[:, None] == jnp.arange(dp_count, dtype=jnp.int32)[None, :]).astype(jnp.int32)
    rank = jnp.sum((jnp.cumsum(hits, axis=0) - 1) * hits, axis=1)
    slot = owners * capacity + rank
    requests = jnp.full((dp_count * capacity,), -1, jnp.int32).at[slot].set(item_row)
    requests = requests.reshape(dp_count, capacity)
    asked = lax.all_to_all(requests, "dp", split_axis=0, concat_axis=0, tiled=True)
    part = lax.dynamic_slice_in_dim(table, lax.axis_index("mp") * width, width, 1)
    found = jnp.take(part, jnp.maximum(asked, 0), axis=0)
    fetched = lax.all_to_all(found, "dp", split_axis=0, concat_axis=0, tiled=True)
    return fetched.reshape(dp_count * capacity, width)[slot]


def on_device(
    item_owner, item_row, segments, neighbors, table, gains, w_in, w_out, w_ctx, ctx_bias
):
    dp_count, mp_count = lax.axis_size("dp"), lax.axis_size("mp")
    phase = lax.axis_index("phase")
    table_rows, width = table.shape
    batches, rows = segments.shape[1], segments.shape[2]
    imps = neighbors.shape[2]
    local_cols = w_out.shape[1]
    part = width // mp_count

    w_own = jnp.transpose(w_in[0], (1, 0, 2))
    w_other = exchange(w_own, "phase", 1)
    o_all = lax.all_gather(w_out[0], ("phase", "mp"), axis=0, tiled=True)
    gain_other = exchange(gains, "phase", 1)
    gain0 = jnp.where(phase == 0, gains, gain_other)
    gain1 = jnp.where(phase == 0, gain_other, gains)
    seg = lax.dynamic_index_in_dim(segments[0], phase, 0, keepdims=True)
    neigh = lax.dynamic_index_in_dim(neighbors[0], phase, 0, keepdims=False)

    if is_pow2(dp_count) and dp_count <= 8:
        wanted = (item_owner[:, 0] * table_rows + item_row).reshape(batches, rows)
        wanted = lax.dynamic_index_in_dim(wanted, phase, 0, keepdims=True)
        found = fetch(spread(wanted, "dp"), table, part)
        piece = found[0]
        for k in range(1, dp_count):
            piece = piece + exchange(found[k], "dp", k)
    else:
        piece = fetch_rows_padded(item_owner[:, 0], item_row, table, part)
        piece = lax.dynamic_index_in_dim(
            piece.reshape(batches, rows, part), phase, 0, keepdims=False
        )
    x_pieces = spread(piece, "mp")

    sem4 = pltpu.SemaphoreType.DMA((4,))
    semk = pltpu.SemaphoreType.DMA((mp_count,))
    w_buf = pltpu.VMEM((4, width, local_cols), BF16)
    o_buf = pltpu.VMEM((mp_count, local_cols, width), BF16)
    x_shape = jax.ShapeDtypeStruct((rows, width), BF16)
    gated_shape = jax.ShapeDtypeStruct((rows, local_cols), BF16)
    front_flops = section_flops(rows, width, local_cols)
    back_flops = 2 * rows * width * local_cols * mp_count

    gated, x0 = pl.pallas_call(
        functools.partial(first_kernel, mp_count),
        out_shape=[gated_shape, x_shape],
        in_specs=[VMEM] * (mp_count + 2) + [HBM] * 2,
        out_specs=[VMEM] * 2,
        scratch_shapes=[w_buf, sem4],
        compiler_params=params(),
        cost_estimate=pl.CostEstimate(
            flops=front_flops, bytes_accessed=8 * width * local_cols, transcendentals=0
        ),
        name="section0_front",
    )(*x_pieces, gain0, seg, w_own, w_other)

    gated, x1 = pl.pallas_call(
        functools.partial(middle_kernel, mp_count),
        out_shape=[gated_shape, x_shape],
        in_specs=[VMEM] * mp_count + [HBM] + [VMEM] * 3 + [HBM] * 2,
        out_specs=[VMEM] * 2,
        scratch_shapes=[o_buf, semk, w_buf, sem4],
        compiler_params=params(),
        cost_estimate=pl.CostEstimate(
            flops=front_flops + back_flops,
            bytes_accessed=(8 + 2 * mp_count) * width * local_cols,
            transcendentals=0,
        ),
        name="section0_back_section1_front",
    )(*spread(gated, "mp"), o_all, x0, gain1, seg, w_own, w_other)

    states, ctx = pl.pallas_call(
        functools.partial(last_kernel, mp_count),
        out_shape=[x_shape, jax.ShapeDtypeStruct((imps, w_ctx.shape[1]), BF16)],
        in_specs=[VMEM] * mp_count + [HBM] + [VMEM] * 4,
        out_specs=[VMEM] * 2,
        scratch_shapes=[o_buf, semk],
        compiler_params=params(),
        cost_estimate=pl.CostEstimate(
            flops=back_flops + 2 * imps * width * (rows + w_ctx.shape[1]),
            bytes_accessed=2 * mp_count * width * local_cols,
            transcendentals=0,
        ),
        name="section1_back_context",
    )(*spread(gated, "mp"), o_all, x1, neigh, w_ctx, ctx_bias[None])

    return (
        states.reshape(1, 1, rows, width),
        ctx.reshape(1, 1, imps, w_ctx.shape[1]),
    )


def solution(mesh):
    in_specs = (
        P("dp", None),
        P("dp"),
        P("dp", None, None),
        P("dp", None, None, None),
        P("dp", None),
        P("phase", None),
        P("phase", None, None, "mp"),
        P("phase", "mp", None),
        P(None, "mp"),
        P("mp"),
    )
    out_specs = (P("dp", "phase", None, None), P("dp", "phase", None, "mp"))
    return jax.shard_map(
        on_device, mesh=mesh, in_specs=in_specs, out_specs=out_specs, check_vma=False
    )
```

```python
import functools

import jax
import jax.numpy as jnp
from jax import lax
from jax.experimental import pallas as pl
from jax.experimental.pallas import tpu as pltpu
from jax.sharding import PartitionSpec as P

HD = 128
NBR = 8
LANES = 128
EPS = 1e-06
VMEM_LIMIT = 20 * 1024 * 1024
VMEM = pl.BlockSpec(memory_space=pltpu.VMEM)
HBM = pl.BlockSpec(memory_space=pltpu.HBM)
F32 = jnp.float32
BF16 = jnp.bfloat16


def params():
    return pltpu.CompilerParams(vmem_limit_bytes=VMEM_LIMIT)


def is_pow2(n):
    return n & (n - 1) == 0


def source_of(me, k, n):
    return me ^ k if is_pow2(n) else lax.rem(me + n - k, n)


def exchange(value, axis, k):
    n = lax.axis_size(axis)
    pairs = [(i, i ^ k if is_pow2(n) else (i + k) % n) for i in range(n)]
    return lax.ppermute(value, axis, pairs)


def spread(value, axis):
    return [value] + [exchange(value, axis, k) for k in range(1, lax.axis_size(axis))]


def swap(blocks, axis):
    return lax.all_to_all(blocks, axis, split_axis=0, concat_axis=0, tiled=True)


def columns_of(row, count):
    return jnp.transpose(jnp.broadcast_to(row, (count, row.shape[1])))


def silu(x):
    return x * jax.nn.sigmoid(x)


def fetch_kernel(asked_ref, table_ref, out_ref, tab, sem):
    width = tab.shape[1]
    at = pl.multiple_of(lax.axis_index("mp") * width, width)
    copy = pltpu.make_async_copy(table_ref.at[:, pl.ds(at, width)], tab, sem)
    copy.start()
    first = lax.axis_index("dp") * tab.shape[0]
    phase = lax.axis_index("phase")
    hots = []
    for d in range(out_ref.shape[0]):
        cols = columns_of(asked_ref[d, pl.ds(phase, 1), :] - first, LANES)
        lane = lax.broadcasted_iota(jnp.int32, cols.shape, 1)
        hots.append(
            jnp.concatenate(
                [
                    jnp.where(cols == lane + c, 1.0, 0.0).astype(BF16)
                    for c in range(0, tab.shape[0], LANES)
                ],
                axis=1,
            )
        )
    copy.wait()
    for d, hot in enumerate(hots):
        out_ref[d] = jnp.dot(hot, tab[...], preferred_element_type=F32).astype(BF16)


def fetch(asked, table, width):
    count, rows = asked.shape[0], asked.shape[2]
    return pl.pallas_call(
        fetch_kernel,
        out_shape=jax.ShapeDtypeStruct((count, rows, width), BF16),
        in_specs=[VMEM, HBM],
        out_specs=VMEM,
        scratch_shapes=[pltpu.VMEM((table.shape[0], width), BF16), pltpu.SemaphoreType.DMA],
        compiler_params=params(),
        cost_estimate=pl.CostEstimate(
            flops=2 * count * rows * width * table.shape[0],
            bytes_accessed=2 * width * table.shape[0],
            transcendentals=0,
        ),
        name="fetch",
    )(asked, table)


def start_picked(section, own, other, dst, sem):
    phase = lax.axis_index("phase")

    @pl.when(phase == section)
    def _():
        pltpu.make_async_copy(own, dst, sem).start()

    @pl.when(phase != section)
    def _():
        pltpu.make_async_copy(other, dst, sem).start()


def wait_picked(own, dst, sem):
    pltpu.make_async_copy(own, dst, sem).wait()


def front(x, section, gain_own, gain_other, seg_ref, w_own, w_buf, w_sem, gated_ref):
    phase = lax.axis_index("phase")
    rows, local_cols = x.shape[0], w_buf.shape[2]
    gain = jnp.where(phase == section, gain_own[...].astype(F32), gain_other[...].astype(F32))
    inv = lax.rsqrt(jnp.mean(x * x, axis=-1, keepdims=True) + EPS)
    normed = (x * inv * gain).astype(BF16)
    proj = []
    for g in range(4):
        wait_picked(w_own.at[g], w_buf.at[g], w_sem.at[g])
        proj.append(
            silu(jnp.dot(normed, w_buf[g], preferred_element_type=F32)).astype(BF16)
        )
    gates, values, queries, keys = proj
    seg = seg_ref[0, pl.ds(phase, 1), :]
    seg_cols = columns_of(seg, rows)
    at_row = lax.broadcasted_iota(jnp.int32, (rows, rows), 0)
    at_col = lax.broadcasted_iota(jnp.int32, (rows, rows), 1)
    allowed = (at_col <= at_row) & (seg_cols == seg)
    for h in range(0, local_cols, HD):
        head = slice(h, h + HD)
        scores = lax.dot_general(
            queries[:, head], keys[:, head], (((1,), (1,)), ((), ())), preferred_element_type=F32
        ) * HD ** (-0.5)
        weights = (jnp.where(allowed, silu(scores), 0.0) / rows).astype(BF16)
        mixed = jnp.dot(weights, values[:, head], preferred_element_type=F32)
        mixed = mixed * lax.rsqrt(jnp.mean(mixed * mixed, axis=-1, keepdims=True) + EPS)
        gated = (mixed * gates[:, head].astype(F32)).astype(BF16)
        for j in range(gated_ref.shape[0]):
            gated_ref[j, :, head] = gated


def back(x, gated_ref, o_own, o_buf, o_sem):
    steps = len(o_own)
    total = x.astype(F32)
    for k in range(steps):
        wait_picked(o_own[k], o_buf.at[k], o_sem.at[k])
        gated = gated_ref[source_of(lax.axis_index("mp"), k, steps)]
        part = jnp.dot(gated, o_buf[k], preferred_element_type=F32)
        total = total + part.astype(BF16).astype(F32)
    return total.astype(BF16)


def first_kernel(
    pieces_ref, gain_own, gain_other, seg_ref, w_own, w_other, *refs
):
    gated_ref, x_ref, w_buf, w_sem = refs[-4:]
    for g in range(4):
        start_picked(0, w_own.at[g], w_other.at[g], w_buf.at[g], w_sem.at[g])
    width = pieces_ref.shape[2]
    for j in range(pieces_ref.shape[0]):
        x_ref[:, j * width : (j + 1) * width] = pieces_ref[j]
    front(
        x_ref[...].astype(F32), 0, gain_own, gain_other, seg_ref, w_own, w_buf, w_sem, gated_ref
    )


def middle_kernel(steps, gated_in, x_ref, gain_own, gain_other, seg_ref, w_own, w_other, *refs):
    o_own, o_other = refs[:steps], refs[steps : 2 * steps]
    gated_ref, x1_ref, o_buf, o_sem, w_buf, w_sem = refs[2 * steps :]
    for k in range(steps):
        start_picked(0, o_own[k], o_other[k], o_buf.at[k], o_sem.at[k])
    for g in range(4):
        start_picked(1, w_own.at[g], w_other.at[g], w_buf.at[g], w_sem.at[g])
    x1 = back(x_ref[...], gated_in, o_own, o_buf, o_sem)
    x1_ref[...] = x1
    front(x1.astype(F32), 1, gain_own, gain_other, seg_ref, w_own, w_buf, w_sem, gated_ref)


def last_kernel(steps, gated_in, x_ref, neigh_ref, w_ref, bias_ref, *refs):
    o_own, o_other = refs[:steps], refs[steps : 2 * steps]
    states_ref, ctx_ref, o_buf, o_sem = refs[2 * steps :]
    for k in range(steps):
        start_picked(1, o_own[k], o_other[k], o_buf.at[k], o_sem.at[k])
    near = neigh_ref[lax.axis_index("phase")]
    row = lax.broadcasted_iota(jnp.int32, (x_ref.shape[0], near.shape[1]), 0)
    share = jnp.zeros(row.shape, F32)
    for n in range(NBR):
        share = share + jnp.where(near[n : n + 1, :] == row, 1.0 / NBR, 0.0)
    share = jnp.transpose(share).astype(BF16)
    states = back(x_ref[...], gated_in, o_own, o_buf, o_sem)
    states_ref[...] = states
    context = jnp.dot(share, states, preferred_element_type=F32).astype(BF16)
    summed = jnp.dot(context, w_ref[...], preferred_element_type=F32) + bias_ref[...].astype(F32)
    ctx_ref[...] = silu(summed).astype(BF16)


def section_flops(rows, width, local_cols):
    return 2 * rows * (width * 4 * local_cols + 2 * rows * local_cols)


def fetch_rows_padded(owners, item_row, table, width):
    dp_count = lax.axis_size("dp")
    row_total = item_row.shape[0]
    capacity = max(2, 7 * row_total // (4 * dp_count))
    hits = (owners[:, None] == jnp.arange(dp_count, dtype=jnp.int32)[None, :]).astype(jnp.int32)
    rank = jnp.sum((jnp.cumsum(hits, axis=0) - 1) * hits, axis=1)
    slot = owners * capacity + rank
    requests = jnp.full((dp_count * capacity,), -1, jnp.int32).at[slot].set(item_row)
    asked = swap(requests.reshape(dp_count, capacity), "dp")
    part = lax.dynamic_slice_in_dim(table, lax.axis_index("mp") * width, width, 1)
    found = jnp.take(part, jnp.maximum(asked, 0), axis=0)
    return swap(found, "dp").reshape(dp_count * capacity, width)[slot]


def on_device(
    item_owner, item_row, segments, neighbors, table, gains, w_in, w_out, w_ctx, ctx_bias
):
    dp_count, mp_count = lax.axis_size("dp"), lax.axis_size("mp")
    table_rows, width = table.shape
    batches, rows = segments.shape[1], segments.shape[2]
    imps = neighbors.shape[2]
    local_cols = w_out.shape[1]
    part = width // mp_count

    w_own = jnp.transpose(w_in[0], (1, 0, 2))
    w_other = exchange(w_own, "phase", 1)
    o_own = spread(w_out[0], "mp")
    o_other = [exchange(piece, "phase", 1) for piece in o_own]
    gain_other = exchange(gains, "phase", 1)
    near = jnp.transpose(neighbors[0], (0, 2, 1))
    bias = ctx_bias.reshape(1, -1)

    if dp_count <= 8:
        wanted = (item_owner[:, 0] * table_rows + item_row).reshape(1, batches, rows)
        asked = swap(jnp.broadcast_to(wanted, (dp_count, batches, rows)), "dp")
        found = swap(fetch(asked, table, part), "dp")
        piece = functools.reduce(jnp.add, [found[d] for d in range(dp_count)])
    else:
        piece = fetch_rows_padded(item_owner[:, 0], item_row, table, part)
        piece = lax.dynamic_index_in_dim(
            piece.reshape(batches, rows, part), lax.axis_index("phase"), 0, keepdims=False
        )
    x_pieces = swap(jnp.broadcast_to(piece[None], (mp_count, rows, part)), "mp")

    sem4 = pltpu.SemaphoreType.DMA((4,))
    semk = pltpu.SemaphoreType.DMA((mp_count,))
    w_buf = pltpu.VMEM((4, width, local_cols), BF16)
    o_buf = pltpu.VMEM((mp_count, local_cols, width), BF16)
    x_shape = jax.ShapeDtypeStruct((rows, width), BF16)
    gated_shape = jax.ShapeDtypeStruct((mp_count, rows, local_cols), BF16)
    front_flops = section_flops(rows, width, local_cols)
    back_flops = 2 * rows * width * local_cols * mp_count

    gated, x0 = pl.pallas_call(
        first_kernel,
        out_shape=[gated_shape, x_shape],
        in_specs=[VMEM] * 4 + [HBM] * (2 + mp_count),
        out_specs=[VMEM] * 2,
        scratch_shapes=[w_buf, sem4],
        compiler_params=params(),
        cost_estimate=pl.CostEstimate(
            flops=front_flops, bytes_accessed=8 * width * local_cols, transcendentals=0
        ),
        name="section0_front",
    )(x_pieces, gains, gain_other, segments, w_own, w_other, *o_other)

    gated, x1 = pl.pallas_call(
        functools.partial(middle_kernel, mp_count),
        out_shape=[gated_shape, x_shape],
        in_specs=[VMEM] * 5 + [HBM] * (2 + 2 * mp_count),
        out_specs=[VMEM] * 2,
        scratch_shapes=[o_buf, semk, w_buf, sem4],
        compiler_params=params(),
        cost_estimate=pl.CostEstimate(
            flops=front_flops + back_flops,
            bytes_accessed=(8 + 2 * mp_count) * width * local_cols,
            transcendentals=0,
        ),
        name="section0_back_section1_front",
    )(swap(gated, "mp"), x0, gains, gain_other, segments, w_own, w_other, *o_own, *o_other)

    states, ctx = pl.pallas_call(
        functools.partial(last_kernel, mp_count),
        out_shape=[x_shape, jax.ShapeDtypeStruct((imps, w_ctx.shape[1]), BF16)],
        in_specs=[VMEM] * 5 + [HBM] * (2 * mp_count),
        out_specs=[VMEM] * 2,
        scratch_shapes=[o_buf, semk],
        compiler_params=params(),
        cost_estimate=pl.CostEstimate(
            flops=back_flops + 2 * imps * width * (rows + w_ctx.shape[1]),
            bytes_accessed=2 * mp_count * width * local_cols,
            transcendentals=0,
        ),
        name="section1_back_context",
    )(swap(gated, "mp"), x1, near, w_ctx, bias, *o_own, *o_other)

    return (
        states.reshape(1, 1, rows, width),
        ctx.reshape(1, 1, imps, w_ctx.shape[1]),
    )


def solution(mesh):
    in_specs = (
        P("dp", None),
        P("dp"),
        P("dp", None, None),
        P("dp", None, None, None),
        P("dp", None),
        P("phase", None),
        P("phase", None, None, "mp"),
        P("phase", "mp", None),
        P(None, "mp"),
        P("mp"),
    )
    out_specs = (P("dp", "phase", None, None), P("dp", "phase", None, "mp"))
    return jax.shard_map(
        on_device, mesh=mesh, in_specs=in_specs, out_specs=out_specs, check_vma=False
    )
```

```python
import functools

import jax
import jax.numpy as jnp
from jax import lax
from jax.experimental import pallas as pl
from jax.experimental.pallas import tpu as pltpu
from jax.sharding import PartitionSpec as P

HD = 128
NBR = 8
LANES = 128
EPS = 1e-06
VMEM_LIMIT = 20 * 1024 * 1024
VMEM = pl.BlockSpec(memory_space=pltpu.VMEM)
HBM = pl.BlockSpec(memory_space=pltpu.HBM)
F32 = jnp.float32
BF16 = jnp.bfloat16


def params():
    return pltpu.CompilerParams(vmem_limit_bytes=VMEM_LIMIT)


def is_pow2(n):
    return n & (n - 1) == 0


def source_of(me, k, n):
    return me ^ k if is_pow2(n) else lax.rem(me + n - k, n)


def exchange(value, axis, k):
    n = lax.axis_size(axis)
    pairs = [(i, i ^ k if is_pow2(n) else (i + k) % n) for i in range(n)]
    return lax.ppermute(value, axis, pairs)


def spread(value, axis):
    return [value] + [exchange(value, axis, k) for k in range(1, lax.axis_size(axis))]


def swap(blocks, axis):
    return lax.all_to_all(blocks, axis, split_axis=0, concat_axis=0, tiled=True)


def columns_of(row, count):
    return jnp.transpose(jnp.broadcast_to(row, (count, row.shape[1])))


def silu(x):
    return x * jax.nn.sigmoid(x)


def fetch_kernel(steps, *refs):
    asked_refs, table_ref = refs[:steps], refs[steps]
    out_refs, (tab, sem) = refs[-steps - 2 : -2], refs[-2:]
    width = tab.shape[1]
    at = pl.multiple_of(lax.axis_index("mp") * width, width)
    copy = pltpu.make_async_copy(table_ref.at[:, pl.ds(at, width)], tab, sem)
    copy.start()
    first = lax.axis_index("dp") * tab.shape[0]
    phase = lax.axis_index("phase")
    hots = []
    for asked_ref in asked_refs:
        cols = columns_of(asked_ref[pl.ds(phase, 1), :] - first, LANES)
        lane = lax.broadcasted_iota(jnp.int32, cols.shape, 1)
        hots.append(
            jnp.concatenate(
                [
                    jnp.where(cols == lane + c, 1.0, 0.0).astype(BF16)
                    for c in range(0, tab.shape[0], LANES)
                ],
                axis=1,
            )
        )
    copy.wait()
    for hot, out_ref in zip(hots, out_refs):
        out_ref[...] = jnp.dot(hot, tab[...], preferred_element_type=F32).astype(BF16)


def fetch(asked, table, width, after):
    steps, rows = len(asked), asked[0].shape[1]
    return pl.pallas_call(
        functools.partial(fetch_kernel, steps),
        out_shape=[jax.ShapeDtypeStruct((rows, width), BF16)] * steps,
        in_specs=[VMEM] * steps + [HBM] * (1 + len(after)),
        out_specs=[VMEM] * steps,
        scratch_shapes=[pltpu.VMEM((table.shape[0], width), BF16), pltpu.SemaphoreType.DMA],
        compiler_params=params(),
        cost_estimate=pl.CostEstimate(
            flops=2 * steps * rows * width * table.shape[0],
            bytes_accessed=2 * width * table.shape[0],
            transcendentals=0,
        ),
        name="fetch",
    )(*asked, table, *after)


def merge_kernel(a_ref, b_ref, *refs):
    refs[-1][...] = a_ref[...] + b_ref[...]


def merge(a, b, after):
    return pl.pallas_call(
        merge_kernel,
        out_shape=jax.ShapeDtypeStruct(a.shape, BF16),
        in_specs=[VMEM] * 2 + [HBM] * len(after),
        out_specs=VMEM,
        compiler_params=params(),
        name="merge",
    )(a, b, *after)


def hold_kernel(*refs):
    pass


def hold(value, after):
    return pl.pallas_call(
        hold_kernel,
        out_shape=jax.ShapeDtypeStruct(value.shape, value.dtype),
        in_specs=[HBM] * (1 + len(after)),
        out_specs=HBM,
        input_output_aliases={0: 0},
        compiler_params=params(),
        name="hold",
    )(value, *after)


def ask_around(wanted):
    asked, step = [wanted], 1
    while step < lax.axis_size("dp"):
        got = exchange(jnp.concatenate(asked), "dp", step)
        asked = asked + jnp.split(got, step)
        step = 2 * step
    return asked


def gather_in(blocks, after):
    blocks, step = dict(enumerate(blocks)), 1
    while step < lax.axis_size("dp"):
        for k in sorted((k for k in blocks if k & step), reverse=True):
            got = exchange(blocks.pop(k), "dp", step)
            last = 2 * step == lax.axis_size("dp")
            blocks[k ^ step] = merge(blocks[k ^ step], got, after if last else [])
        step = 2 * step
    return blocks[0]


def start_picked(section, own, other, dst, sem):
    phase = lax.axis_index("phase")

    @pl.when(phase == section)
    def _():
        pltpu.make_async_copy(own, dst, sem).start()

    @pl.when(phase != section)
    def _():
        pltpu.make_async_copy(other, dst, sem).start()


def wait_picked(own, dst, sem):
    pltpu.make_async_copy(own, dst, sem).wait()


def start_weights(section, w_own, w_other, w_buf, w_sem):
    for g in range(4):
        start_picked(section, w_own.at[g], w_other.at[g], w_buf.at[g], w_sem.at[g])


def front(x, section, gain_own, gain_other, seg_ref, w_own, w_buf, w_sem, gated_ref):
    phase = lax.axis_index("phase")
    rows, local_cols = x.shape[0], w_buf.shape[2]
    gain = jnp.where(phase == section, gain_own[...].astype(F32), gain_other[...].astype(F32))
    inv = lax.rsqrt(jnp.mean(x * x, axis=-1, keepdims=True) + EPS)
    normed = (x * inv * gain).astype(BF16)
    proj = []
    for g in range(4):
        wait_picked(w_own.at[g], w_buf.at[g], w_sem.at[g])
        proj.append(
            silu(jnp.dot(normed, w_buf[g], preferred_element_type=F32)).astype(BF16)
        )
    gates, values, queries, keys = proj
    seg = seg_ref[0, pl.ds(phase, 1), :]
    seg_cols = columns_of(seg, rows)
    at_row = lax.broadcasted_iota(jnp.int32, (rows, rows), 0)
    at_col = lax.broadcasted_iota(jnp.int32, (rows, rows), 1)
    allowed = (at_col <= at_row) & (seg_cols == seg)
    for h in range(0, local_cols, HD):
        head = slice(h, h + HD)
        scores = lax.dot_general(
            queries[:, head], keys[:, head], (((1,), (1,)), ((), ())), preferred_element_type=F32
        ) * HD ** (-0.5)
        weights = (jnp.where(allowed, silu(scores), 0.0) / rows).astype(BF16)
        mixed = jnp.dot(weights, values[:, head], preferred_element_type=F32)
        mixed = mixed * lax.rsqrt(jnp.mean(mixed * mixed, axis=-1, keepdims=True) + EPS)
        gated_ref[:, head] = (mixed * gates[:, head].astype(F32)).astype(BF16)


def back(x, gated_refs, o_own, o_buf, o_sem):
    total = x.astype(F32)
    for k, gated_ref in enumerate(gated_refs):
        wait_picked(o_own.at[k], o_buf.at[k], o_sem.at[k])
        part = jnp.dot(gated_ref[...], o_buf[k], preferred_element_type=F32)
        total = total + part.astype(BF16).astype(F32)
    return total.astype(BF16)


def first_kernel(steps, *refs):
    x_refs, o_own = refs[:steps], refs[steps : 2 * steps]
    gain_own, gain_other, seg_ref, w_own, w_other = refs[2 * steps : -6]
    gated_ref, x_ref, stack_ref, w_buf, w_sem, o_sem = refs[-6:]
    start_weights(0, w_own, w_other, w_buf, w_sem)
    copies = [
        pltpu.make_async_copy(o_own[k], stack_ref.at[k], o_sem.at[k]) for k in range(steps)
    ]
    for copy in copies:
        copy.start()
    width = x_refs[0].shape[1]
    for k, piece in enumerate(x_refs):
        at = pl.multiple_of(source_of(lax.axis_index("mp"), k, steps) * width, width)
        x_ref[:, pl.ds(at, width)] = piece[...]
    x = x_ref[...].astype(F32)
    front(x, 0, gain_own, gain_other, seg_ref, w_own, w_buf, w_sem, gated_ref)
    for copy in copies:
        copy.wait()


def middle_kernel(steps, *refs):
    gated_refs = refs[:steps]
    x_ref, gain_own, gain_other, seg_ref, w_own, w_other, o_own, o_other = refs[steps : steps + 8]
    gated_ref, x1_ref, o_buf, o_sem, w_buf, w_sem = refs[steps + 8 :]
    for k in range(steps):
        start_picked(0, o_own.at[k], o_other.at[k], o_buf.at[k], o_sem.at[k])
    start_weights(1, w_own, w_other, w_buf, w_sem)
    x1 = back(x_ref[...], gated_refs, o_own, o_buf, o_sem)
    x1_ref[...] = x1
    x1 = x1.astype(F32)
    front(x1, 1, gain_own, gain_other, seg_ref, w_own, w_buf, w_sem, gated_ref)


def last_kernel(steps, *refs):
    gated_refs = refs[:steps]
    x_ref, neigh_ref, w_ref, bias_ref, o_own, o_other, states_ref, ctx_ref = refs[steps : steps + 8]
    o_buf, o_sem = refs[steps + 8 :]
    for k in range(steps):
        start_picked(1, o_own.at[k], o_other.at[k], o_buf.at[k], o_sem.at[k])
    near = neigh_ref[lax.axis_index("phase")]
    row = lax.broadcasted_iota(jnp.int32, (x_ref.shape[0], near.shape[1]), 0)
    share = jnp.zeros(row.shape, F32)
    for n in range(NBR):
        share = share + jnp.where(near[n : n + 1, :] == row, 1.0 / NBR, 0.0)
    share = jnp.transpose(share).astype(BF16)
    states = back(x_ref[...], gated_refs, o_own, o_buf, o_sem)
    states_ref[...] = states
    context = jnp.dot(share, states, preferred_element_type=F32).astype(BF16)
    summed = jnp.dot(context, w_ref[...], preferred_element_type=F32) + bias_ref[...].astype(F32)
    ctx_ref[...] = silu(summed).astype(BF16)


def section_flops(rows, width, local_cols):
    return 2 * rows * (width * 4 * local_cols + 2 * rows * local_cols)


def fetch_rows_padded(owners, item_row, table, width):
    dp_count = lax.axis_size("dp")
    row_total = item_row.shape[0]
    capacity = max(2, 7 * row_total // (4 * dp_count))
    hits = (owners[:, None] == jnp.arange(dp_count, dtype=jnp.int32)[None, :]).astype(jnp.int32)
    rank = jnp.sum((jnp.cumsum(hits, axis=0) - 1) * hits, axis=1)
    slot = owners * capacity + rank
    requests = jnp.full((dp_count * capacity,), -1, jnp.int32).at[slot].set(item_row)
    asked = swap(requests.reshape(dp_count, capacity), "dp")
    part = lax.dynamic_slice_in_dim(table, lax.axis_index("mp") * width, width, 1)
    found = jnp.take(part, jnp.maximum(asked, 0), axis=0)
    return swap(found, "dp").reshape(dp_count * capacity, width)[slot]


def on_device(
    item_owner, item_row, segments, neighbors, table, gains, w_in, w_out, w_ctx, ctx_bias
):
    dp_count, mp_count = lax.axis_size("dp"), lax.axis_size("mp")
    table_rows, width = table.shape
    batches, rows = segments.shape[1], segments.shape[2]
    imps = neighbors.shape[2]
    local_cols = w_out.shape[1]
    part = width // mp_count

    w_own = jnp.transpose(w_in[0], (1, 0, 2))
    o_pieces = spread(w_out[0], "mp")
    gain_other = exchange(gains, "phase", 1)
    near = jnp.transpose(neighbors[0], (0, 2, 1))
    bias = ctx_bias.reshape(1, -1)

    if is_pow2(dp_count) and dp_count <= 8:
        wanted = (item_owner[:, 0] * table_rows + item_row).reshape(batches, rows)
        asked = ask_around(wanted)
        w_own = hold(w_own, asked[1:2])
        w_other = exchange(w_own, "phase", 1)
        found = fetch(asked, table, part, [gain_other])
        piece = gather_in(found, o_pieces[1:3] + [w_other])
    else:
        piece = fetch_rows_padded(item_owner[:, 0], item_row, table, part)
        piece = lax.dynamic_index_in_dim(
            piece.reshape(batches, rows, part), lax.axis_index("phase"), 0, keepdims=False
        )
        w_other = exchange(w_own, "phase", 1)
    x_pieces = spread(piece, "mp")

    sem4 = pltpu.SemaphoreType.DMA((4,))
    semk = pltpu.SemaphoreType.DMA((mp_count,))
    w_buf = pltpu.VMEM((4, width, local_cols), BF16)
    o_buf = pltpu.VMEM((mp_count, local_cols, width), BF16)
    x_shape = jax.ShapeDtypeStruct((rows, width), BF16)
    gated_shape = jax.ShapeDtypeStruct((rows, local_cols), BF16)
    front_flops = section_flops(rows, width, local_cols)
    back_flops = 2 * rows * width * local_cols * mp_count

    gated, x0, o_own = pl.pallas_call(
        functools.partial(first_kernel, mp_count),
        out_shape=[
            gated_shape,
            x_shape,
            jax.ShapeDtypeStruct((mp_count, local_cols, width), BF16),
        ],
        in_specs=[VMEM] * mp_count + [HBM] * mp_count + [VMEM] * 3 + [HBM] * 2,
        out_specs=[VMEM] * 2 + [HBM],
        scratch_shapes=[w_buf, sem4, semk],
        compiler_params=params(),
        cost_estimate=pl.CostEstimate(
            flops=front_flops, bytes_accessed=8 * width * local_cols, transcendentals=0
        ),
        name="section0_front",
    )(*x_pieces, *o_pieces, gains, gain_other, segments, w_own, w_other)
    o_other = exchange(o_own, "phase", 1)

    gated, x1 = pl.pallas_call(
        functools.partial(middle_kernel, mp_count),
        out_shape=[gated_shape, x_shape],
        in_specs=[VMEM] * (mp_count + 4) + [HBM] * 4,
        out_specs=[VMEM] * 2,
        scratch_shapes=[o_buf, semk, w_buf, sem4],
        compiler_params=params(),
        cost_estimate=pl.CostEstimate(
            flops=front_flops + back_flops,
            bytes_accessed=(8 + 2 * mp_count) * width * local_cols,
            transcendentals=0,
        ),
        name="section0_back_section1_front",
    )(*spread(gated, "mp"), x0, gains, gain_other, segments, w_own, w_other, o_own, o_other)

    states, ctx = pl.pallas_call(
        functools.partial(last_kernel, mp_count),
        out_shape=[x_shape, jax.ShapeDtypeStruct((imps, w_ctx.shape[1]), BF16)],
        in_specs=[VMEM] * (mp_count + 4) + [HBM] * 2,
        out_specs=[VMEM] * 2,
        scratch_shapes=[o_buf, semk],
        compiler_params=params(),
        cost_estimate=pl.CostEstimate(
            flops=back_flops + 2 * imps * width * (rows + w_ctx.shape[1]),
            bytes_accessed=2 * mp_count * width * local_cols,
            transcendentals=0,
        ),
        name="section1_back_context",
    )(*spread(gated, "mp"), x1, near, w_ctx, bias, o_own, o_other)

    return (
        states.reshape(1, 1, rows, width),
        ctx.reshape(1, 1, imps, w_ctx.shape[1]),
    )


def solution(mesh):
    in_specs = (
        P("dp", None),
        P("dp"),
        P("dp", None, None),
        P("dp", None, None, None),
        P("dp", None),
        P("phase", None),
        P("phase", None, None, "mp"),
        P("phase", "mp", None),
        P(None, "mp"),
        P("mp"),
    )
    out_specs = (P("dp", "phase", None, None), P("dp", "phase", None, "mp"))
    return jax.shard_map(
        on_device, mesh=mesh, in_specs=in_specs, out_specs=out_specs, check_vma=False
    )
```

```python
import functools

import jax
import jax.numpy as jnp
from jax import lax
from jax.experimental import pallas as pl
from jax.experimental.pallas import tpu as pltpu
from jax.sharding import PartitionSpec as P

HD = 128
NBR = 8
LANES = 128
EPS = 1e-06
VMEM_LIMIT = 20 * 1024 * 1024
VMEM = pl.BlockSpec(memory_space=pltpu.VMEM)
HBM = pl.BlockSpec(memory_space=pltpu.HBM)
F32 = jnp.float32
BF16 = jnp.bfloat16


def params():
    return pltpu.CompilerParams(vmem_limit_bytes=VMEM_LIMIT)


def is_pow2(n):
    return n & (n - 1) == 0


def source_of(me, k, n):
    return me ^ k if is_pow2(n) else lax.rem(me + n - k, n)


def exchange(value, axis, k):
    n = lax.axis_size(axis)
    pairs = [(i, i ^ k if is_pow2(n) else (i + k) % n) for i in range(n)]
    return lax.ppermute(value, axis, pairs)


def spread(value, axis):
    return [value] + [exchange(value, axis, k) for k in range(1, lax.axis_size(axis))]


def swap(blocks, axis):
    return lax.all_to_all(blocks, axis, split_axis=0, concat_axis=0, tiled=True)


def columns_of(row, count):
    return jnp.transpose(jnp.broadcast_to(row, (count, row.shape[1])))


def silu(x):
    return x * jax.nn.sigmoid(x)


def fetch_kernel(steps, *refs):
    asked_refs, table_ref = refs[:steps], refs[steps]
    out_refs, (tab, sem) = refs[-steps - 2 : -2], refs[-2:]
    width = tab.shape[1]
    at = pl.multiple_of(lax.axis_index("mp") * width, width)
    copy = pltpu.make_async_copy(table_ref.at[:, pl.ds(at, width)], tab, sem)
    copy.start()
    first = lax.axis_index("dp") * tab.shape[0]
    phase = lax.axis_index("phase")
    hots = []
    for asked_ref in asked_refs:
        cols = columns_of(asked_ref[pl.ds(phase, 1), :] - first, LANES)
        lane = lax.broadcasted_iota(jnp.int32, cols.shape, 1)
        hots.append(
            jnp.concatenate(
                [
                    jnp.where(cols == lane + c, 1.0, 0.0).astype(BF16)
                    for c in range(0, tab.shape[0], LANES)
                ],
                axis=1,
            )
        )
    copy.wait()
    for hot, out_ref in zip(hots, out_refs):
        out_ref[...] = jnp.dot(hot, tab[...], preferred_element_type=F32).astype(BF16)


def fetch(asked, table, width, after):
    steps, rows = len(asked), asked[0].shape[1]
    return pl.pallas_call(
        functools.partial(fetch_kernel, steps),
        out_shape=[jax.ShapeDtypeStruct((rows, width), BF16)] * steps,
        in_specs=[VMEM] * steps + [HBM] * (1 + len(after)),
        out_specs=[VMEM] * steps,
        scratch_shapes=[pltpu.VMEM((table.shape[0], width), BF16), pltpu.SemaphoreType.DMA],
        compiler_params=params(),
        cost_estimate=pl.CostEstimate(
            flops=2 * steps * rows * width * table.shape[0],
            bytes_accessed=2 * width * table.shape[0],
            transcendentals=0,
        ),
        name="fetch",
    )(*asked, table, *after)


def merge_kernel(a_ref, b_ref, *refs):
    refs[-1][...] = a_ref[...] + b_ref[...]


def merge(a, b, after):
    return pl.pallas_call(
        merge_kernel,
        out_shape=jax.ShapeDtypeStruct(a.shape, BF16),
        in_specs=[VMEM] * 2 + [HBM] * len(after),
        out_specs=VMEM,
        compiler_params=params(),
        name="merge",
    )(a, b, *after)


def hold_kernel(*refs):
    pass


def hold(value, after):
    return pl.pallas_call(
        hold_kernel,
        out_shape=jax.ShapeDtypeStruct(value.shape, value.dtype),
        in_specs=[HBM] * (1 + len(after)),
        out_specs=HBM,
        input_output_aliases={0: 0},
        compiler_params=params(),
        name="hold",
    )(value, *after)


def cut_kernel(near_ref, far_ref, *refs):
    low_ref, high_ref, sems = refs[-3:]
    half = low_ref.shape[0]
    copies = [
        pltpu.make_async_copy(far_ref.at[pl.ds(0, half), :], low_ref, sems.at[0]),
        pltpu.make_async_copy(near_ref.at[pl.ds(half, half), :], high_ref, sems.at[1]),
    ]
    for copy in copies:
        copy.start()
    for copy in copies:
        copy.wait()


def relay(near, far, axis, after):
    half = jax.ShapeDtypeStruct((near.shape[0] // 2,) + near.shape[1:], near.dtype)
    low, high = pl.pallas_call(
        cut_kernel,
        out_shape=[half] * 2,
        in_specs=[HBM] * (2 + len(after)),
        out_specs=[HBM] * 2,
        scratch_shapes=[pltpu.SemaphoreType.DMA((2,))],
        compiler_params=params(),
        name="cut",
    )(near, far, *after)
    return [exchange(low, axis, 1), exchange(high, axis, 2)]


def ask_around(wanted):
    asked, step = [wanted], 1
    while step < lax.axis_size("dp"):
        got = exchange(jnp.concatenate(asked), "dp", step)
        asked = asked + jnp.split(got, step)
        step = 2 * step
    return asked


def gather_in(blocks, first, then):
    blocks, step = dict(enumerate(blocks)), 1
    while step < lax.axis_size("dp"):
        at_end = 2 * step == lax.axis_size("dp")
        for k in sorted((k for k in blocks if k & step), reverse=True):
            got = exchange(blocks.pop(k), "dp", step)
            after = then(blocks[k ^ step]) if at_end else first
            blocks[k ^ step] = merge(blocks[k ^ step], got, after)
            first = [blocks[k ^ step]]
        step = 2 * step
    return blocks[0]


def start_picked(section, own, other, dst, sem):
    phase = lax.axis_index("phase")

    @pl.when(phase == section)
    def _():
        pltpu.make_async_copy(own, dst, sem).start()

    @pl.when(phase != section)
    def _():
        pltpu.make_async_copy(other, dst, sem).start()


def wait_picked(own, dst, sem):
    pltpu.make_async_copy(own, dst, sem).wait()


def start_weights(section, w_own, w_other, w_buf, w_sem):
    for g in range(4):
        start_picked(section, w_own.at[g], w_other.at[g], w_buf.at[g], w_sem.at[g])


def front(x, section, gain_own, gain_other, seg_ref, w_own, w_buf, w_sem, gated_ref):
    phase = lax.axis_index("phase")
    rows, local_cols = x.shape[0], w_buf.shape[2]
    gain = jnp.where(phase == section, gain_own[...].astype(F32), gain_other[...].astype(F32))
    inv = lax.rsqrt(jnp.mean(x * x, axis=-1, keepdims=True) + EPS)
    normed = (x * inv * gain).astype(BF16)
    proj = []
    for g in range(4):
        wait_picked(w_own.at[g], w_buf.at[g], w_sem.at[g])
        proj.append(
            silu(jnp.dot(normed, w_buf[g], preferred_element_type=F32)).astype(BF16)
        )
    gates, values, queries, keys = proj
    seg = seg_ref[0, pl.ds(phase, 1), :]
    seg_cols = columns_of(seg, rows)
    at_row = lax.broadcasted_iota(jnp.int32, (rows, rows), 0)
    at_col = lax.broadcasted_iota(jnp.int32, (rows, rows), 1)
    allowed = (at_col <= at_row) & (seg_cols == seg)
    for h in range(0, local_cols, HD):
        head = slice(h, h + HD)
        scores = lax.dot_general(
            queries[:, head], keys[:, head], (((1,), (1,)), ((), ())), preferred_element_type=F32
        ) * HD ** (-0.5)
        weights = (jnp.where(allowed, silu(scores), 0.0) / rows).astype(BF16)
        mixed = jnp.dot(weights, values[:, head], preferred_element_type=F32)
        mixed = mixed * lax.rsqrt(jnp.mean(mixed * mixed, axis=-1, keepdims=True) + EPS)
        gated_ref[:, head] = (mixed * gates[:, head].astype(F32)).astype(BF16)


def back(x, gated_refs, o_own, o_buf, o_sem):
    total = x.astype(F32)
    for k, gated_ref in enumerate(gated_refs):
        wait_picked(o_own.at[k], o_buf.at[k], o_sem.at[k])
        part = jnp.dot(gated_ref[...], o_buf[k], preferred_element_type=F32)
        total = total + part.astype(BF16).astype(F32)
    return total.astype(BF16)


def first_kernel(steps, places, *refs):
    x_refs, o_own = refs[:steps], refs[steps : steps + len(places)]
    gain_own, gain_other, seg_ref, w_own, w_other = refs[steps + len(places) : -6]
    gated_ref, x_ref, stack_ref, w_buf, w_sem, o_sem = refs[-6:]
    start_weights(0, w_own, w_other, w_buf, w_sem)
    copies = []
    for n, (k, row) in enumerate(places):
        at = stack_ref.at[k, pl.ds(row, o_own[n].shape[0]), :]
        copies.append(pltpu.make_async_copy(o_own[n], at, o_sem.at[n]))
    for copy in copies:
        copy.start()
    width = x_refs[0].shape[1]
    for k, piece in enumerate(x_refs):
        at = pl.multiple_of(source_of(lax.axis_index("mp"), k, steps) * width, width)
        x_ref[:, pl.ds(at, width)] = piece[...]
    x = x_ref[...].astype(F32)
    front(x, 0, gain_own, gain_other, seg_ref, w_own, w_buf, w_sem, gated_ref)
    for copy in copies:
        copy.wait()


def middle_kernel(steps, *refs):
    gated_refs = refs[:steps]
    x_ref, gain_own, gain_other, seg_ref, w_own, w_other, o_own, o_other = refs[steps : steps + 8]
    gated_ref, x1_ref, o_buf, o_sem, w_buf, w_sem = refs[steps + 8 :]
    for k in range(steps):
        start_picked(0, o_own.at[k], o_other.at[k], o_buf.at[k], o_sem.at[k])
    start_weights(1, w_own, w_other, w_buf, w_sem)
    x1 = back(x_ref[...], gated_refs, o_own, o_buf, o_sem)
    x1_ref[...] = x1
    x1 = x1.astype(F32)
    front(x1, 1, gain_own, gain_other, seg_ref, w_own, w_buf, w_sem, gated_ref)


def last_kernel(steps, *refs):
    gated_refs = refs[:steps]
    x_ref, neigh_ref, w_ref, bias_ref, o_own, o_other, states_ref, ctx_ref = refs[steps : steps + 8]
    o_buf, o_sem = refs[steps + 8 :]
    for k in range(steps):
        start_picked(1, o_own.at[k], o_other.at[k], o_buf.at[k], o_sem.at[k])
    near = neigh_ref[lax.axis_index("phase")]
    row = lax.broadcasted_iota(jnp.int32, (x_ref.shape[0], near.shape[1]), 0)
    share = jnp.zeros(row.shape, F32)
    for n in range(NBR):
        share = share + jnp.where(near[n : n + 1, :] == row, 1.0 / NBR, 0.0)
    share = jnp.transpose(share).astype(BF16)
    states = back(x_ref[...], gated_refs, o_own, o_buf, o_sem)
    states_ref[...] = states
    context = jnp.dot(share, states, preferred_element_type=F32).astype(BF16)
    summed = jnp.dot(context, w_ref[...], preferred_element_type=F32) + bias_ref[...].astype(F32)
    ctx_ref[...] = silu(summed).astype(BF16)


def section_flops(rows, width, local_cols):
    return 2 * rows * (width * 4 * local_cols + 2 * rows * local_cols)


def fetch_rows_padded(owners, item_row, table, width):
    dp_count = lax.axis_size("dp")
    row_total = item_row.shape[0]
    capacity = max(2, 7 * row_total // (4 * dp_count))
    hits = (owners[:, None] == jnp.arange(dp_count, dtype=jnp.int32)[None, :]).astype(jnp.int32)
    rank = jnp.sum((jnp.cumsum(hits, axis=0) - 1) * hits, axis=1)
    slot = owners * capacity + rank
    requests = jnp.full((dp_count * capacity,), -1, jnp.int32).at[slot].set(item_row)
    asked = swap(requests.reshape(dp_count, capacity), "dp")
    part = lax.dynamic_slice_in_dim(table, lax.axis_index("mp") * width, width, 1)
    found = jnp.take(part, jnp.maximum(asked, 0), axis=0)
    return swap(found, "dp").reshape(dp_count * capacity, width)[slot]


def on_device(
    item_owner, item_row, segments, neighbors, table, gains, w_in, w_out, w_ctx, ctx_bias
):
    dp_count, mp_count = lax.axis_size("dp"), lax.axis_size("mp")
    table_rows, width = table.shape
    batches, rows = segments.shape[1], segments.shape[2]
    imps = neighbors.shape[2]
    local_cols = w_out.shape[1]
    part = width // mp_count

    w_own = jnp.transpose(w_in[0], (1, 0, 2))
    places = [(k, 0) for k in range(mp_count)]
    if mp_count == 4:
        near, far = exchange(w_out[0], "mp", 1), exchange(w_out[0], "mp", 2)
        o_pieces = [w_out[0], near, far]
        places.append((3, local_cols // 2))
    else:
        o_pieces = spread(w_out[0], "mp")
    gain_other = exchange(gains, "phase", 1)
    neigh = jnp.transpose(neighbors[0], (0, 2, 1))
    bias = ctx_bias.reshape(1, -1)

    if is_pow2(dp_count) and dp_count <= 8:
        wanted = (item_owner[:, 0] * table_rows + item_row).reshape(batches, rows)
        asked = ask_around(wanted)
        w_own = hold(w_own, asked[1:2])
        w_other = exchange(w_own, "phase", 1)
        late = fetch(asked[-1:], table, part, [])
        found = fetch(asked[:-1], table, part, late) + late

        def then(first):
            if mp_count == 4:
                o_pieces.extend(relay(near, far, "mp", [first]))
            return [w_other, gain_other]

        piece = gather_in(found, [], then)
    else:
        piece = fetch_rows_padded(item_owner[:, 0], item_row, table, part)
        piece = lax.dynamic_index_in_dim(
            piece.reshape(batches, rows, part), lax.axis_index("phase"), 0, keepdims=False
        )
        w_other = exchange(w_own, "phase", 1)
        if mp_count == 4:
            o_pieces.extend(relay(near, far, "mp", [piece]))
    x_pieces = spread(piece, "mp")

    sem4 = pltpu.SemaphoreType.DMA((4,))
    semk = pltpu.SemaphoreType.DMA((mp_count,))
    w_buf = pltpu.VMEM((4, width, local_cols), BF16)
    o_buf = pltpu.VMEM((mp_count, local_cols, width), BF16)
    x_shape = jax.ShapeDtypeStruct((rows, width), BF16)
    gated_shape = jax.ShapeDtypeStruct((rows, local_cols), BF16)
    front_flops = section_flops(rows, width, local_cols)
    back_flops = 2 * rows * width * local_cols * mp_count

    gated, x0, o_own = pl.pallas_call(
        functools.partial(first_kernel, mp_count, places),
        out_shape=[
            gated_shape,
            x_shape,
            jax.ShapeDtypeStruct((mp_count, local_cols, width), BF16),
        ],
        in_specs=[VMEM] * mp_count + [HBM] * len(places) + [VMEM] * 3 + [HBM] * 2,
        out_specs=[VMEM] * 2 + [HBM],
        scratch_shapes=[w_buf, sem4, pltpu.SemaphoreType.DMA((len(places),))],
        compiler_params=params(),
        cost_estimate=pl.CostEstimate(
            flops=front_flops, bytes_accessed=8 * width * local_cols, transcendentals=0
        ),
        name="section0_front",
    )(*x_pieces, *o_pieces, gains, gain_other, segments, w_own, w_other)
    o_other = exchange(o_own, "phase", 1)

    gated, x1 = pl.pallas_call(
        functools.partial(middle_kernel, mp_count),
        out_shape=[gated_shape, x_shape],
        in_specs=[VMEM] * (mp_count + 4) + [HBM] * 4,
        out_specs=[VMEM] * 2,
        scratch_shapes=[o_buf, semk, w_buf, sem4],
        compiler_params=params(),
        cost_estimate=pl.CostEstimate(
            flops=front_flops + back_flops,
            bytes_accessed=(8 + 2 * mp_count) * width * local_cols,
            transcendentals=0,
        ),
        name="section0_back_section1_front",
    )(*spread(gated, "mp"), x0, gains, gain_other, segments, w_own, w_other, o_own, o_other)

    states, ctx = pl.pallas_call(
        functools.partial(last_kernel, mp_count),
        out_shape=[x_shape, jax.ShapeDtypeStruct((imps, w_ctx.shape[1]), BF16)],
        in_specs=[VMEM] * (mp_count + 4) + [HBM] * 2,
        out_specs=[VMEM] * 2,
        scratch_shapes=[o_buf, semk],
        compiler_params=params(),
        cost_estimate=pl.CostEstimate(
            flops=back_flops + 2 * imps * width * (rows + w_ctx.shape[1]),
            bytes_accessed=2 * mp_count * width * local_cols,
            transcendentals=0,
        ),
        name="section1_back_context",
    )(*spread(gated, "mp"), x1, neigh, w_ctx, bias, o_own, o_other)

    return (
        states.reshape(1, 1, rows, width),
        ctx.reshape(1, 1, imps, w_ctx.shape[1]),
    )


def solution(mesh):
    in_specs = (
        P("dp", None),
        P("dp"),
        P("dp", None, None),
        P("dp", None, None, None),
        P("dp", None),
        P("phase", None),
        P("phase", None, None, "mp"),
        P("phase", "mp", None),
        P(None, "mp"),
        P("mp"),
    )
    out_specs = (P("dp", "phase", None, None), P("dp", "phase", None, "mp"))
    return jax.shard_map(
        on_device, mesh=mesh, in_specs=in_specs, out_specs=out_specs, check_vma=False
    )
```

```python
import functools

import jax
import jax.numpy as jnp
from jax import lax
from jax.experimental import pallas as pl
from jax.experimental.pallas import tpu as pltpu
from jax.sharding import PartitionSpec as P

HD = 128
NBR = 8
LANES = 128
EPS = 1e-06
VMEM_LIMIT = 20 * 1024 * 1024
VMEM = pl.BlockSpec(memory_space=pltpu.VMEM)
HBM = pl.BlockSpec(memory_space=pltpu.HBM)
F32 = jnp.float32
BF16 = jnp.bfloat16


def params():
    return pltpu.CompilerParams(vmem_limit_bytes=VMEM_LIMIT)


def is_pow2(n):
    return n & (n - 1) == 0


def source_of(me, slot, n):
    k = (n - slot) % n
    return me ^ k if is_pow2(n) else lax.rem(me + n - k, n)


def exchange(value, axis, k):
    n = lax.axis_size(axis)
    pairs = [(i, i ^ k if is_pow2(n) else (i + k) % n) for i in range(n)]
    return lax.ppermute(value, axis, pairs)


def spread(value, axis):
    return [value] + [exchange(value, axis, k) for k in reversed(range(1, lax.axis_size(axis)))]


def swap(blocks, axis):
    return lax.all_to_all(blocks, axis, split_axis=0, concat_axis=0, tiled=True)


def columns_of(row, count):
    return jnp.transpose(jnp.broadcast_to(row, (count, row.shape[1])))


def silu(x):
    return x * jax.nn.sigmoid(x)


def fetch_kernel(steps, batches, *refs):
    asked_refs, table_ref = refs[:steps], refs[steps]
    out_refs, (tab, sem) = refs[-steps - 2 : -2], refs[-2:]
    width = tab.shape[1]
    at = pl.multiple_of(lax.axis_index("mp") * width, width)
    copy = pltpu.make_async_copy(table_ref.at[:, pl.ds(at, width)], tab, sem)
    copy.start()
    first = lax.axis_index("dp") * tab.shape[0]
    phase = lax.axis_index("phase")
    hots = []
    for asked_ref in asked_refs:
        per = asked_ref.shape[0] // batches
        cols = jnp.concatenate(
            [
                columns_of(asked_ref[pl.ds(phase * per + n, 1), :] - first, LANES)
                for n in range(per)
            ]
        )
        lane = lax.broadcasted_iota(jnp.int32, cols.shape, 1)
        hots.append(
            jnp.concatenate(
                [
                    jnp.where(cols == lane + c, 1.0, 0.0).astype(BF16)
                    for c in range(0, tab.shape[0], LANES)
                ],
                axis=1,
            )
        )
    copy.wait()
    for hot, out_ref in zip(hots, out_refs):
        out_ref[...] = jnp.dot(hot, tab[...], preferred_element_type=F32).astype(BF16)


def fetch(asked, batches, table, width, after):
    steps, rows = len(asked), asked[0].size // batches
    return pl.pallas_call(
        functools.partial(fetch_kernel, steps, batches),
        out_shape=[jax.ShapeDtypeStruct((rows, width), BF16)] * steps,
        in_specs=[VMEM] * steps + [HBM] * (1 + len(after)),
        out_specs=[VMEM] * steps,
        scratch_shapes=[pltpu.VMEM((table.shape[0], width), BF16), pltpu.SemaphoreType.DMA],
        compiler_params=params(),
        cost_estimate=pl.CostEstimate(
            flops=2 * steps * rows * width * table.shape[0],
            bytes_accessed=2 * width * table.shape[0],
            transcendentals=0,
        ),
        name="fetch",
    )(*asked, table, *after)


def merge_kernel(a_ref, b_ref, *refs):
    refs[-1][...] = a_ref[...] + b_ref[...]


def merge(a, b, after):
    return pl.pallas_call(
        merge_kernel,
        out_shape=jax.ShapeDtypeStruct(a.shape, BF16),
        in_specs=[VMEM] * 2 + [HBM] * len(after),
        out_specs=VMEM,
        compiler_params=params(),
        name="merge",
    )(a, b, *after)


def hold_kernel(*refs):
    pass


def hold(value, after):
    return pl.pallas_call(
        hold_kernel,
        out_shape=jax.ShapeDtypeStruct(value.shape, value.dtype),
        in_specs=[HBM] * (1 + len(after)),
        out_specs=HBM,
        input_output_aliases={0: 0},
        compiler_params=params(),
        name="hold",
    )(value, *after)


def cut_kernel(near_ref, far_ref, *refs):
    low_ref, high_ref, sems = refs[-3:]
    half = low_ref.shape[0]
    copies = [
        pltpu.make_async_copy(far_ref.at[pl.ds(0, half), :], low_ref, sems.at[0]),
        pltpu.make_async_copy(near_ref.at[pl.ds(half, half), :], high_ref, sems.at[1]),
    ]
    for copy in copies:
        copy.start()
    for copy in copies:
        copy.wait()


def relay(near, far, axis, after):
    half = jax.ShapeDtypeStruct((near.shape[0] // 2,) + near.shape[1:], near.dtype)
    low, high = pl.pallas_call(
        cut_kernel,
        out_shape=[half] * 2,
        in_specs=[HBM] * (2 + len(after)),
        out_specs=[HBM] * 2,
        scratch_shapes=[pltpu.SemaphoreType.DMA((2,))],
        compiler_params=params(),
        name="cut",
    )(near, far, *after)
    return [exchange(low, axis, 1), exchange(high, axis, 2)]


def ask_around(wanted):
    asked, step = [wanted], 1
    while step < lax.axis_size("dp"):
        got = exchange(jnp.concatenate(asked), "dp", step)
        asked = asked + jnp.split(got, step)
        step = 2 * step
    return asked


def gather_in(blocks, first, then):
    blocks, step = dict(enumerate(blocks)), 1
    while step < lax.axis_size("dp"):
        at_end = 2 * step == lax.axis_size("dp")
        for k in sorted((k for k in blocks if k & step), reverse=True):
            got = exchange(blocks.pop(k), "dp", step)
            after = then(blocks[k ^ step]) if at_end else first
            blocks[k ^ step] = merge(blocks[k ^ step], got, after)
            first = [blocks[k ^ step]]
        step = 2 * step
    return blocks[0]


def start_picked(section, own, other, dst, sem):
    phase = lax.axis_index("phase")

    @pl.when(phase == section)
    def _():
        pltpu.make_async_copy(own, dst, sem).start()

    @pl.when(phase != section)
    def _():
        pltpu.make_async_copy(other, dst, sem).start()


def wait_picked(own, dst, sem):
    pltpu.make_async_copy(own, dst, sem).wait()


def start_weights(section, w_own, w_other, w_buf, w_sem):
    for g in range(4):
        start_picked(section, w_own.at[g], w_other.at[g], w_buf.at[g], w_sem.at[g])


def front(x, seg_ref, w_own, w_buf, w_sem, gated_ref):
    rows, local_cols = x.shape[0], w_buf.shape[2]
    xf = x.astype(F32)
    inv = lax.rsqrt(jnp.mean(xf * xf, axis=-1, keepdims=True) + EPS)
    proj = []
    for g in range(4):
        wait_picked(w_own.at[g], w_buf.at[g], w_sem.at[g])
        raw = jnp.dot(x, w_buf[g], preferred_element_type=F32)
        proj.append(silu(raw * inv).astype(BF16))
    gates, values, queries, keys = proj
    seg = seg_ref[0, pl.ds(lax.axis_index("phase"), 1), :]
    seg_cols = columns_of(seg, rows)
    at_row = lax.broadcasted_iota(jnp.int32, (rows, rows), 0)
    at_col = lax.broadcasted_iota(jnp.int32, (rows, rows), 1)
    allowed = (at_col <= at_row) & (seg_cols == seg)
    for h in range(0, local_cols, HD):
        head = slice(h, h + HD)
        scores = lax.dot_general(
            queries[:, head], keys[:, head], (((1,), (1,)), ((), ())), preferred_element_type=F32
        ) * HD ** (-0.5)
        weights = (jnp.where(allowed, silu(scores), 0.0) / rows).astype(BF16)
        mixed = jnp.dot(weights, values[:, head], preferred_element_type=F32)
        mixed = mixed * lax.rsqrt(jnp.mean(mixed * mixed, axis=-1, keepdims=True) + EPS)
        gated_ref[:, head] = (mixed * gates[:, head].astype(F32)).astype(BF16)


def back(x, gated_refs, o_own, o_buf, o_sem):
    steps, cols, width = o_buf.shape
    gated = jnp.concatenate([gated_ref[...] for gated_ref in gated_refs], axis=1)
    for k in range(steps):
        wait_picked(o_own.at[k], o_buf.at[k], o_sem.at[k])
    weights = o_buf[...].reshape(steps * cols, width)
    total = x.astype(F32) + jnp.dot(gated, weights, preferred_element_type=F32)
    return total.astype(BF16)


def first_kernel(steps, places, *refs):
    x_refs, pieces, refs = refs[:steps], refs[steps : steps + len(places)], refs[steps + len(places) :]
    seg_ref, w_own, w_other, gated_ref, x_ref, stack_ref, w_buf, w_sem, o_sem = refs
    start_weights(0, w_own, w_other, w_buf, w_sem)
    copies = []
    for n, (slot, row) in enumerate(places):
        at = stack_ref.at[slot, pl.ds(row, pieces[n].shape[0]), :]
        copies.append(pltpu.make_async_copy(pieces[n], at, o_sem.at[n]))
    for copy in copies:
        copy.start()
    width = x_refs[0].shape[1]
    for k, piece in enumerate(x_refs):
        at = pl.multiple_of(source_of(lax.axis_index("mp"), k, steps) * width, width)
        x_ref[:, pl.ds(at, width)] = piece[...]
    front(x_ref[...], seg_ref, w_own, w_buf, w_sem, gated_ref)
    for copy in copies:
        copy.wait()


def middle_kernel(steps, *refs):
    gated_refs = refs[:steps]
    x_ref, seg_ref, w_own, w_other, o_own, o_other = refs[steps : steps + 6]
    gated_ref, x1_ref, o_buf, o_sem, w_buf, w_sem = refs[steps + 6 :]
    for k in range(steps):
        start_picked(0, o_own.at[k], o_other.at[k], o_buf.at[k], o_sem.at[k])
    start_weights(1, w_own, w_other, w_buf, w_sem)
    x1 = back(x_ref[...], gated_refs, o_own, o_buf, o_sem)
    x1_ref[...] = x1
    front(x1, seg_ref, w_own, w_buf, w_sem, gated_ref)


def last_kernel(steps, *refs):
    gated_refs = refs[:steps]
    x_ref, neigh_ref, w_ref, bias_ref, o_own, o_other, states_ref, ctx_ref = refs[steps : steps + 8]
    o_buf, o_sem = refs[steps + 8 :]
    for k in range(steps):
        start_picked(1, o_own.at[k], o_other.at[k], o_buf.at[k], o_sem.at[k])
    near = neigh_ref[lax.axis_index("phase")]
    row = lax.broadcasted_iota(jnp.int32, (x_ref.shape[0], near.shape[1]), 0)
    share = jnp.zeros(row.shape, F32)
    for n in range(NBR):
        share = share + jnp.where(near[n : n + 1, :] == row, 1.0 / NBR, 0.0)
    share = jnp.transpose(share).astype(BF16)
    states = back(x_ref[...], gated_refs, o_own, o_buf, o_sem)
    states_ref[...] = states
    context = jnp.dot(share, states, preferred_element_type=F32).astype(BF16)
    summed = jnp.dot(context, w_ref[...], preferred_element_type=F32) + bias_ref[...].astype(F32)
    ctx_ref[...] = silu(summed).astype(BF16)


def section_flops(rows, width, local_cols):
    return 2 * rows * (width * 4 * local_cols + 2 * rows * local_cols)


def fetch_rows_padded(owners, item_row, table, width):
    dp_count = lax.axis_size("dp")
    row_total = item_row.shape[0]
    capacity = max(2, 7 * row_total // (4 * dp_count))
    hits = (owners[:, None] == jnp.arange(dp_count, dtype=jnp.int32)[None, :]).astype(jnp.int32)
    rank = jnp.sum((jnp.cumsum(hits, axis=0) - 1) * hits, axis=1)
    slot = owners * capacity + rank
    requests = jnp.full((dp_count * capacity,), -1, jnp.int32).at[slot].set(item_row)
    asked = swap(requests.reshape(dp_count, capacity), "dp")
    part = lax.dynamic_slice_in_dim(table, lax.axis_index("mp") * width, width, 1)
    found = jnp.take(part, jnp.maximum(asked, 0), axis=0)
    return swap(found, "dp").reshape(dp_count * capacity, width)[slot]


def on_device(
    item_owner, item_row, segments, neighbors, table, gains, w_in, w_out, w_ctx, ctx_bias
):
    dp_count, mp_count = lax.axis_size("dp"), lax.axis_size("mp")
    table_rows, width = table.shape
    batches, rows = segments.shape[1], segments.shape[2]
    imps = neighbors.shape[2]
    local_cols = w_out.shape[1]
    part = width // mp_count

    w_own = jnp.transpose(w_in[0], (1, 0, 2)).astype(F32) * gains[0].astype(F32)[None, :, None]
    w_own = w_own.astype(BF16)
    if mp_count == 4:
        near, far = exchange(w_out[0], "mp", 1), exchange(w_out[0], "mp", 2)
        o_pieces, places = [w_out[0], near, far], [(0, 0), (3, 0), (2, 0)]
    else:
        o_pieces, places = spread(w_out[0], "mp"), [(slot, 0) for slot in range(mp_count)]
    neigh = jnp.transpose(neighbors[0], (0, 2, 1))
    bias = ctx_bias.reshape(1, -1)

    if is_pow2(dp_count) and dp_count <= 8:
        wanted = item_owner.reshape(-1, LANES) * table_rows + item_row.reshape(-1, LANES)
        asked = ask_around(wanted)
        w_own = hold(w_own, asked[1:2])
        w_other = exchange(w_own, "phase", 1)
        late = fetch(asked[-1:], batches, table, part, [])
        found = fetch(asked[:-1], batches, table, part, late) + late

        def then(first):
            if mp_count == 4:
                o_pieces.extend(relay(near, far, "mp", [first]))
                places.extend([(1, 0), (1, local_cols // 2)])
            return [w_other]

        piece = gather_in(found, [], then)
    else:
        piece = fetch_rows_padded(item_owner[:, 0], item_row, table, part)
        piece = lax.dynamic_index_in_dim(
            piece.reshape(batches, rows, part), lax.axis_index("phase"), 0, keepdims=False
        )
        w_other = exchange(w_own, "phase", 1)
        if mp_count == 4:
            o_pieces.extend(relay(near, far, "mp", [piece]))
            places.extend([(1, 0), (1, local_cols // 2)])
    x_pieces = spread(piece, "mp")

    sem4 = pltpu.SemaphoreType.DMA((4,))
    semk = pltpu.SemaphoreType.DMA((mp_count,))
    w_buf = pltpu.VMEM((4, width, local_cols), BF16)
    o_buf = pltpu.VMEM((mp_count, local_cols, width), BF16)
    x_shape = jax.ShapeDtypeStruct((rows, width), BF16)
    gated_shape = jax.ShapeDtypeStruct((rows, local_cols), BF16)
    front_flops = section_flops(rows, width, local_cols)
    back_flops = 2 * rows * width * local_cols * mp_count

    gated, x0, o_own = pl.pallas_call(
        functools.partial(first_kernel, mp_count, places),
        out_shape=[
            gated_shape,
            x_shape,
            jax.ShapeDtypeStruct((mp_count, local_cols, width), BF16),
        ],
        in_specs=[VMEM] * mp_count + [HBM] * len(places) + [VMEM] + [HBM] * 2,
        out_specs=[VMEM] * 2 + [HBM],
        scratch_shapes=[w_buf, sem4, pltpu.SemaphoreType.DMA((len(places),))],
        compiler_params=params(),
        cost_estimate=pl.CostEstimate(
            flops=front_flops, bytes_accessed=8 * width * local_cols, transcendentals=0
        ),
        name="section0_front",
    )(*x_pieces, *o_pieces, segments, w_own, w_other)
    o_other = exchange(o_own, "phase", 1)

    gated, x1 = pl.pallas_call(
        functools.partial(middle_kernel, mp_count),
        out_shape=[gated_shape, x_shape],
        in_specs=[VMEM] * (mp_count + 2) + [HBM] * 4,
        out_specs=[VMEM] * 2,
        scratch_shapes=[o_buf, semk, w_buf, sem4],
        compiler_params=params(),
        cost_estimate=pl.CostEstimate(
            flops=front_flops + back_flops,
            bytes_accessed=(8 + 2 * mp_count) * width * local_cols,
            transcendentals=0,
        ),
        name="section0_back_section1_front",
    )(*spread(gated, "mp"), x0, segments, w_own, w_other, o_own, o_other)

    states, ctx = pl.pallas_call(
        functools.partial(last_kernel, mp_count),
        out_shape=[x_shape, jax.ShapeDtypeStruct((imps, w_ctx.shape[1]), BF16)],
        in_specs=[VMEM] * (mp_count + 4) + [HBM] * 2,
        out_specs=[VMEM] * 2,
        scratch_shapes=[o_buf, semk],
        compiler_params=params(),
        cost_estimate=pl.CostEstimate(
            flops=back_flops + 2 * imps * width * (rows + w_ctx.shape[1]),
            bytes_accessed=2 * mp_count * width * local_cols,
            transcendentals=0,
        ),
        name="section1_back_context",
    )(*spread(gated, "mp"), x1, neigh, w_ctx, bias, o_own, o_other)

    return (
        states.reshape(1, 1, rows, width),
        ctx.reshape(1, 1, imps, w_ctx.shape[1]),
    )


def solution(mesh):
    in_specs = (
        P("dp", None),
        P("dp"),
        P("dp", None, None),
        P("dp", None, None, None),
        P("dp", None),
        P("phase", None),
        P("phase", None, None, "mp"),
        P("phase", "mp", None),
        P(None, "mp"),
        P("mp"),
    )
    out_specs = (P("dp", "phase", None, None), P("dp", "phase", None, "mp"))
    return jax.shard_map(
        on_device, mesh=mesh, in_specs=in_specs, out_specs=out_specs, check_vma=False
    )
```

```python
import functools

import jax
import jax.numpy as jnp
from jax import lax
from jax.experimental import pallas as pl
from jax.experimental.pallas import tpu as pltpu
from jax.sharding import PartitionSpec as P

HD = 128
NBR = 8
LANES = 128
EPS = 1e-06
VMEM_LIMIT = 20 * 1024 * 1024
VMEM = pl.BlockSpec(memory_space=pltpu.VMEM)
HBM = pl.BlockSpec(memory_space=pltpu.HBM)
F32 = jnp.float32
BF16 = jnp.bfloat16


def params():
    return pltpu.CompilerParams(vmem_limit_bytes=VMEM_LIMIT)


def is_pow2(n):
    return n & (n - 1) == 0


def source_of(me, k, n):
    return me ^ k if is_pow2(n) else lax.rem(me + n - k, n)


def exchange(value, axis, k):
    n = lax.axis_size(axis)
    pairs = [(i, i ^ k if is_pow2(n) else (i + k) % n) for i in range(n)]
    return lax.ppermute(value, axis, pairs)


def spread(value, axis):
    return [value] + [exchange(value, axis, k) for k in range(1, lax.axis_size(axis))]


def swap(blocks, axis):
    return lax.all_to_all(blocks, axis, split_axis=0, concat_axis=0, tiled=True)


def columns_of(row, count):
    return jnp.transpose(jnp.broadcast_to(row, (count, row.shape[1])))


def silu(x):
    return x * jax.nn.sigmoid(x)


def fetch_kernel(steps, batches, *refs):
    asked_refs, table_ref = refs[:steps], refs[steps]
    out_refs, width = refs[-steps:], refs[-1].shape[1]
    first = lax.axis_index("dp") * table_ref.shape[0]
    phase = lax.axis_index("phase")
    hots = []
    for asked_ref in asked_refs:
        per = asked_ref.shape[0] // batches
        cols = jnp.concatenate(
            [
                columns_of(asked_ref[pl.ds(phase * per + n, 1), :] - first, LANES)
                for n in range(per)
            ]
        )
        lane = lax.broadcasted_iota(jnp.int32, cols.shape, 1)
        hots.append(
            jnp.concatenate(
                [
                    jnp.where(cols == lane + c, 1.0, 0.0).astype(BF16)
                    for c in range(0, table_ref.shape[0], LANES)
                ],
                axis=1,
            )
        )
    held = table_ref[:, pl.ds(pl.multiple_of(lax.axis_index("mp") * width, width), width)]
    for hot, out_ref in zip(hots, out_refs):
        out_ref[...] = jnp.dot(hot, held, preferred_element_type=F32).astype(BF16)


def fetch(asked, batches, table, width, after):
    steps, rows = len(asked), asked[0].size // batches
    return pl.pallas_call(
        functools.partial(fetch_kernel, steps, batches),
        out_shape=[jax.ShapeDtypeStruct((rows, width), BF16)] * steps,
        in_specs=[VMEM] * (steps + 1) + [HBM] * len(after),
        out_specs=[VMEM] * steps,
        compiler_params=params(),
        cost_estimate=pl.CostEstimate(
            flops=8 * steps * rows * width * table.shape[0],
            bytes_accessed=2 * width * table.shape[0],
            transcendentals=0,
        ),
        name="fetch",
    )(*asked, table, *after)


def merge_kernel(a_ref, b_ref, *refs):
    refs[-1][...] = a_ref[...] + b_ref[...]


def merge(a, b, after):
    return pl.pallas_call(
        merge_kernel,
        out_shape=jax.ShapeDtypeStruct(a.shape, BF16),
        in_specs=[VMEM] * 2 + [HBM] * len(after),
        out_specs=VMEM,
        compiler_params=params(),
        name="merge",
    )(a, b, *after)


def hold_kernel(*refs):
    pass


def hold(value, after):
    return pl.pallas_call(
        hold_kernel,
        out_shape=jax.ShapeDtypeStruct(value.shape, value.dtype),
        in_specs=[HBM] * (1 + len(after)),
        out_specs=HBM,
        input_output_aliases={0: 0},
        compiler_params=params(),
        name="hold",
    )(value, *after)


def cut_kernel(near_ref, far_ref, *refs):
    low_ref, high_ref, sems = refs[-3:]
    half = low_ref.shape[0]
    copies = [
        pltpu.make_async_copy(far_ref.at[pl.ds(0, half), :], low_ref, sems.at[0]),
        pltpu.make_async_copy(near_ref.at[pl.ds(half, half), :], high_ref, sems.at[1]),
    ]
    for copy in copies:
        copy.start()
    for copy in copies:
        copy.wait()


def relay(near, far, axis, after):
    half = jax.ShapeDtypeStruct((near.shape[0] // 2,) + near.shape[1:], near.dtype)
    low, high = pl.pallas_call(
        cut_kernel,
        out_shape=[half] * 2,
        in_specs=[HBM] * (2 + len(after)),
        out_specs=[HBM] * 2,
        scratch_shapes=[pltpu.SemaphoreType.DMA((2,))],
        compiler_params=params(),
        name="cut",
    )(near, far, *after)
    return [exchange(low, axis, 1), exchange(high, axis, 2)]


def ask_around(wanted):
    asked, step = [wanted], 1
    while step < lax.axis_size("dp"):
        got = exchange(jnp.concatenate(asked), "dp", step)
        asked = asked + jnp.split(got, step)
        step = 2 * step
    return asked


def gather_in(blocks, first, then):
    blocks, step = dict(enumerate(blocks)), 1
    while step < lax.axis_size("dp"):
        at_end = 2 * step == lax.axis_size("dp")
        for k in sorted((k for k in blocks if k & step), reverse=True):
            got = exchange(blocks.pop(k), "dp", step)
            after = then(blocks[k ^ step]) if at_end else first
            blocks[k ^ step] = merge(blocks[k ^ step], got, after)
            first = [blocks[k ^ step]]
        step = 2 * step
    return blocks[0]


def prepare_kernel(seg_ref, neigh_ref, mask_ref, share_ref):
    phase, rows, imps = lax.axis_index("phase"), mask_ref.shape[0], share_ref.shape[0]
    seg = seg_ref[0, pl.ds(phase, 1), :]
    at_row = lax.broadcasted_iota(jnp.int32, (rows, rows), 0)
    at_col = lax.broadcasted_iota(jnp.int32, (rows, rows), 1)
    allowed = (at_col <= at_row) & (columns_of(seg, rows) == seg)
    mask_ref[...] = jnp.where(allowed, 1.0 / rows, 0.0)
    near = neigh_ref[phase]
    row = lax.broadcasted_iota(jnp.int32, (rows, imps), 0)
    share = jnp.zeros((rows, imps), F32)
    for n in range(NBR):
        share = share + jnp.where(near[n : n + 1, :] == row, 1.0 / NBR, 0.0)
    share_ref[...] = jnp.transpose(share).astype(BF16)


def prepare(segments, neigh):
    rows, imps = segments.shape[2], neigh.shape[2]
    return pl.pallas_call(
        prepare_kernel,
        out_shape=[
            jax.ShapeDtypeStruct((rows, rows), F32),
            jax.ShapeDtypeStruct((imps, rows), BF16),
        ],
        in_specs=[VMEM] * 2,
        out_specs=[VMEM] * 2,
        compiler_params=params(),
        cost_estimate=pl.CostEstimate(
            flops=16 * rows * imps, bytes_accessed=8 * rows * rows, transcendentals=0
        ),
        name="prepare",
    )(segments, neigh)


def by_phase(body, zero, one):
    phase = lax.axis_index("phase")
    pl.when(phase == 0)(functools.partial(body, *zero))
    pl.when(phase != 0)(functools.partial(body, *one))


def front(x, mask_ref, w_ref, gated_ref):
    local_cols = w_ref.shape[2]
    xf = x.astype(F32)
    inv = lax.rsqrt(jnp.mean(xf * xf, axis=-1, keepdims=True) + EPS)
    proj = []
    for g in range(4):
        raw = jnp.dot(x, w_ref[g], preferred_element_type=F32)
        proj.append(silu(raw * inv).astype(BF16))
    gates, values, queries, keys = proj
    mask = mask_ref[...]
    for h in range(0, local_cols, HD):
        head = slice(h, h + HD)
        scores = lax.dot_general(
            queries[:, head], keys[:, head], (((1,), (1,)), ((), ())), preferred_element_type=F32
        ) * HD ** (-0.5)
        weights = (silu(scores) * mask).astype(BF16)
        mixed = jnp.dot(weights, values[:, head], preferred_element_type=F32)
        mixed = mixed * lax.rsqrt(jnp.mean(mixed * mixed, axis=-1, keepdims=True) + EPS)
        gated_ref[:, head] = (mixed * gates[:, head].astype(F32)).astype(BF16)


def back(x, gated_refs, o_ref):
    steps, cols, width = o_ref.shape
    gated = jnp.concatenate([gated_ref[...] for gated_ref in gated_refs], axis=1)
    weights = o_ref[...].reshape(steps * cols, width)
    total = x.astype(F32) + jnp.dot(gated, weights, preferred_element_type=F32)
    return total.astype(BF16)


def first_kernel(steps, places, *refs):
    x_refs, pieces, refs = refs[:steps], refs[steps : steps + len(places)], refs[steps + len(places) :]
    mask_ref, w_own, w_other, gated_ref, x_ref, stack_ref, sems = refs
    copies = []
    for n, (k, row) in enumerate(places):
        at = stack_ref.at[k, pl.ds(row, pieces[n].shape[0]), :]
        copies.append(pltpu.make_async_copy(pieces[n], at, sems.at[n]))
    for copy in copies:
        copy.start()
    width = x_refs[0].shape[1]
    for k, piece in enumerate(x_refs):
        at = pl.multiple_of(source_of(lax.axis_index("mp"), k, steps) * width, width)
        x_ref[:, pl.ds(at, width)] = piece[...]

    def body(w_ref):
        front(x_ref[...], mask_ref, w_ref, gated_ref)

    by_phase(body, [w_own], [w_other])
    for copy in copies:
        copy.wait()


def middle_kernel(steps, *refs):
    gated_refs = refs[:steps]
    x_ref, mask_ref, w_own, w_other, o_own, o_other, gated_ref, x1_ref = refs[steps:]

    def body(o_ref, w_ref):
        x1 = back(x_ref[...], gated_refs, o_ref)
        x1_ref[...] = x1
        front(x1, mask_ref, w_ref, gated_ref)

    by_phase(body, [o_own, w_other], [o_other, w_own])


def last_kernel(steps, *refs):
    gated_refs = refs[:steps]
    x_ref, share_ref, w_ref, bias_ref, o_own, o_other, states_ref, ctx_ref = refs[steps:]

    def body(o_ref):
        states = back(x_ref[...], gated_refs, o_ref)
        states_ref[...] = states
        context = jnp.dot(share_ref[...], states, preferred_element_type=F32).astype(BF16)
        summed = jnp.dot(context, w_ref[...], preferred_element_type=F32)
        ctx_ref[...] = silu(summed + bias_ref[...].astype(F32)).astype(BF16)

    by_phase(body, [o_other], [o_own])


def section_flops(rows, width, local_cols):
    return 2 * rows * (width * 4 * local_cols + 2 * rows * local_cols)


def fetch_rows_padded(owners, item_row, table, width):
    dp_count = lax.axis_size("dp")
    row_total = item_row.shape[0]
    capacity = max(2, 7 * row_total // (4 * dp_count))
    hits = (owners[:, None] == jnp.arange(dp_count, dtype=jnp.int32)[None, :]).astype(jnp.int32)
    rank = jnp.sum((jnp.cumsum(hits, axis=0) - 1) * hits, axis=1)
    slot = owners * capacity + rank
    requests = jnp.full((dp_count * capacity,), -1, jnp.int32).at[slot].set(item_row)
    asked = swap(requests.reshape(dp_count, capacity), "dp")
    part = lax.dynamic_slice_in_dim(table, lax.axis_index("mp") * width, width, 1)
    found = jnp.take(part, jnp.maximum(asked, 0), axis=0)
    return swap(found, "dp").reshape(dp_count * capacity, width)[slot]


def on_device(
    item_owner, item_row, segments, neighbors, table, gains, w_in, w_out, w_ctx, ctx_bias
):
    dp_count, mp_count = lax.axis_size("dp"), lax.axis_size("mp")
    table_rows, width = table.shape
    batches, rows = segments.shape[1], segments.shape[2]
    imps = neighbors.shape[2]
    local_cols = w_out.shape[1]
    part = width // mp_count

    w_own = jnp.transpose(w_in[0], (1, 0, 2)) * gains[0][None, :, None]
    if mp_count == 4:
        near, far = exchange(w_out[0], "mp", 1), exchange(w_out[0], "mp", 2)
        o_pieces, places = [w_out[0], near, far], [(0, 0), (1, 0), (2, 0)]
    else:
        o_pieces, places = spread(w_out[0], "mp"), [(k, 0) for k in range(mp_count)]
    neigh = jnp.transpose(neighbors[0], (0, 2, 1))
    bias = ctx_bias.reshape(1, -1)
    mask, share = prepare(segments, neigh)

    if is_pow2(dp_count) and dp_count <= 8:
        wanted = item_owner.reshape(-1, LANES) * table_rows + item_row.reshape(-1, LANES)
        asked = ask_around(wanted)
        w_own = hold(w_own, asked[1:2])
        w_other = exchange(w_own, "phase", 1)
        late = fetch(asked[-1:], batches, table, part, [])
        found = fetch(asked[:-1], batches, table, part, late) + late

        def then(first):
            if mp_count == 4:
                o_pieces.extend(relay(near, far, "mp", [first]))
                places.extend([(3, 0), (3, local_cols // 2)])
            return [w_other]

        piece = gather_in(found, [], then)
    else:
        piece = fetch_rows_padded(item_owner[:, 0], item_row, table, part)
        piece = lax.dynamic_index_in_dim(
            piece.reshape(batches, rows, part), lax.axis_index("phase"), 0, keepdims=False
        )
        w_other = exchange(w_own, "phase", 1)
        if mp_count == 4:
            o_pieces.extend(relay(near, far, "mp", [piece]))
            places.extend([(3, 0), (3, local_cols // 2)])
    x_pieces = spread(piece, "mp")

    x_shape = jax.ShapeDtypeStruct((rows, width), BF16)
    gated_shape = jax.ShapeDtypeStruct((rows, local_cols), BF16)
    front_flops = section_flops(rows, width, local_cols)
    back_flops = 2 * rows * width * local_cols * mp_count

    gated, x0, o_own = pl.pallas_call(
        functools.partial(first_kernel, mp_count, places),
        out_shape=[
            gated_shape,
            x_shape,
            jax.ShapeDtypeStruct((mp_count, local_cols, width), BF16),
        ],
        in_specs=[VMEM] * mp_count + [HBM] * len(places) + [VMEM] * 3,
        out_specs=[VMEM] * 2 + [HBM],
        scratch_shapes=[pltpu.SemaphoreType.DMA((len(places),))],
        compiler_params=params(),
        cost_estimate=pl.CostEstimate(
            flops=front_flops, bytes_accessed=8 * width * local_cols, transcendentals=0
        ),
        name="section0_front",
    )(*x_pieces, *o_pieces, mask, w_own, w_other)
    o_other = exchange(o_own, "phase", 1)

    gated, x1 = pl.pallas_call(
        functools.partial(middle_kernel, mp_count),
        out_shape=[gated_shape, x_shape],
        in_specs=[VMEM] * (mp_count + 6),
        out_specs=[VMEM] * 2,
        compiler_params=params(),
        cost_estimate=pl.CostEstimate(
            flops=front_flops + back_flops,
            bytes_accessed=(8 + 2 * mp_count) * width * local_cols,
            transcendentals=0,
        ),
        name="section0_back_section1_front",
    )(*spread(gated, "mp"), x0, mask, w_own, w_other, o_own, o_other)

    states, ctx = pl.pallas_call(
        functools.partial(last_kernel, mp_count),
        out_shape=[x_shape, jax.ShapeDtypeStruct((imps, w_ctx.shape[1]), BF16)],
        in_specs=[VMEM] * (mp_count + 6),
        out_specs=[VMEM] * 2,
        compiler_params=params(),
        cost_estimate=pl.CostEstimate(
            flops=back_flops + 2 * imps * width * (rows + w_ctx.shape[1]),
            bytes_accessed=2 * mp_count * width * local_cols,
            transcendentals=0,
        ),
        name="section1_back_context",
    )(*spread(gated, "mp"), x1, share, w_ctx, bias, o_own, o_other)

    return (
        states.reshape(1, 1, rows, width),
        ctx.reshape(1, 1, imps, w_ctx.shape[1]),
    )


def solution(mesh):
    in_specs = (
        P("dp", None),
        P("dp"),
        P("dp", None, None),
        P("dp", None, None, None),
        P("dp", None),
        P("phase", None),
        P("phase", None, None, "mp"),
        P("phase", "mp", None),
        P(None, "mp"),
        P("mp"),
    )
    out_specs = (P("dp", "phase", None, None), P("dp", "phase", None, "mp"))
    return jax.shard_map(
        on_device, mesh=mesh, in_specs=in_specs, out_specs=out_specs, check_vma=False
    )
```

```python
import functools

import jax
import jax.numpy as jnp
from jax import lax
from jax.experimental import pallas as pl
from jax.experimental.pallas import tpu as pltpu
from jax.sharding import PartitionSpec as P

HD = 128
NBR = 8
LANES = 128
EPS = 1e-06
VMEM_LIMIT = 20 * 1024 * 1024
VMEM = pl.BlockSpec(memory_space=pltpu.VMEM)
HBM = pl.BlockSpec(memory_space=pltpu.HBM)
F32 = jnp.float32
BF16 = jnp.bfloat16


def params():
    return pltpu.CompilerParams(vmem_limit_bytes=VMEM_LIMIT)


def is_pow2(n):
    return n & (n - 1) == 0


def source_of(me, k, n):
    return me ^ k if is_pow2(n) else lax.rem(me + n - k, n)


def exchange(value, axis, k):
    n = lax.axis_size(axis)
    pairs = [(i, i ^ k if is_pow2(n) else (i + k) % n) for i in range(n)]
    return lax.ppermute(value, axis, pairs)


def spread(value, axis):
    return [value] + [exchange(value, axis, k) for k in range(1, lax.axis_size(axis))]


def swap(blocks, axis):
    return lax.all_to_all(blocks, axis, split_axis=0, concat_axis=0, tiled=True)


def columns_of(row, count):
    return jnp.transpose(jnp.broadcast_to(row, (count, row.shape[1])))


def silu(x):
    return x * jax.nn.sigmoid(x)


def fetch_kernel(steps, batches, *refs):
    asked_refs, table_ref = refs[:steps], refs[steps]
    out_refs, width = refs[-steps:], refs[-1].shape[1]
    first = lax.axis_index("dp") * table_ref.shape[0]
    phase = lax.axis_index("phase")
    hots = []
    for asked_ref in asked_refs:
        per = asked_ref.shape[0] // batches
        cols = jnp.concatenate(
            [
                columns_of(asked_ref[pl.ds(phase * per + n, 1), :] - first, LANES)
                for n in range(per)
            ]
        )
        lane = lax.broadcasted_iota(jnp.int32, cols.shape, 1)
        hots.append(
            jnp.concatenate(
                [
                    jnp.where(cols == lane + c, 1.0, 0.0).astype(BF16)
                    for c in range(0, table_ref.shape[0], LANES)
                ],
                axis=1,
            )
        )
    held = table_ref[:, pl.ds(pl.multiple_of(lax.axis_index("mp") * width, width), width)]
    for hot, out_ref in zip(hots, out_refs):
        out_ref[...] = jnp.dot(hot, held, preferred_element_type=F32).astype(BF16)


def fetch(asked, batches, table, width, after):
    steps, rows = len(asked), asked[0].size // batches
    return pl.pallas_call(
        functools.partial(fetch_kernel, steps, batches),
        out_shape=[jax.ShapeDtypeStruct((rows, width), BF16)] * steps,
        in_specs=[VMEM] * (steps + 1) + [HBM] * len(after),
        out_specs=[VMEM] * steps,
        compiler_params=params(),
        cost_estimate=pl.CostEstimate(
            flops=2 * steps * rows * width * table.shape[0],
            bytes_accessed=2 * width * table.shape[0],
            transcendentals=0,
        ),
        name="fetch",
    )(*asked, table, *after)


def merge_kernel(a_ref, b_ref, *refs):
    refs[-1][...] = a_ref[...] + b_ref[...]


def merge(a, b, after):
    return pl.pallas_call(
        merge_kernel,
        out_shape=jax.ShapeDtypeStruct(a.shape, BF16),
        in_specs=[VMEM] * 2 + [HBM] * len(after),
        out_specs=VMEM,
        compiler_params=params(),
        name="merge",
    )(a, b, *after)


def hold_kernel(*refs):
    pass


def hold(value, after):
    return pl.pallas_call(
        hold_kernel,
        out_shape=jax.ShapeDtypeStruct(value.shape, value.dtype),
        in_specs=[HBM] * (1 + len(after)),
        out_specs=HBM,
        input_output_aliases={0: 0},
        compiler_params=params(),
        name="hold",
    )(value, *after)


def cut_kernel(near_ref, far_ref, *refs):
    low_ref, high_ref, sems = refs[-3:]
    half = low_ref.shape[0]
    copies = [
        pltpu.make_async_copy(far_ref.at[pl.ds(0, half), :], low_ref, sems.at[0]),
        pltpu.make_async_copy(near_ref.at[pl.ds(half, half), :], high_ref, sems.at[1]),
    ]
    for copy in copies:
        copy.start()
    for copy in copies:
        copy.wait()


def relay(near, far, axis, after):
    half = jax.ShapeDtypeStruct((near.shape[0] // 2,) + near.shape[1:], near.dtype)
    low, high = pl.pallas_call(
        cut_kernel,
        out_shape=[half] * 2,
        in_specs=[HBM] * (2 + len(after)),
        out_specs=[HBM] * 2,
        scratch_shapes=[pltpu.SemaphoreType.DMA((2,))],
        compiler_params=params(),
        name="cut",
    )(near, far, *after)
    return [exchange(low, axis, 1), exchange(high, axis, 2)]


def ask_around(wanted):
    asked, step = [wanted], 1
    while step < lax.axis_size("dp"):
        got = exchange(jnp.concatenate(asked), "dp", step)
        asked = asked + jnp.split(got, step)
        step = 2 * step
    return asked


def gather_in(blocks, then):
    blocks, step, after, last = dict(enumerate(blocks)), 1, None, []
    while step < lax.axis_size("dp"):
        at_end = 2 * step == lax.axis_size("dp")
        for k in sorted((k for k in blocks if k & step), reverse=True):
            got = exchange(blocks.pop(k), "dp", step)
            blocks[k ^ step] = merge(blocks[k ^ step], got, last if at_end else after or [])
            if after is None:
                after, last = then(blocks[k ^ step])
            else:
                after = [blocks[k ^ step]]
        step = 2 * step
    return blocks[0]


def prepare_kernel(seg_ref, neigh_ref, mask_ref, share_ref):
    phase, rows, imps = lax.axis_index("phase"), mask_ref.shape[0], share_ref.shape[0]
    seg = seg_ref[0, pl.ds(phase, 1), :]
    at_row = lax.broadcasted_iota(jnp.int32, (rows, rows), 0)
    at_col = lax.broadcasted_iota(jnp.int32, (rows, rows), 1)
    allowed = (at_col <= at_row) & (columns_of(seg, rows) == seg)
    mask_ref[...] = jnp.where(allowed, 1.0 / rows, 0.0)
    near = neigh_ref[phase]
    row = lax.broadcasted_iota(jnp.int32, (rows, imps), 0)
    share = jnp.zeros((rows, imps), F32)
    for n in range(NBR):
        share = share + jnp.where(near[n : n + 1, :] == row, 1.0 / NBR, 0.0)
    share_ref[...] = jnp.transpose(share).astype(BF16)


def prepare(segments, neigh):
    rows, imps = segments.shape[2], neigh.shape[2]
    return pl.pallas_call(
        prepare_kernel,
        out_shape=[
            jax.ShapeDtypeStruct((rows, rows), F32),
            jax.ShapeDtypeStruct((imps, rows), BF16),
        ],
        in_specs=[VMEM] * 2,
        out_specs=[VMEM] * 2,
        compiler_params=params(),
        cost_estimate=pl.CostEstimate(
            flops=16 * rows * imps, bytes_accessed=8 * rows * rows, transcendentals=0
        ),
        name="prepare",
    )(segments, neigh)


def by_phase(body, zero, one):
    phase = lax.axis_index("phase")
    pl.when(phase == 0)(functools.partial(body, *zero))
    pl.when(phase != 0)(functools.partial(body, *one))


def front(x, mask_ref, w_ref, gated_ref):
    local_cols = w_ref.shape[2]
    xf = x.astype(F32)
    inv = lax.rsqrt(jnp.mean(xf * xf, axis=-1, keepdims=True) + EPS)
    proj = []
    for g in range(4):
        raw = jnp.dot(x, w_ref[g], preferred_element_type=F32)
        proj.append(silu(raw * inv).astype(BF16))
    gates, values, queries, keys = proj
    mask = mask_ref[...]
    for h in range(0, local_cols, HD):
        head = slice(h, h + HD)
        scores = lax.dot_general(
            queries[:, head], keys[:, head], (((1,), (1,)), ((), ())), preferred_element_type=F32
        ) * HD ** (-0.5)
        weights = (silu(scores) * mask).astype(BF16)
        mixed = jnp.dot(weights, values[:, head], preferred_element_type=F32)
        mixed = mixed * lax.rsqrt(jnp.mean(mixed * mixed, axis=-1, keepdims=True) + EPS)
        gated_ref[:, head] = (mixed * gates[:, head].astype(F32)).astype(BF16)


def back(x, gated_refs, o_ref):
    steps, cols, width = o_ref.shape
    gated = jnp.concatenate([gated_ref[...] for gated_ref in gated_refs], axis=1)
    weights = o_ref[...].reshape(steps * cols, width)
    total = x.astype(F32) + jnp.dot(gated, weights, preferred_element_type=F32)
    return total.astype(BF16)


def first_kernel(steps, places, *refs):
    x_refs, pieces, refs = refs[:steps], refs[steps : steps + len(places)], refs[steps + len(places) :]
    mask_ref, w_own, w_other, gated_ref, x_ref, stack_ref, sems = refs
    copies = []
    for n, (k, row) in enumerate(places):
        at = stack_ref.at[k, pl.ds(row, pieces[n].shape[0]), :]
        copies.append(pltpu.make_async_copy(pieces[n], at, sems.at[n]))
    for copy in copies:
        copy.start()
    width = x_refs[0].shape[1]
    for k, piece in enumerate(x_refs):
        at = pl.multiple_of(source_of(lax.axis_index("mp"), k, steps) * width, width)
        x_ref[:, pl.ds(at, width)] = piece[...]

    def body(w_ref):
        front(x_ref[...], mask_ref, w_ref, gated_ref)

    by_phase(body, [w_own], [w_other])
    for copy in copies:
        copy.wait()


def middle_kernel(steps, *refs):
    gated_refs = refs[:steps]
    x_ref, mask_ref, w_own, w_other, o_own, o_other, gated_ref, x1_ref = refs[steps:]

    def body(o_ref, w_ref):
        x1 = back(x_ref[...], gated_refs, o_ref)
        x1_ref[...] = x1
        front(x1, mask_ref, w_ref, gated_ref)

    by_phase(body, [o_own, w_other], [o_other, w_own])


def last_kernel(steps, *refs):
    gated_refs = refs[:steps]
    x_ref, share_ref, w_ref, bias_ref, o_own, o_other, states_ref, ctx_ref = refs[steps:]

    def body(o_ref):
        states = back(x_ref[...], gated_refs, o_ref)
        states_ref[...] = states
        context = jnp.dot(share_ref[...], states, preferred_element_type=F32).astype(BF16)
        summed = jnp.dot(context, w_ref[...], preferred_element_type=F32)
        ctx_ref[...] = silu(summed + bias_ref[...].astype(F32)).astype(BF16)

    by_phase(body, [o_other], [o_own])


def section_flops(rows, width, local_cols):
    return 2 * rows * (width * 4 * local_cols + 2 * rows * local_cols)


def fetch_rows_padded(owners, item_row, table, width):
    dp_count = lax.axis_size("dp")
    row_total = item_row.shape[0]
    capacity = max(2, 7 * row_total // (4 * dp_count))
    hits = (owners[:, None] == jnp.arange(dp_count, dtype=jnp.int32)[None, :]).astype(jnp.int32)
    rank = jnp.sum((jnp.cumsum(hits, axis=0) - 1) * hits, axis=1)
    slot = owners * capacity + rank
    requests = jnp.full((dp_count * capacity,), -1, jnp.int32).at[slot].set(item_row)
    asked = swap(requests.reshape(dp_count, capacity), "dp")
    part = lax.dynamic_slice_in_dim(table, lax.axis_index("mp") * width, width, 1)
    found = jnp.take(part, jnp.maximum(asked, 0), axis=0)
    return swap(found, "dp").reshape(dp_count * capacity, width)[slot]


def on_device(
    item_owner, item_row, segments, neighbors, table, gains, w_in, w_out, w_ctx, ctx_bias
):
    dp_count, mp_count = lax.axis_size("dp"), lax.axis_size("mp")
    table_rows, width = table.shape
    batches, rows = segments.shape[1], segments.shape[2]
    imps = neighbors.shape[2]
    local_cols = w_out.shape[1]
    part = width // mp_count

    w_own = jnp.transpose(w_in[0], (1, 0, 2)) * gains[0][None, :, None]
    if mp_count == 4:
        near, far = exchange(w_out[0], "mp", 1), exchange(w_out[0], "mp", 2)
        o_pieces, places = [w_out[0], near, far], [(0, 0), (1, 0), (2, 0)]
    else:
        o_pieces, places = spread(w_out[0], "mp"), [(k, 0) for k in range(mp_count)]
    neigh = jnp.transpose(neighbors[0], (0, 2, 1))
    bias = ctx_bias.reshape(1, -1)
    mask, share = prepare(segments, neigh)

    if is_pow2(dp_count) and dp_count <= 8:
        wanted = item_owner.reshape(-1, LANES) * table_rows + item_row.reshape(-1, LANES)
        asked = ask_around(wanted)
        w_own = hold(w_own, asked[1:2])
        w_other = exchange(w_own, "phase", 1)
        late = fetch(asked[-1:], batches, table, part, [])
        found = fetch(asked[:-1], batches, table, part, late) + late

        def then(first):
            rest = []
            if mp_count == 4:
                rest = relay(near, far, "mp", [first])
                o_pieces.extend(rest)
                places.extend([(3, 0), (3, local_cols // 2)])
            return [first], [w_other]

        piece = gather_in(found, then)
    else:
        piece = fetch_rows_padded(item_owner[:, 0], item_row, table, part)
        piece = lax.dynamic_index_in_dim(
            piece.reshape(batches, rows, part), lax.axis_index("phase"), 0, keepdims=False
        )
        w_other = exchange(w_own, "phase", 1)
        if mp_count == 4:
            o_pieces.extend(relay(near, far, "mp", [piece]))
            places.extend([(3, 0), (3, local_cols // 2)])
    x_pieces = spread(piece, "mp")

    x_shape = jax.ShapeDtypeStruct((rows, width), BF16)
    gated_shape = jax.ShapeDtypeStruct((rows, local_cols), BF16)
    front_flops = section_flops(rows, width, local_cols)
    back_flops = 2 * rows * width * local_cols * mp_count

    gated, x0, o_own = pl.pallas_call(
        functools.partial(first_kernel, mp_count, places),
        out_shape=[
            gated_shape,
            x_shape,
            jax.ShapeDtypeStruct((mp_count, local_cols, width), BF16),
        ],
        in_specs=[VMEM] * mp_count + [HBM] * len(places) + [VMEM] * 3,
        out_specs=[VMEM] * 2 + [HBM],
        scratch_shapes=[pltpu.SemaphoreType.DMA((len(places),))],
        compiler_params=params(),
        cost_estimate=pl.CostEstimate(
            flops=front_flops, bytes_accessed=8 * width * local_cols, transcendentals=0
        ),
        name="section0_front",
    )(*x_pieces, *o_pieces, mask, w_own, w_other)
    o_other = exchange(o_own, "phase", 1)

    gated, x1 = pl.pallas_call(
        functools.partial(middle_kernel, mp_count),
        out_shape=[gated_shape, x_shape],
        in_specs=[VMEM] * (mp_count + 6),
        out_specs=[VMEM] * 2,
        compiler_params=params(),
        cost_estimate=pl.CostEstimate(
            flops=front_flops + back_flops,
            bytes_accessed=(8 + 2 * mp_count) * width * local_cols,
            transcendentals=0,
        ),
        name="section0_back_section1_front",
    )(*spread(gated, "mp"), x0, mask, w_own, w_other, o_own, o_other)

    states, ctx = pl.pallas_call(
        functools.partial(last_kernel, mp_count),
        out_shape=[x_shape, jax.ShapeDtypeStruct((imps, w_ctx.shape[1]), BF16)],
        in_specs=[VMEM] * (mp_count + 6),
        out_specs=[VMEM] * 2,
        compiler_params=params(),
        cost_estimate=pl.CostEstimate(
            flops=back_flops + 2 * imps * width * (rows + w_ctx.shape[1]),
            bytes_accessed=2 * mp_count * width * local_cols,
            transcendentals=0,
        ),
        name="section1_back_context",
    )(*spread(gated, "mp"), x1, share, w_ctx, bias, o_own, o_other)

    return (
        states.reshape(1, 1, rows, width),
        ctx.reshape(1, 1, imps, w_ctx.shape[1]),
    )


def solution(mesh):
    in_specs = (
        P("dp", None),
        P("dp"),
        P("dp", None, None),
        P("dp", None, None, None),
        P("dp", None),
        P("phase", None),
        P("phase", None, None, "mp"),
        P("phase", "mp", None),
        P(None, "mp"),
        P("mp"),
    )
    out_specs = (P("dp", "phase", None, None), P("dp", "phase", None, "mp"))
    return jax.shard_map(
        on_device, mesh=mesh, in_specs=in_specs, out_specs=out_specs, check_vma=False
    )
```

```python
import functools

import jax
import jax.numpy as jnp
from jax import lax
from jax.experimental import pallas as pl
from jax.experimental.pallas import tpu as pltpu
from jax.sharding import PartitionSpec as P

HD = 128
NBR = 8
LANES = 128
EPS = 1e-06
VMEM_LIMIT = 20 * 1024 * 1024
VMEM = pl.BlockSpec(memory_space=pltpu.VMEM)
HBM = pl.BlockSpec(memory_space=pltpu.HBM)
F32 = jnp.float32
BF16 = jnp.bfloat16


def params():
    return pltpu.CompilerParams(vmem_limit_bytes=VMEM_LIMIT)


def is_pow2(n):
    return n & (n - 1) == 0


def source_of(me, k, n):
    return me ^ k if is_pow2(n) else lax.rem(me + n - k, n)


def exchange(value, axis, k):
    n = lax.axis_size(axis)
    pairs = [(i, i ^ k if is_pow2(n) else (i + k) % n) for i in range(n)]
    return lax.ppermute(value, axis, pairs)


def spread(value, axis):
    return [value] + [exchange(value, axis, k) for k in range(1, lax.axis_size(axis))]


def swap(blocks, axis):
    return lax.all_to_all(blocks, axis, split_axis=0, concat_axis=0, tiled=True)


def columns_of(row, count):
    return jnp.transpose(jnp.broadcast_to(row, (count, row.shape[1])))


def silu(x):
    return x * jax.nn.sigmoid(x)


def fetch_kernel(steps, batches, *refs):
    asked_refs, table_ref = refs[:steps], refs[steps]
    out_refs, width = refs[-steps:], refs[-1].shape[1]
    first = lax.axis_index("dp") * table_ref.shape[0]
    phase = lax.axis_index("phase")
    hots = []
    for asked_ref in asked_refs:
        per = asked_ref.shape[0] // batches
        cols = jnp.concatenate(
            [
                columns_of(asked_ref[pl.ds(phase * per + n, 1), :] - first, LANES)
                for n in range(per)
            ]
        )
        lane = lax.broadcasted_iota(jnp.int32, cols.shape, 1)
        hots.append(
            jnp.concatenate(
                [
                    jnp.where(cols == lane + c, 1.0, 0.0).astype(BF16)
                    for c in range(0, table_ref.shape[0], LANES)
                ],
                axis=1,
            )
        )
    held = table_ref[:, pl.ds(pl.multiple_of(lax.axis_index("mp") * width, width), width)]
    for hot, out_ref in zip(hots, out_refs):
        out_ref[...] = jnp.dot(hot, held, preferred_element_type=F32).astype(BF16)


def fetch(asked, batches, table, width, after):
    steps, rows = len(asked), asked[0].size // batches
    return pl.pallas_call(
        functools.partial(fetch_kernel, steps, batches),
        out_shape=[jax.ShapeDtypeStruct((rows, width), BF16)] * steps,
        in_specs=[VMEM] * (steps + 1) + [HBM] * len(after),
        out_specs=[VMEM] * steps,
        compiler_params=params(),
        cost_estimate=pl.CostEstimate(
            flops=2 * steps * rows * width * table.shape[0],
            bytes_accessed=2 * width * table.shape[0],
            transcendentals=0,
        ),
        name="fetch",
    )(*asked, table, *after)


def merge_kernel(a_ref, b_ref, *refs):
    refs[-1][...] = a_ref[...] + b_ref[...]


def merge(a, b, after):
    return pl.pallas_call(
        merge_kernel,
        out_shape=jax.ShapeDtypeStruct(a.shape, BF16),
        in_specs=[VMEM] * 2 + [HBM] * len(after),
        out_specs=VMEM,
        compiler_params=params(),
        name="merge",
    )(a, b, *after)


def hold_kernel(*refs):
    pass


def hold(value, after, flops=0):
    return pl.pallas_call(
        hold_kernel,
        out_shape=jax.ShapeDtypeStruct(value.shape, value.dtype),
        in_specs=[HBM] * (1 + len(after)),
        out_specs=HBM,
        input_output_aliases={0: 0},
        compiler_params=params(),
        cost_estimate=pl.CostEstimate(flops=flops, bytes_accessed=0, transcendentals=0),
        name="hold",
    )(value, *after)


def cut_kernel(near_ref, far_ref, *refs):
    low_ref, high_ref, sems = refs[-3:]
    half = low_ref.shape[0]
    copies = [
        pltpu.make_async_copy(far_ref.at[pl.ds(0, half), :], low_ref, sems.at[0]),
        pltpu.make_async_copy(near_ref.at[pl.ds(half, half), :], high_ref, sems.at[1]),
    ]
    for copy in copies:
        copy.start()
    for copy in copies:
        copy.wait()


def relay(near, far, after):
    half = jax.ShapeDtypeStruct((near.shape[0] // 2,) + near.shape[1:], near.dtype)
    low, high = pl.pallas_call(
        cut_kernel,
        out_shape=[half] * 2,
        in_specs=[HBM] * (2 + len(after)),
        out_specs=[HBM] * 2,
        scratch_shapes=[pltpu.SemaphoreType.DMA((2,))],
        compiler_params=params(),
        name="cut",
    )(near, far, *after)
    return [exchange(low, "mp", 1), exchange(high, "mp", 2)]


def ask_around(wanted):
    asked, step = [wanted], 1
    while step < lax.axis_size("dp"):
        got = exchange(jnp.concatenate(asked), "dp", step)
        asked = asked + jnp.split(got, step)
        step = 2 * step
    return asked


def gather_in(blocks, first, last):
    blocks, step = dict(enumerate(blocks)), 1
    while step < lax.axis_size("dp"):
        at_end = 2 * step == lax.axis_size("dp")
        for k in sorted((k for k in blocks if k & step), reverse=True):
            got = exchange(blocks.pop(k), "dp", step)
            after = last if at_end else first
            blocks[k ^ step] = merge(blocks[k ^ step], got, after)
            first = [blocks[k ^ step]]
        step = 2 * step
    return blocks[0]


def prepare_kernel(seg_ref, neigh_ref, mask_ref, share_ref):
    phase, rows, imps = lax.axis_index("phase"), mask_ref.shape[0], share_ref.shape[0]
    seg = seg_ref[0, pl.ds(phase, 1), :]
    at_row = lax.broadcasted_iota(jnp.int32, (rows, rows), 0)
    at_col = lax.broadcasted_iota(jnp.int32, (rows, rows), 1)
    allowed = (at_col <= at_row) & (columns_of(seg, rows) == seg)
    mask_ref[...] = jnp.where(allowed, 1.0 / rows, 0.0)
    near = neigh_ref[phase]
    row = lax.broadcasted_iota(jnp.int32, (rows, imps), 0)
    share = jnp.zeros((rows, imps), F32)
    for n in range(NBR):
        share = share + jnp.where(near[n : n + 1, :] == row, 1.0 / NBR, 0.0)
    share_ref[...] = jnp.transpose(share).astype(BF16)


def prepare(segments, neigh):
    rows, imps = segments.shape[2], neigh.shape[2]
    return pl.pallas_call(
        prepare_kernel,
        out_shape=[
            jax.ShapeDtypeStruct((rows, rows), F32),
            jax.ShapeDtypeStruct((imps, rows), BF16),
        ],
        in_specs=[VMEM] * 2,
        out_specs=[VMEM] * 2,
        compiler_params=params(),
        cost_estimate=pl.CostEstimate(
            flops=16 * rows * imps, bytes_accessed=8 * rows * rows, transcendentals=0
        ),
        name="prepare",
    )(segments, neigh)


def by_phase(body, zero, one):
    phase = lax.axis_index("phase")
    pl.when(phase == 0)(functools.partial(body, *zero))
    pl.when(phase != 0)(functools.partial(body, *one))


def front(x, mask_ref, w_ref, gated_ref):
    local_cols = w_ref.shape[2]
    xf = x.astype(F32)
    inv = lax.rsqrt(jnp.mean(xf * xf, axis=-1, keepdims=True) + EPS)
    proj = []
    for g in range(4):
        raw = jnp.dot(x, w_ref[g], preferred_element_type=F32)
        proj.append(silu(raw * inv).astype(BF16))
    gates, values, queries, keys = proj
    mask = mask_ref[...]
    for h in range(0, local_cols, HD):
        head = slice(h, h + HD)
        scores = lax.dot_general(
            queries[:, head], keys[:, head], (((1,), (1,)), ((), ())), preferred_element_type=F32
        ) * HD ** (-0.5)
        weights = (silu(scores) * mask).astype(BF16)
        mixed = jnp.dot(weights, values[:, head], preferred_element_type=F32)
        mixed = mixed * lax.rsqrt(jnp.mean(mixed * mixed, axis=-1, keepdims=True) + EPS)
        gated_ref[:, head] = (mixed * gates[:, head].astype(F32)).astype(BF16)


def back(x, gated_refs, o_refs):
    total, at = x.astype(F32), 0
    for o_ref in o_refs:
        steps, cols, width = o_ref.shape
        gated = jnp.concatenate([ref[...] for ref in gated_refs[at : at + steps]], axis=1)
        weights = o_ref[...].reshape(steps * cols, width)
        total = total + jnp.dot(gated, weights, preferred_element_type=F32)
        at += steps
    return total.astype(BF16)


def stack_copies(pieces, places, stack_ref, sems):
    copies = []
    for n, (k, row) in enumerate(places):
        at = stack_ref.at[k, pl.ds(row, pieces[n].shape[0]), :]
        copies.append(pltpu.make_async_copy(pieces[n], at, sems.at[n]))
    return copies


def stack_kernel(places, *refs):
    copies = stack_copies(refs[: len(places)], places, refs[-2], refs[-1])
    for copy in copies:
        copy.start()
    for copy in copies:
        copy.wait()


def stack(pieces, places, count, after):
    rows, width = sum(piece.shape[0] for piece in pieces) // count, pieces[0].shape[1]
    return pl.pallas_call(
        functools.partial(stack_kernel, places),
        out_shape=jax.ShapeDtypeStruct((count, rows, width), BF16),
        in_specs=[HBM] * (len(pieces) + len(after)),
        out_specs=HBM,
        scratch_shapes=[pltpu.SemaphoreType.DMA((len(places),))],
        compiler_params=params(),
        name="stack",
    )(*pieces, *after)


def first_kernel(steps, places, *refs):
    x_refs, pieces, refs = refs[:steps], refs[steps : steps + len(places)], refs[steps + len(places) :]
    mask_ref, w_own, w_other, gated_ref, x_ref, stack_ref, sems = refs
    copies = stack_copies(pieces, places, stack_ref, sems)
    for copy in copies:
        copy.start()
    width = x_refs[0].shape[1]
    for k, piece in enumerate(x_refs):
        at = pl.multiple_of(source_of(lax.axis_index("mp"), k, steps) * width, width)
        x_ref[:, pl.ds(at, width)] = piece[...]

    def body(w_ref):
        front(x_ref[...], mask_ref, w_ref, gated_ref)

    by_phase(body, [w_own], [w_other])
    for copy in copies:
        copy.wait()


def middle_kernel(steps, parts, *refs):
    gated_refs, refs = refs[:steps], refs[steps:]
    x_ref, mask_ref, w_own, w_other = refs[:4]
    o_own, o_other = refs[4 : 4 + parts], refs[4 + parts : 4 + 2 * parts]
    gated_ref, x1_ref = refs[-2:]

    def body(w_ref, *o_refs):
        x1 = back(x_ref[...], gated_refs, o_refs)
        x1_ref[...] = x1
        front(x1, mask_ref, w_ref, gated_ref)

    by_phase(body, (w_other, *o_own), (w_own, *o_other))


def last_kernel(steps, parts, *refs):
    gated_refs, refs = refs[:steps], refs[steps:]
    x_ref, share_ref, w_ref, bias_ref = refs[:4]
    o_own, o_other = refs[4 : 4 + parts], refs[4 + parts : 4 + 2 * parts]
    states_ref, ctx_ref = refs[-2:]

    def body(*o_refs):
        states = back(x_ref[...], gated_refs, o_refs)
        states_ref[...] = states
        context = jnp.dot(share_ref[...], states, preferred_element_type=F32).astype(BF16)
        summed = jnp.dot(context, w_ref[...], preferred_element_type=F32)
        ctx_ref[...] = silu(summed + bias_ref[...].astype(F32)).astype(BF16)

    by_phase(body, o_other, o_own)


def section_flops(rows, width, local_cols):
    return 2 * rows * (width * 4 * local_cols + 2 * rows * local_cols)


def fetch_rows_padded(owners, item_row, table, width):
    dp_count = lax.axis_size("dp")
    row_total = item_row.shape[0]
    capacity = max(2, 7 * row_total // (4 * dp_count))
    hits = (owners[:, None] == jnp.arange(dp_count, dtype=jnp.int32)[None, :]).astype(jnp.int32)
    rank = jnp.sum((jnp.cumsum(hits, axis=0) - 1) * hits, axis=1)
    slot = owners * capacity + rank
    requests = jnp.full((dp_count * capacity,), -1, jnp.int32).at[slot].set(item_row)
    asked = swap(requests.reshape(dp_count, capacity), "dp")
    part = lax.dynamic_slice_in_dim(table, lax.axis_index("mp") * width, width, 1)
    found = jnp.take(part, jnp.maximum(asked, 0), axis=0)
    return swap(found, "dp").reshape(dp_count * capacity, width)[slot]


def on_device(
    item_owner, item_row, segments, neighbors, table, gains, w_in, w_out, w_ctx, ctx_bias
):
    dp_count, mp_count = lax.axis_size("dp"), lax.axis_size("mp")
    table_rows, width = table.shape
    batches, rows = segments.shape[1], segments.shape[2]
    imps = neighbors.shape[2]
    local_cols = w_out.shape[1]
    part = width // mp_count

    w_own = jnp.transpose(w_in[0], (1, 0, 2)) * gains[0][None, :, None]
    relayed = mp_count == 4
    direct = range(1, 3 if relayed else mp_count)
    pieces = [w_out[0]] + [exchange(w_out[0], "mp", k) for k in direct]
    places = [(k, 0) for k in range(len(pieces))]
    corner = [(0, 0), (0, local_cols // 2)]
    neigh = jnp.transpose(neighbors[0], (0, 2, 1))
    bias = ctx_bias.reshape(1, -1)
    mask, share = prepare(segments, neigh)

    if is_pow2(dp_count) and dp_count <= 8:
        wanted = item_owner.reshape(-1, LANES) * table_rows + item_row.reshape(-1, LANES)
        asked = ask_around(wanted)
        w_own = hold(w_own, asked[1:2])
        w_other = exchange(w_own, "phase", 1)
        late = fetch(asked[-1:], batches, table, part, [])
        found = fetch(asked[:-1], batches, table, part, late) + late

        piece = gather_in(found, [], [w_other])
    else:
        piece = fetch_rows_padded(item_owner[:, 0], item_row, table, part)
        piece = lax.dynamic_index_in_dim(
            piece.reshape(batches, rows, part), lax.axis_index("phase"), 0, keepdims=False
        )
        w_other = exchange(w_own, "phase", 1)
    x_pieces = spread(piece, "mp")

    x_shape = jax.ShapeDtypeStruct((rows, width), BF16)
    gated_shape = jax.ShapeDtypeStruct((rows, local_cols), BF16)
    front_flops = section_flops(rows, width, local_cols)
    back_flops = 2 * rows * width * local_cols * mp_count

    gated, x0, o_own = pl.pallas_call(
        functools.partial(first_kernel, mp_count, places),
        out_shape=[
            gated_shape,
            x_shape,
            jax.ShapeDtypeStruct((len(pieces), local_cols, width), BF16),
        ],
        in_specs=[VMEM] * mp_count + [HBM] * len(places) + [VMEM] * 3,
        out_specs=[VMEM] * 2 + [HBM],
        scratch_shapes=[pltpu.SemaphoreType.DMA((len(places),))],
        compiler_params=params(),
        cost_estimate=pl.CostEstimate(
            flops=1 * front_flops, bytes_accessed=8 * width * local_cols, transcendentals=0
        ),
        name="section0_front",
    )(*x_pieces, *pieces, mask, w_own, w_other)
    o_own = [o_own]
    if relayed:
        o_own.append(stack(relay(*pieces[1:], [piece]), corner, 1, []))
    o_other = [exchange(block, "phase", 1) for block in o_own]

    arrived = spread(gated, "mp")
    arrived[-1] = hold(arrived[-1], arrived[1:-1], 32 * front_flops)
    gated, x1 = pl.pallas_call(
        functools.partial(middle_kernel, mp_count, len(o_own)),
        out_shape=[gated_shape, x_shape],
        in_specs=[VMEM] * (mp_count + 4 + 2 * len(o_own)),
        out_specs=[VMEM] * 2,
        compiler_params=params(),
        cost_estimate=pl.CostEstimate(
            flops=front_flops + back_flops,
            bytes_accessed=(8 + 2 * mp_count) * width * local_cols,
            transcendentals=0,
        ),
        name="section0_back_section1_front",
    )(*arrived, x0, mask, w_own, w_other, *o_own, *o_other)

    states, ctx = pl.pallas_call(
        functools.partial(last_kernel, mp_count, len(o_own)),
        out_shape=[x_shape, jax.ShapeDtypeStruct((imps, w_ctx.shape[1]), BF16)],
        in_specs=[VMEM] * (mp_count + 4 + 2 * len(o_own)),
        out_specs=[VMEM] * 2,
        compiler_params=params(),
        cost_estimate=pl.CostEstimate(
            flops=back_flops + 2 * imps * width * (rows + w_ctx.shape[1]),
            bytes_accessed=2 * mp_count * width * local_cols,
            transcendentals=0,
        ),
        name="section1_back_context",
    )(*spread(gated, "mp"), x1, share, w_ctx, bias, *o_own, *o_other)

    return (
        states.reshape(1, 1, rows, width),
        ctx.reshape(1, 1, imps, w_ctx.shape[1]),
    )


def solution(mesh):
    in_specs = (
        P("dp", None),
        P("dp"),
        P("dp", None, None),
        P("dp", None, None, None),
        P("dp", None),
        P("phase", None),
        P("phase", None, None, "mp"),
        P("phase", "mp", None),
        P(None, "mp"),
        P("mp"),
    )
    out_specs = (P("dp", "phase", None, None), P("dp", "phase", None, "mp"))
    return jax.shard_map(
        on_device, mesh=mesh, in_specs=in_specs, out_specs=out_specs, check_vma=False
    )
```

```python
import functools

import jax
import jax.numpy as jnp
from jax import lax
from jax.experimental import pallas as pl
from jax.experimental.pallas import tpu as pltpu
from jax.sharding import PartitionSpec as P

HD = 128
NBR = 8
LANES = 128
EPS = 1e-06
VMEM_LIMIT = 20 * 1024 * 1024
VMEM = pl.BlockSpec(memory_space=pltpu.VMEM)
HBM = pl.BlockSpec(memory_space=pltpu.HBM)
F32 = jnp.float32
BF16 = jnp.bfloat16


def params():
    return pltpu.CompilerParams(vmem_limit_bytes=VMEM_LIMIT)


def is_pow2(n):
    return n & (n - 1) == 0


def source_of(me, k, n):
    return me ^ k if is_pow2(n) else lax.rem(me + n - k, n)


def exchange(value, axis, k):
    n = lax.axis_size(axis)
    pairs = [(i, i ^ k if is_pow2(n) else (i + k) % n) for i in range(n)]
    return lax.ppermute(value, axis, pairs)


def spread(value, axis):
    return [value] + [exchange(value, axis, k) for k in range(1, lax.axis_size(axis))]


def swap(blocks, axis):
    return lax.all_to_all(blocks, axis, split_axis=0, concat_axis=0, tiled=True)


def columns_of(row, count):
    return jnp.transpose(jnp.broadcast_to(row, (count, row.shape[1])))


def silu(x):
    return x * jax.nn.sigmoid(x)


def fetch_kernel(steps, batches, *refs):
    asked_refs, table_ref = refs[:steps], refs[steps]
    out_refs, width = refs[-steps:], refs[-1].shape[1]
    first = lax.axis_index("dp") * table_ref.shape[0]
    phase = lax.axis_index("phase")
    hots = []
    for asked_ref in asked_refs:
        per = asked_ref.shape[0] // batches
        cols = jnp.concatenate(
            [
                columns_of(asked_ref[pl.ds(phase * per + n, 1), :] - first, LANES)
                for n in range(per)
            ]
        )
        lane = lax.broadcasted_iota(jnp.int32, cols.shape, 1)
        hots.append(
            jnp.concatenate(
                [
                    jnp.where(cols == lane + c, 1.0, 0.0).astype(BF16)
                    for c in range(0, table_ref.shape[0], LANES)
                ],
                axis=1,
            )
        )
    held = table_ref[:, pl.ds(pl.multiple_of(lax.axis_index("mp") * width, width), width)]
    for hot, out_ref in zip(hots, out_refs):
        out_ref[...] = jnp.dot(hot, held, preferred_element_type=F32).astype(BF16)


def fetch(asked, batches, table, width, after):
    steps, rows = len(asked), asked[0].size // batches
    return pl.pallas_call(
        functools.partial(fetch_kernel, steps, batches),
        out_shape=[jax.ShapeDtypeStruct((rows, width), BF16)] * steps,
        in_specs=[VMEM] * (steps + 1) + [HBM] * len(after),
        out_specs=[VMEM] * steps,
        compiler_params=params(),
        cost_estimate=pl.CostEstimate(
            flops=2 * steps * rows * width * table.shape[0],
            bytes_accessed=2 * width * table.shape[0],
            transcendentals=0,
        ),
        name="fetch",
    )(*asked, table, *after)


def merge_kernel(count, *refs):
    total = refs[0][...]
    for ref in refs[1:count]:
        total = total + ref[...]
    refs[-1][...] = total


def merge(a, b, more, after):
    count = 2 + len(more)
    return pl.pallas_call(
        functools.partial(merge_kernel, count),
        out_shape=jax.ShapeDtypeStruct(a.shape, BF16),
        in_specs=[VMEM] * count + [HBM] * len(after),
        out_specs=VMEM,
        compiler_params=params(),
        name="merge",
    )(a, b, *more, *after)


def hold_kernel(*refs):
    pass


def hold(value, after, flops=0):
    return pl.pallas_call(
        hold_kernel,
        out_shape=jax.ShapeDtypeStruct(value.shape, value.dtype),
        in_specs=[HBM] * (1 + len(after)),
        out_specs=HBM,
        input_output_aliases={0: 0},
        compiler_params=params(),
        cost_estimate=pl.CostEstimate(flops=flops, bytes_accessed=0, transcendentals=0),
        name="hold",
    )(value, *after)


def cut_kernel(near_ref, far_ref, *refs):
    low_ref, high_ref, sems = refs[-3:]
    half = low_ref.shape[0]
    copies = [
        pltpu.make_async_copy(far_ref.at[pl.ds(0, half), :], low_ref, sems.at[0]),
        pltpu.make_async_copy(near_ref.at[pl.ds(half, half), :], high_ref, sems.at[1]),
    ]
    for copy in copies:
        copy.start()
    for copy in copies:
        copy.wait()


def relay(near, far, after):
    half = jax.ShapeDtypeStruct((near.shape[0] // 2,) + near.shape[1:], near.dtype)
    low, high = pl.pallas_call(
        cut_kernel,
        out_shape=[half] * 2,
        in_specs=[HBM] * (2 + len(after)),
        out_specs=[HBM] * 2,
        scratch_shapes=[pltpu.SemaphoreType.DMA((2,))],
        compiler_params=params(),
        name="cut",
    )(near, far, *after)
    return [exchange(low, "mp", 1), exchange(high, "mp", 2)]


def ask_around(wanted):
    asked, step = [wanted], 1
    while step < lax.axis_size("dp"):
        got = exchange(jnp.concatenate(asked), "dp", step)
        asked = asked + jnp.split(got, step)
        step = 2 * step
    return asked


def gather_in(blocks, last):
    n = lax.axis_size("dp")
    blocks, step, late, first = dict(enumerate(blocks)), 1, [], None
    while step < n:
        for k in sorted((k for k in blocks if k & step), reverse=True):
            block = blocks.pop(k)
            if k == step and 2 * step < n:
                late.append((block, step))
                continue
            got = exchange(block, "dp", step)
            if 2 * step == n:
                got = hold(got, [], 32 * 10**9)
                late = [exchange(hold(b, [first] if first is not None else []), "dp", at) for b, at in late]
                blocks[k ^ step] = merge(blocks[k ^ step], got, late, last)
            else:
                blocks[k ^ step] = merge(blocks[k ^ step], got, [], [])
            first = blocks[k ^ step]
        step = 2 * step
    return blocks[0]


def prepare_kernel(seg_ref, neigh_ref, mask_ref, share_ref):
    phase, rows, imps = lax.axis_index("phase"), mask_ref.shape[0], share_ref.shape[0]
    seg = seg_ref[0, pl.ds(phase, 1), :]
    at_row = lax.broadcasted_iota(jnp.int32, (rows, rows), 0)
    at_col = lax.broadcasted_iota(jnp.int32, (rows, rows), 1)
    allowed = (at_col <= at_row) & (columns_of(seg, rows) == seg)
    mask_ref[...] = jnp.where(allowed, 1.0 / rows, 0.0)
    near = neigh_ref[phase]
    row = lax.broadcasted_iota(jnp.int32, (rows, imps), 0)
    share = jnp.zeros((rows, imps), F32)
    for n in range(NBR):
        share = share + jnp.where(near[n : n + 1, :] == row, 1.0 / NBR, 0.0)
    share_ref[...] = jnp.transpose(share).astype(BF16)


def prepare(segments, neigh):
    rows, imps = segments.shape[2], neigh.shape[2]
    return pl.pallas_call(
        prepare_kernel,
        out_shape=[
            jax.ShapeDtypeStruct((rows, rows), F32),
            jax.ShapeDtypeStruct((imps, rows), BF16),
        ],
        in_specs=[VMEM] * 2,
        out_specs=[VMEM] * 2,
        compiler_params=params(),
        cost_estimate=pl.CostEstimate(
            flops=16 * rows * imps, bytes_accessed=8 * rows * rows, transcendentals=0
        ),
        name="prepare",
    )(segments, neigh)


def by_phase(body, zero, one):
    phase = lax.axis_index("phase")
    pl.when(phase == 0)(functools.partial(body, *zero))
    pl.when(phase != 0)(functools.partial(body, *one))


def front(x, mask_ref, w_ref, gated_ref):
    local_cols = w_ref.shape[2]
    xf = x.astype(F32)
    inv = lax.rsqrt(jnp.mean(xf * xf, axis=-1, keepdims=True) + EPS)
    proj = []
    for g in range(4):
        raw = jnp.dot(x, w_ref[g], preferred_element_type=F32)
        proj.append(silu(raw * inv).astype(BF16))
    gates, values, queries, keys = proj
    mask = mask_ref[...]
    for h in range(0, local_cols, HD):
        head = slice(h, h + HD)
        scores = lax.dot_general(
            queries[:, head], keys[:, head], (((1,), (1,)), ((), ())), preferred_element_type=F32
        ) * HD ** (-0.5)
        weights = (silu(scores) * mask).astype(BF16)
        mixed = jnp.dot(weights, values[:, head], preferred_element_type=F32)
        mixed = mixed * lax.rsqrt(jnp.mean(mixed * mixed, axis=-1, keepdims=True) + EPS)
        gated_ref[:, head] = (mixed * gates[:, head].astype(F32)).astype(BF16)


def back(x, gated_refs, o_refs):
    total, at = x.astype(F32), 0
    for o_ref in o_refs:
        steps, cols, width = o_ref.shape
        gated = jnp.concatenate([ref[...] for ref in gated_refs[at : at + steps]], axis=1)
        weights = o_ref[...].reshape(steps * cols, width)
        total = total + jnp.dot(gated, weights, preferred_element_type=F32)
        at += steps
    return total.astype(BF16)


def stack_copies(pieces, places, stack_ref, sems):
    copies = []
    for n, (k, row) in enumerate(places):
        at = stack_ref.at[k, pl.ds(row, pieces[n].shape[0]), :]
        copies.append(pltpu.make_async_copy(pieces[n], at, sems.at[n]))
    return copies


def stack_kernel(places, *refs):
    copies = stack_copies(refs[: len(places)], places, refs[-2], refs[-1])
    for copy in copies:
        copy.start()
    for copy in copies:
        copy.wait()


def stack(pieces, places, count, after):
    rows, width = sum(piece.shape[0] for piece in pieces) // count, pieces[0].shape[1]
    return pl.pallas_call(
        functools.partial(stack_kernel, places),
        out_shape=jax.ShapeDtypeStruct((count, rows, width), BF16),
        in_specs=[HBM] * (len(pieces) + len(after)),
        out_specs=HBM,
        scratch_shapes=[pltpu.SemaphoreType.DMA((len(places),))],
        compiler_params=params(),
        name="stack",
    )(*pieces, *after)


def first_kernel(steps, places, *refs):
    x_refs, pieces, refs = refs[:steps], refs[steps : steps + len(places)], refs[steps + len(places) :]
    mask_ref, w_own, w_other, gated_ref, x_ref, stack_ref, sems = refs
    copies = stack_copies(pieces, places, stack_ref, sems)
    for copy in copies:
        copy.start()
    width = x_refs[0].shape[1]
    for k, piece in enumerate(x_refs):
        at = pl.multiple_of(source_of(lax.axis_index("mp"), k, steps) * width, width)
        x_ref[:, pl.ds(at, width)] = piece[...]

    def body(w_ref):
        front(x_ref[...], mask_ref, w_ref, gated_ref)

    by_phase(body, [w_own], [w_other])
    for copy in copies:
        copy.wait()


def middle_kernel(steps, parts, *refs):
    gated_refs, refs = refs[:steps], refs[steps:]
    x_ref, mask_ref, w_own, w_other = refs[:4]
    o_own, o_other = refs[4 : 4 + parts], refs[4 + parts : 4 + 2 * parts]
    gated_ref, x1_ref = refs[-2:]

    def body(w_ref, *o_refs):
        x1 = back(x_ref[...], gated_refs, o_refs)
        x1_ref[...] = x1
        front(x1, mask_ref, w_ref, gated_ref)

    by_phase(body, (w_other, *o_own), (w_own, *o_other))


def last_kernel(steps, parts, *refs):
    gated_refs, refs = refs[:steps], refs[steps:]
    x_ref, share_ref, w_ref, bias_ref = refs[:4]
    o_own, o_other = refs[4 : 4 + parts], refs[4 + parts : 4 + 2 * parts]
    states_ref, ctx_ref = refs[-2:]

    def body(*o_refs):
        states = back(x_ref[...], gated_refs, o_refs)
        states_ref[...] = states
        context = jnp.dot(share_ref[...], states, preferred_element_type=F32).astype(BF16)
        summed = jnp.dot(context, w_ref[...], preferred_element_type=F32)
        ctx_ref[...] = silu(summed + bias_ref[...].astype(F32)).astype(BF16)

    by_phase(body, o_other, o_own)


def section_flops(rows, width, local_cols):
    return 2 * rows * (width * 4 * local_cols + 2 * rows * local_cols)


def fetch_rows_padded(owners, item_row, table, width):
    dp_count = lax.axis_size("dp")
    row_total = item_row.shape[0]
    capacity = max(2, 7 * row_total // (4 * dp_count))
    hits = (owners[:, None] == jnp.arange(dp_count, dtype=jnp.int32)[None, :]).astype(jnp.int32)
    rank = jnp.sum((jnp.cumsum(hits, axis=0) - 1) * hits, axis=1)
    slot = owners * capacity + rank
    requests = jnp.full((dp_count * capacity,), -1, jnp.int32).at[slot].set(item_row)
    asked = swap(requests.reshape(dp_count, capacity), "dp")
    part = lax.dynamic_slice_in_dim(table, lax.axis_index("mp") * width, width, 1)
    found = jnp.take(part, jnp.maximum(asked, 0), axis=0)
    return swap(found, "dp").reshape(dp_count * capacity, width)[slot]


def on_device(
    item_owner, item_row, segments, neighbors, table, gains, w_in, w_out, w_ctx, ctx_bias
):
    dp_count, mp_count = lax.axis_size("dp"), lax.axis_size("mp")
    table_rows, width = table.shape
    batches, rows = segments.shape[1], segments.shape[2]
    imps = neighbors.shape[2]
    local_cols = w_out.shape[1]
    part = width // mp_count

    w_own = jnp.transpose(w_in[0], (1, 0, 2)) * gains[0][None, :, None]
    relayed = mp_count == 4
    direct = range(1, 3 if relayed else mp_count)
    pieces = [w_out[0]] + [exchange(w_out[0], "mp", k) for k in direct]
    places = [(k, 0) for k in range(len(pieces))]
    corner = [(0, 0), (0, local_cols // 2)]
    neigh = jnp.transpose(neighbors[0], (0, 2, 1))
    bias = ctx_bias.reshape(1, -1)
    mask, share = prepare(segments, neigh)

    if is_pow2(dp_count) and dp_count <= 8:
        wanted = item_owner.reshape(-1, LANES) * table_rows + item_row.reshape(-1, LANES)
        asked = ask_around(wanted)
        w_own = hold(w_own, asked[1:2])
        w_other = exchange(w_own, "phase", 1)
        late = fetch(asked[-1:], batches, table, part, [])
        found = fetch(asked[:-1], batches, table, part, late) + late

        piece = gather_in(found, [])
    else:
        piece = fetch_rows_padded(item_owner[:, 0], item_row, table, part)
        piece = lax.dynamic_index_in_dim(
            piece.reshape(batches, rows, part), lax.axis_index("phase"), 0, keepdims=False
        )
        w_other = exchange(w_own, "phase", 1)
    x_pieces = spread(piece, "mp")

    x_shape = jax.ShapeDtypeStruct((rows, width), BF16)
    gated_shape = jax.ShapeDtypeStruct((rows, local_cols), BF16)
    front_flops = section_flops(rows, width, local_cols)
    back_flops = 2 * rows * width * local_cols * mp_count

    gated, x0, o_own = pl.pallas_call(
        functools.partial(first_kernel, mp_count, places),
        out_shape=[
            gated_shape,
            x_shape,
            jax.ShapeDtypeStruct((len(pieces), local_cols, width), BF16),
        ],
        in_specs=[VMEM] * mp_count + [HBM] * len(places) + [VMEM] * 3,
        out_specs=[VMEM] * 2 + [HBM],
        scratch_shapes=[pltpu.SemaphoreType.DMA((len(places),))],
        compiler_params=params(),
        cost_estimate=pl.CostEstimate(
            flops=1 * front_flops, bytes_accessed=8 * width * local_cols, transcendentals=0
        ),
        name="section0_front",
    )(*x_pieces, *pieces, mask, w_own, w_other)
    o_own = [o_own]
    if relayed:
        o_own.append(stack(relay(*pieces[1:], [piece]), corner, 1, []))
    o_other = [exchange(block, "phase", 1) for block in o_own]

    arrived = spread(gated, "mp")
    arrived[-1] = hold(arrived[-1], arrived[1:-1], 32 * front_flops)
    gated, x1 = pl.pallas_call(
        functools.partial(middle_kernel, mp_count, len(o_own)),
        out_shape=[gated_shape, x_shape],
        in_specs=[VMEM] * (mp_count + 4 + 2 * len(o_own)),
        out_specs=[VMEM] * 2,
        compiler_params=params(),
        cost_estimate=pl.CostEstimate(
            flops=front_flops + back_flops,
            bytes_accessed=(8 + 2 * mp_count) * width * local_cols,
            transcendentals=0,
        ),
        name="section0_back_section1_front",
    )(*arrived, x0, mask, w_own, w_other, *o_own, *o_other)

    states, ctx = pl.pallas_call(
        functools.partial(last_kernel, mp_count, len(o_own)),
        out_shape=[x_shape, jax.ShapeDtypeStruct((imps, w_ctx.shape[1]), BF16)],
        in_specs=[VMEM] * (mp_count + 4 + 2 * len(o_own)),
        out_specs=[VMEM] * 2,
        compiler_params=params(),
        cost_estimate=pl.CostEstimate(
            flops=back_flops + 2 * imps * width * (rows + w_ctx.shape[1]),
            bytes_accessed=2 * mp_count * width * local_cols,
            transcendentals=0,
        ),
        name="section1_back_context",
    )(*spread(gated, "mp"), x1, share, w_ctx, bias, *o_own, *o_other)

    return (
        states.reshape(1, 1, rows, width),
        ctx.reshape(1, 1, imps, w_ctx.shape[1]),
    )


def solution(mesh):
    in_specs = (
        P("dp", None),
        P("dp"),
        P("dp", None, None),
        P("dp", None, None, None),
        P("dp", None),
        P("phase", None),
        P("phase", None, None, "mp"),
        P("phase", "mp", None),
        P(None, "mp"),
        P("mp"),
    )
    out_specs = (P("dp", "phase", None, None), P("dp", "phase", None, "mp"))
    return jax.shard_map(
        on_device, mesh=mesh, in_specs=in_specs, out_specs=out_specs, check_vma=False
    )
```

```python
import functools

import jax
import jax.numpy as jnp
from jax import lax
from jax.experimental import pallas as pl
from jax.experimental.pallas import tpu as pltpu
from jax.sharding import PartitionSpec as P

HD = 128
NBR = 8
LANES = 128
EPS = 1e-06
VMEM_LIMIT = 20 * 1024 * 1024
VMEM = pl.BlockSpec(memory_space=pltpu.VMEM)
HBM = pl.BlockSpec(memory_space=pltpu.HBM)
F32 = jnp.float32
BF16 = jnp.bfloat16


def params():
    return pltpu.CompilerParams(vmem_limit_bytes=VMEM_LIMIT)


def is_pow2(n):
    return n & (n - 1) == 0


def source_of(me, k, n):
    return me ^ k if is_pow2(n) else lax.rem(me + n - k, n)


def exchange(value, axis, k):
    n = lax.axis_size(axis)
    pairs = [(i, i ^ k if is_pow2(n) else (i + k) % n) for i in range(n)]
    return lax.ppermute(value, axis, pairs)


def spread(value, axis):
    return [value] + [exchange(value, axis, k) for k in range(1, lax.axis_size(axis))]


def swap(blocks, axis):
    return lax.all_to_all(blocks, axis, split_axis=0, concat_axis=0, tiled=True)


def columns_of(row, count):
    return jnp.transpose(jnp.broadcast_to(row, (count, row.shape[1])))


def silu(x):
    return x * jax.nn.sigmoid(x)


def begin_kernel(table_rows, owner_ref, row_ref, gain_ref, wanted_ref, column_ref):
    wanted_ref[...] = owner_ref[...] * table_rows + row_ref[...]
    gain = gain_ref[...].astype(F32)
    column_ref[...] = jnp.concatenate(
        [gain[:, c : c + LANES] for c in range(0, gain.shape[1], LANES)], axis=0
    )


def begin(item_owner, item_row, gains, table_rows):
    owners, at = item_owner.reshape(-1, LANES), item_row.reshape(-1, LANES)
    width = gains.shape[1]
    wanted, gain = pl.pallas_call(
        functools.partial(begin_kernel, table_rows),
        out_shape=[
            jax.ShapeDtypeStruct(at.shape, jnp.int32),
            jax.ShapeDtypeStruct((width // LANES, LANES), F32),
        ],
        in_specs=[VMEM] * 3,
        out_specs=[VMEM] * 2,
        compiler_params=params(),
        name="begin",
    )(owners, at, gains)
    return wanted, gain.reshape(width)


def fetch_kernel(steps, batches, *refs):
    asked_refs, table_ref = refs[:steps], refs[steps]
    out_refs, width = refs[-steps:], refs[-1].shape[1]
    first = lax.axis_index("dp") * table_ref.shape[0]
    phase = lax.axis_index("phase")
    hots = []
    for asked_ref in asked_refs:
        per = asked_ref.shape[0] // batches
        cols = jnp.concatenate(
            [
                columns_of(asked_ref[pl.ds(phase * per + n, 1), :] - first, LANES)
                for n in range(per)
            ]
        )
        lane = lax.broadcasted_iota(jnp.int32, cols.shape, 1)
        hots.append(
            jnp.concatenate(
                [
                    jnp.where(cols == lane + c, 1.0, 0.0).astype(BF16)
                    for c in range(0, table_ref.shape[0], LANES)
                ],
                axis=1,
            )
        )
    held = table_ref[:, pl.ds(pl.multiple_of(lax.axis_index("mp") * width, width), width)]
    for hot, out_ref in zip(hots, out_refs):
        out_ref[...] = jnp.dot(hot, held, preferred_element_type=F32).astype(BF16)


def fetch(asked, batches, table, width, after):
    steps, rows = len(asked), asked[0].size // batches
    return pl.pallas_call(
        functools.partial(fetch_kernel, steps, batches),
        out_shape=[jax.ShapeDtypeStruct((rows, width), BF16)] * steps,
        in_specs=[VMEM] * (steps + 1) + [HBM] * len(after),
        out_specs=[VMEM] * steps,
        compiler_params=params(),
        cost_estimate=pl.CostEstimate(
            flops=2 * steps * rows * width * table.shape[0],
            bytes_accessed=2 * width * table.shape[0],
            transcendentals=0,
        ),
        name="fetch",
    )(*asked, table, *after)


def merge_kernel(a_ref, b_ref, *refs):
    refs[-1][...] = a_ref[...] + b_ref[...]


def merge(a, b, after):
    return pl.pallas_call(
        merge_kernel,
        out_shape=jax.ShapeDtypeStruct(a.shape, BF16),
        in_specs=[VMEM] * 2 + [HBM] * len(after),
        out_specs=VMEM,
        compiler_params=params(),
        name="merge",
    )(a, b, *after)


def hold_kernel(*refs):
    pass


def hold(value, after, flops=0):
    return pl.pallas_call(
        hold_kernel,
        out_shape=jax.ShapeDtypeStruct(value.shape, value.dtype),
        in_specs=[HBM] * (1 + len(after)),
        out_specs=HBM,
        input_output_aliases={0: 0},
        compiler_params=params(),
        cost_estimate=pl.CostEstimate(flops=flops, bytes_accessed=0, transcendentals=0),
        name="hold",
    )(value, *after)


def cut_kernel(near_ref, far_ref, *refs):
    low_ref, high_ref, sems = refs[-3:]
    half = low_ref.shape[0]
    copies = [
        pltpu.make_async_copy(far_ref.at[pl.ds(0, half), :], low_ref, sems.at[0]),
        pltpu.make_async_copy(near_ref.at[pl.ds(half, half), :], high_ref, sems.at[1]),
    ]
    for copy in copies:
        copy.start()
    for copy in copies:
        copy.wait()


def relay(near, far, after):
    half = jax.ShapeDtypeStruct((near.shape[0] // 2,) + near.shape[1:], near.dtype)
    low, high = pl.pallas_call(
        cut_kernel,
        out_shape=[half] * 2,
        in_specs=[HBM] * (2 + len(after)),
        out_specs=[HBM] * 2,
        scratch_shapes=[pltpu.SemaphoreType.DMA((2,))],
        compiler_params=params(),
        name="cut",
    )(near, far, *after)
    return [exchange(low, "mp", 1), exchange(high, "mp", 2)]


def ask_around(wanted):
    asked, step = [wanted], 1
    while step < lax.axis_size("dp"):
        got = exchange(jnp.concatenate(asked), "dp", step)
        asked = asked + jnp.split(got, step)
        step = 2 * step
    return asked


def gather_in(blocks, first, last):
    blocks, step = dict(enumerate(blocks)), 1
    while step < lax.axis_size("dp"):
        at_end = 2 * step == lax.axis_size("dp")
        for k in sorted((k for k in blocks if k & step), reverse=True):
            got = exchange(blocks.pop(k), "dp", step)
            after = last if at_end else first
            blocks[k ^ step] = merge(blocks[k ^ step], got, after)
            first = [blocks[k ^ step]]
        step = 2 * step
    return blocks[0]


def prepare_kernel(seg_ref, neigh_ref, mask_ref, share_ref):
    phase, rows, imps = lax.axis_index("phase"), mask_ref.shape[0], share_ref.shape[0]
    seg = seg_ref[0, pl.ds(phase, 1), :]
    at_row = lax.broadcasted_iota(jnp.int32, (rows, rows), 0)
    at_col = lax.broadcasted_iota(jnp.int32, (rows, rows), 1)
    allowed = (at_col <= at_row) & (columns_of(seg, rows) == seg)
    mask_ref[...] = jnp.where(allowed, 1.0 / rows, 0.0)
    near = neigh_ref[phase]
    row = lax.broadcasted_iota(jnp.int32, (rows, imps), 0)
    share = jnp.zeros((rows, imps), F32)
    for n in range(NBR):
        share = share + jnp.where(near[n : n + 1, :] == row, 1.0 / NBR, 0.0)
    share_ref[...] = jnp.transpose(share).astype(BF16)


def prepare(segments, neigh):
    rows, imps = segments.shape[2], neigh.shape[2]
    return pl.pallas_call(
        prepare_kernel,
        out_shape=[
            jax.ShapeDtypeStruct((rows, rows), F32),
            jax.ShapeDtypeStruct((imps, rows), BF16),
        ],
        in_specs=[VMEM] * 2,
        out_specs=[VMEM] * 2,
        compiler_params=params(),
        cost_estimate=pl.CostEstimate(
            flops=16 * rows * imps, bytes_accessed=8 * rows * rows, transcendentals=0
        ),
        name="prepare",
    )(segments, neigh)


def by_phase(body, zero, one):
    phase = lax.axis_index("phase")
    pl.when(phase == 0)(functools.partial(body, *zero))
    pl.when(phase != 0)(functools.partial(body, *one))


def front(x, mask_ref, w_ref, gated_ref):
    local_cols = w_ref.shape[2]
    xf = x.astype(F32)
    inv = lax.rsqrt(jnp.mean(xf * xf, axis=-1, keepdims=True) + EPS)
    proj = []
    for g in range(4):
        raw = jnp.dot(x, w_ref[g], preferred_element_type=F32)
        proj.append(silu(raw * inv).astype(BF16))
    gates, values, queries, keys = proj
    mask = mask_ref[...]
    for h in range(0, local_cols, HD):
        head = slice(h, h + HD)
        scores = lax.dot_general(
            queries[:, head], keys[:, head], (((1,), (1,)), ((), ())), preferred_element_type=F32
        ) * HD ** (-0.5)
        weights = (silu(scores) * mask).astype(BF16)
        mixed = jnp.dot(weights, values[:, head], preferred_element_type=F32)
        mixed = mixed * lax.rsqrt(jnp.mean(mixed * mixed, axis=-1, keepdims=True) + EPS)
        gated_ref[:, head] = (mixed * gates[:, head].astype(F32)).astype(BF16)


def back(x, gated_refs, o_refs):
    total, at = x.astype(F32), 0
    for o_ref in o_refs:
        steps, cols, width = o_ref.shape
        gated = jnp.concatenate([ref[...] for ref in gated_refs[at : at + steps]], axis=1)
        weights = o_ref[...].reshape(steps * cols, width)
        total = total + jnp.dot(gated, weights, preferred_element_type=F32)
        at += steps
    return total.astype(BF16)


def stack_copies(pieces, places, stack_ref, sems):
    copies = []
    for n, (k, row) in enumerate(places):
        at = stack_ref.at[k, pl.ds(row, pieces[n].shape[0]), :]
        copies.append(pltpu.make_async_copy(pieces[n], at, sems.at[n]))
    return copies


def stack_kernel(places, *refs):
    copies = stack_copies(refs[: len(places)], places, refs[-2], refs[-1])
    for copy in copies:
        copy.start()
    for copy in copies:
        copy.wait()


def stack(pieces, places, count, after):
    rows, width = sum(piece.shape[0] for piece in pieces) // count, pieces[0].shape[1]
    return pl.pallas_call(
        functools.partial(stack_kernel, places),
        out_shape=jax.ShapeDtypeStruct((count, rows, width), BF16),
        in_specs=[HBM] * (len(pieces) + len(after)),
        out_specs=HBM,
        scratch_shapes=[pltpu.SemaphoreType.DMA((len(places),))],
        compiler_params=params(),
        name="stack",
    )(*pieces, *after)


def first_kernel(steps, places, *refs):
    x_refs, pieces, refs = refs[:steps], refs[steps : steps + len(places)], refs[steps + len(places) :]
    mask_ref, w_own, w_other, gated_ref, x_ref, stack_ref, sems = refs
    copies = stack_copies(pieces, places, stack_ref, sems)
    for copy in copies:
        copy.start()
    width = x_refs[0].shape[1]
    for k, piece in enumerate(x_refs):
        at = pl.multiple_of(source_of(lax.axis_index("mp"), k, steps) * width, width)
        x_ref[:, pl.ds(at, width)] = piece[...]

    def body(w_ref):
        front(x_ref[...], mask_ref, w_ref, gated_ref)

    by_phase(body, [w_own], [w_other])
    for copy in copies:
        copy.wait()


def middle_kernel(steps, parts, *refs):
    gated_refs, refs = refs[:steps], refs[steps:]
    x_ref, mask_ref, w_own, w_other = refs[:4]
    o_own, o_other = refs[4 : 4 + parts], refs[4 + parts : 4 + 2 * parts]
    gated_ref, x1_ref = refs[-2:]

    def body(w_ref, *o_refs):
        x1 = back(x_ref[...], gated_refs, o_refs)
        x1_ref[...] = x1
        front(x1, mask_ref, w_ref, gated_ref)

    by_phase(body, (w_other, *o_own), (w_own, *o_other))


def last_kernel(steps, parts, *refs):
    gated_refs, refs = refs[:steps], refs[steps:]
    x_ref, share_ref, w_ref, bias_ref = refs[:4]
    o_own, o_other = refs[4 : 4 + parts], refs[4 + parts : 4 + 2 * parts]
    states_ref, ctx_ref = refs[-2:]

    def body(*o_refs):
        states = back(x_ref[...], gated_refs, o_refs)
        states_ref[...] = states
        context = jnp.dot(share_ref[...], states, preferred_element_type=F32).astype(BF16)
        summed = jnp.dot(context, w_ref[...], preferred_element_type=F32)
        ctx_ref[...] = silu(summed + bias_ref[...].astype(F32)).astype(BF16)

    by_phase(body, o_other, o_own)


def section_flops(rows, width, local_cols):
    return 2 * rows * (width * 4 * local_cols + 2 * rows * local_cols)


def fetch_rows_padded(owners, item_row, table, width):
    dp_count = lax.axis_size("dp")
    row_total = item_row.shape[0]
    capacity = max(2, 7 * row_total // (4 * dp_count))
    hits = (owners[:, None] == jnp.arange(dp_count, dtype=jnp.int32)[None, :]).astype(jnp.int32)
    rank = jnp.sum((jnp.cumsum(hits, axis=0) - 1) * hits, axis=1)
    slot = owners * capacity + rank
    requests = jnp.full((dp_count * capacity,), -1, jnp.int32).at[slot].set(item_row)
    asked = swap(requests.reshape(dp_count, capacity), "dp")
    part = lax.dynamic_slice_in_dim(table, lax.axis_index("mp") * width, width, 1)
    found = jnp.take(part, jnp.maximum(asked, 0), axis=0)
    return swap(found, "dp").reshape(dp_count * capacity, width)[slot]


def on_device(
    item_owner, item_row, segments, neighbors, table, gains, w_in, w_out, w_ctx, ctx_bias
):
    dp_count, mp_count = lax.axis_size("dp"), lax.axis_size("mp")
    table_rows, width = table.shape
    batches, rows = segments.shape[1], segments.shape[2]
    imps = neighbors.shape[2]
    local_cols = w_out.shape[1]
    part = width // mp_count

    wanted, gain = begin(item_owner, item_row, gains, table_rows)
    w_own = jnp.transpose(w_in[0], (1, 0, 2)).astype(F32) * gain[None, :, None]
    w_own = w_own.astype(BF16)
    relayed = mp_count == 4
    direct = range(1, 3 if relayed else mp_count)
    pieces = [w_out[0]] + [exchange(w_out[0], "mp", k) for k in direct]
    places = [(k, 0) for k in range(len(pieces))]
    corner = [(0, 0), (0, local_cols // 2)]
    neigh = jnp.transpose(neighbors[0], (0, 2, 1))
    bias = ctx_bias.reshape(1, -1)
    mask, share = prepare(segments, neigh)

    if is_pow2(dp_count) and dp_count <= 8:
        asked = ask_around(wanted)
        w_own = hold(w_own, asked[1:2])
        w_other = exchange(w_own, "phase", 1)
        late = fetch(asked[-1:], batches, table, part, [])
        found = fetch(asked[:-1], batches, table, part, late) + late

        piece = gather_in(found, [], [w_other])
    else:
        piece = fetch_rows_padded(item_owner[:, 0], item_row, table, part)
        piece = lax.dynamic_index_in_dim(
            piece.reshape(batches, rows, part), lax.axis_index("phase"), 0, keepdims=False
        )
        w_other = exchange(w_own, "phase", 1)
    x_pieces = spread(piece, "mp")

    x_shape = jax.ShapeDtypeStruct((rows, width), BF16)
    gated_shape = jax.ShapeDtypeStruct((rows, local_cols), BF16)
    front_flops = section_flops(rows, width, local_cols)
    back_flops = 2 * rows * width * local_cols * mp_count

    gated, x0, o_own = pl.pallas_call(
        functools.partial(first_kernel, mp_count, places),
        out_shape=[
            gated_shape,
            x_shape,
            jax.ShapeDtypeStruct((len(pieces), local_cols, width), BF16),
        ],
        in_specs=[VMEM] * mp_count + [HBM] * len(places) + [VMEM] * 3,
        out_specs=[VMEM] * 2 + [HBM],
        scratch_shapes=[pltpu.SemaphoreType.DMA((len(places),))],
        compiler_params=params(),
        cost_estimate=pl.CostEstimate(
            flops=1 * front_flops, bytes_accessed=8 * width * local_cols, transcendentals=0
        ),
        name="section0_front",
    )(*x_pieces, *pieces, mask, w_own, w_other)
    o_own = [o_own]
    if relayed:
        o_own.append(stack(relay(*pieces[1:], [piece]), corner, 1, []))
    o_other = [exchange(block, "phase", 1) for block in o_own]

    arrived = spread(gated, "mp")
    arrived[-1] = hold(arrived[-1], arrived[1:-1], 32 * front_flops)
    gated, x1 = pl.pallas_call(
        functools.partial(middle_kernel, mp_count, len(o_own)),
        out_shape=[gated_shape, x_shape],
        in_specs=[VMEM] * (mp_count + 4 + 2 * len(o_own)),
        out_specs=[VMEM] * 2,
        compiler_params=params(),
        cost_estimate=pl.CostEstimate(
            flops=front_flops + back_flops,
            bytes_accessed=(8 + 2 * mp_count) * width * local_cols,
            transcendentals=0,
        ),
        name="section0_back_section1_front",
    )(*arrived, x0, mask, w_own, w_other, *o_own, *o_other)

    states, ctx = pl.pallas_call(
        functools.partial(last_kernel, mp_count, len(o_own)),
        out_shape=[x_shape, jax.ShapeDtypeStruct((imps, w_ctx.shape[1]), BF16)],
        in_specs=[VMEM] * (mp_count + 4 + 2 * len(o_own)),
        out_specs=[VMEM] * 2,
        compiler_params=params(),
        cost_estimate=pl.CostEstimate(
            flops=back_flops + 2 * imps * width * (rows + w_ctx.shape[1]),
            bytes_accessed=2 * mp_count * width * local_cols,
            transcendentals=0,
        ),
        name="section1_back_context",
    )(*spread(gated, "mp"), x1, share, w_ctx, bias, *o_own, *o_other)

    return (
        states.reshape(1, 1, rows, width),
        ctx.reshape(1, 1, imps, w_ctx.shape[1]),
    )


def solution(mesh):
    in_specs = (
        P("dp", None),
        P("dp"),
        P("dp", None, None),
        P("dp", None, None, None),
        P("dp", None),
        P("phase", None),
        P("phase", None, None, "mp"),
        P("phase", "mp", None),
        P(None, "mp"),
        P("mp"),
    )
    out_specs = (P("dp", "phase", None, None), P("dp", "phase", None, "mp"))
    return jax.shard_map(
        on_device, mesh=mesh, in_specs=in_specs, out_specs=out_specs, check_vma=False
    )
```

```python
import functools

import jax
import jax.numpy as jnp
from jax import lax
from jax.experimental import pallas as pl
from jax.experimental.pallas import tpu as pltpu
from jax.sharding import PartitionSpec as P

HD = 128
NBR = 8
LANES = 128
EPS = 1e-06
VMEM_LIMIT = 20 * 1024 * 1024
VMEM = pl.BlockSpec(memory_space=pltpu.VMEM)
HBM = pl.BlockSpec(memory_space=pltpu.HBM)
F32 = jnp.float32
BF16 = jnp.bfloat16


def params():
    return pltpu.CompilerParams(vmem_limit_bytes=VMEM_LIMIT)


def is_pow2(n):
    return n & (n - 1) == 0


def source_of(me, k, n):
    return me ^ k if is_pow2(n) else lax.rem(me + n - k, n)


def exchange(value, axis, k):
    n = lax.axis_size(axis)
    pairs = [(i, i ^ k if is_pow2(n) else (i + k) % n) for i in range(n)]
    return lax.ppermute(value, axis, pairs)


def spread(value, axis):
    return [value] + [exchange(value, axis, k) for k in range(1, lax.axis_size(axis))]


def swap(blocks, axis):
    return lax.all_to_all(blocks, axis, split_axis=0, concat_axis=0, tiled=True)


def columns_of(row, count):
    return jnp.transpose(jnp.broadcast_to(row, (count, row.shape[1])))


def silu(x):
    return x * jax.nn.sigmoid(x)


def fetch_kernel(steps, batches, *refs):
    asked_refs, table_ref = refs[:steps], refs[steps]
    out_refs, width = refs[-steps:], refs[-1].shape[1]
    me = lax.axis_index("dp")
    phase = lax.axis_index("phase")
    hots = []
    for asked_ref in asked_refs:
        half = asked_ref.shape[0] // 2
        per = half // batches
        cols = []
        for n in range(per):
            at = phase * per + n
            mine = asked_ref[pl.ds(at, 1), :] == me
            row = jnp.where(mine, asked_ref[pl.ds(half + at, 1), :], -1)
            cols.append(columns_of(row, LANES))
        cols = jnp.concatenate(cols)
        lane = lax.broadcasted_iota(jnp.int32, cols.shape, 1)
        hots.append(
            jnp.concatenate(
                [
                    jnp.where(cols == lane + c, 1.0, 0.0).astype(BF16)
                    for c in range(0, table_ref.shape[0], LANES)
                ],
                axis=1,
            )
        )
    held = table_ref[:, pl.ds(pl.multiple_of(lax.axis_index("mp") * width, width), width)]
    for hot, out_ref in zip(hots, out_refs):
        out_ref[...] = jnp.dot(hot, held, preferred_element_type=F32).astype(BF16)


def fetch(asked, batches, table, width, after):
    steps, rows = len(asked), asked[0].size // (2 * batches)
    return pl.pallas_call(
        functools.partial(fetch_kernel, steps, batches),
        out_shape=[jax.ShapeDtypeStruct((rows, width), BF16)] * steps,
        in_specs=[VMEM] * (steps + 1) + [HBM] * len(after),
        out_specs=[VMEM] * steps,
        compiler_params=params(),
        cost_estimate=pl.CostEstimate(
            flops=2 * steps * rows * width * table.shape[0],
            bytes_accessed=2 * width * table.shape[0],
            transcendentals=0,
        ),
        name="fetch",
    )(*asked, table, *after)


def merge_kernel(a_ref, b_ref, *refs):
    refs[-1][...] = a_ref[...] + b_ref[...]


def merge(a, b, after):
    return pl.pallas_call(
        merge_kernel,
        out_shape=jax.ShapeDtypeStruct(a.shape, BF16),
        in_specs=[VMEM] * 2 + [HBM] * len(after),
        out_specs=VMEM,
        compiler_params=params(),
        name="merge",
    )(a, b, *after)


def hold_kernel(*refs):
    pass


def hold(value, after, flops=0):
    return pl.pallas_call(
        hold_kernel,
        out_shape=jax.ShapeDtypeStruct(value.shape, value.dtype),
        in_specs=[HBM] * (1 + len(after)),
        out_specs=HBM,
        input_output_aliases={0: 0},
        compiler_params=params(),
        cost_estimate=pl.CostEstimate(flops=flops, bytes_accessed=0, transcendentals=0),
        name="hold",
    )(value, *after)


def cut_kernel(near_ref, far_ref, *refs):
    low_ref, high_ref, sems = refs[-3:]
    half = low_ref.shape[0]
    copies = [
        pltpu.make_async_copy(far_ref.at[pl.ds(0, half), :], low_ref, sems.at[0]),
        pltpu.make_async_copy(near_ref.at[pl.ds(half, half), :], high_ref, sems.at[1]),
    ]
    for copy in copies:
        copy.start()
    for copy in copies:
        copy.wait()


def relay(near, far, after):
    half = jax.ShapeDtypeStruct((near.shape[0] // 2,) + near.shape[1:], near.dtype)
    low, high = pl.pallas_call(
        cut_kernel,
        out_shape=[half] * 2,
        in_specs=[HBM] * (2 + len(after)),
        out_specs=[HBM] * 2,
        scratch_shapes=[pltpu.SemaphoreType.DMA((2,))],
        compiler_params=params(),
        name="cut",
    )(near, far, *after)
    return [exchange(low, "mp", 1), exchange(high, "mp", 2)]


def ask_around(wanted):
    asked, step = [wanted], 1
    while step < lax.axis_size("dp"):
        got = exchange(jnp.concatenate(asked), "dp", step)
        asked = asked + jnp.split(got, step)
        step = 2 * step
    return asked


def gather_in(blocks, first, last):
    blocks, step = dict(enumerate(blocks)), 1
    while step < lax.axis_size("dp"):
        at_end = 2 * step == lax.axis_size("dp")
        for k in sorted((k for k in blocks if k & step), reverse=True):
            got = exchange(blocks.pop(k), "dp", step)
            after = last if at_end else first
            blocks[k ^ step] = merge(blocks[k ^ step], got, after)
            first = [blocks[k ^ step]]
        step = 2 * step
    return blocks[0]


def prepare_kernel(seg_ref, neigh_ref, mask_ref, share_ref):
    phase, rows, imps = lax.axis_index("phase"), mask_ref.shape[0], share_ref.shape[0]
    seg = seg_ref[0, pl.ds(phase, 1), :]
    at_row = lax.broadcasted_iota(jnp.int32, (rows, rows), 0)
    at_col = lax.broadcasted_iota(jnp.int32, (rows, rows), 1)
    allowed = (at_col <= at_row) & (columns_of(seg, rows) == seg)
    mask_ref[...] = jnp.where(allowed, 1.0 / rows, 0.0)
    near = neigh_ref[phase]
    row = lax.broadcasted_iota(jnp.int32, (rows, imps), 0)
    share = jnp.zeros((rows, imps), F32)
    for n in range(NBR):
        share = share + jnp.where(near[n : n + 1, :] == row, 1.0 / NBR, 0.0)
    share_ref[...] = jnp.transpose(share).astype(BF16)


def prepare(segments, neigh):
    rows, imps = segments.shape[2], neigh.shape[2]
    return pl.pallas_call(
        prepare_kernel,
        out_shape=[
            jax.ShapeDtypeStruct((rows, rows), F32),
            jax.ShapeDtypeStruct((imps, rows), BF16),
        ],
        in_specs=[VMEM] * 2,
        out_specs=[VMEM] * 2,
        compiler_params=params(),
        cost_estimate=pl.CostEstimate(
            flops=16 * rows * imps, bytes_accessed=8 * rows * rows, transcendentals=0
        ),
        name="prepare",
    )(segments, neigh)


def by_phase(body, zero, one):
    phase = lax.axis_index("phase")
    pl.when(phase == 0)(functools.partial(body, *zero))
    pl.when(phase != 0)(functools.partial(body, *one))


def front(x, mask_ref, w_ref, gated_ref):
    local_cols = w_ref.shape[2]
    xf = x.astype(F32)
    inv = lax.rsqrt(jnp.mean(xf * xf, axis=-1, keepdims=True) + EPS)
    proj = []
    for g in range(4):
        raw = jnp.dot(x, w_ref[g], preferred_element_type=F32)
        proj.append(silu(raw * inv).astype(BF16))
    gates, values, queries, keys = proj
    mask = mask_ref[...]
    for h in range(0, local_cols, HD):
        head = slice(h, h + HD)
        scores = lax.dot_general(
            queries[:, head], keys[:, head], (((1,), (1,)), ((), ())), preferred_element_type=F32
        ) * HD ** (-0.5)
        weights = (silu(scores) * mask).astype(BF16)
        mixed = jnp.dot(weights, values[:, head], preferred_element_type=F32)
        mixed = mixed * lax.rsqrt(jnp.mean(mixed * mixed, axis=-1, keepdims=True) + EPS)
        gated_ref[:, head] = (mixed * gates[:, head].astype(F32)).astype(BF16)


def back(x, gated_refs, o_refs):
    total, at = x.astype(F32), 0
    for o_ref in o_refs:
        steps, cols, width = o_ref.shape
        gated = jnp.concatenate([ref[...] for ref in gated_refs[at : at + steps]], axis=1)
        weights = o_ref[...].reshape(steps * cols, width)
        total = total + jnp.dot(gated, weights, preferred_element_type=F32)
        at += steps
    return total.astype(BF16)


def stack_copies(pieces, places, stack_ref, sems):
    copies = []
    for n, (k, row) in enumerate(places):
        at = stack_ref.at[k, pl.ds(row, pieces[n].shape[0]), :]
        copies.append(pltpu.make_async_copy(pieces[n], at, sems.at[n]))
    return copies


def stack_kernel(places, *refs):
    copies = stack_copies(refs[: len(places)], places, refs[-2], refs[-1])
    for copy in copies:
        copy.start()
    for copy in copies:
        copy.wait()


def stack(pieces, places, count, after):
    rows, width = sum(piece.shape[0] for piece in pieces) // count, pieces[0].shape[1]
    return pl.pallas_call(
        functools.partial(stack_kernel, places),
        out_shape=jax.ShapeDtypeStruct((count, rows, width), BF16),
        in_specs=[HBM] * (len(pieces) + len(after)),
        out_specs=HBM,
        scratch_shapes=[pltpu.SemaphoreType.DMA((len(places),))],
        compiler_params=params(),
        name="stack",
    )(*pieces, *after)


def first_kernel(steps, places, *refs):
    x_refs, pieces, refs = refs[:steps], refs[steps : steps + len(places)], refs[steps + len(places) :]
    mask_ref, w_own, w_other, gated_ref, x_ref, stack_ref, sems = refs
    copies = stack_copies(pieces, places, stack_ref, sems)
    for copy in copies:
        copy.start()
    width = x_refs[0].shape[1]
    for k, piece in enumerate(x_refs):
        at = pl.multiple_of(source_of(lax.axis_index("mp"), k, steps) * width, width)
        x_ref[:, pl.ds(at, width)] = piece[...]

    def body(w_ref):
        front(x_ref[...], mask_ref, w_ref, gated_ref)

    by_phase(body, [w_own], [w_other])
    for copy in copies:
        copy.wait()


def middle_kernel(steps, parts, *refs):
    gated_refs, refs = refs[:steps], refs[steps:]
    x_ref, mask_ref, w_own, w_other = refs[:4]
    o_own, o_other = refs[4 : 4 + parts], refs[4 + parts : 4 + 2 * parts]
    gated_ref, x1_ref = refs[-2:]

    def body(w_ref, *o_refs):
        x1 = back(x_ref[...], gated_refs, o_refs)
        x1_ref[...] = x1
        front(x1, mask_ref, w_ref, gated_ref)

    by_phase(body, (w_other, *o_own), (w_own, *o_other))


def last_kernel(steps, parts, *refs):
    gated_refs, refs = refs[:steps], refs[steps:]
    x_ref, share_ref, w_ref, bias_ref = refs[:4]
    o_own, o_other = refs[4 : 4 + parts], refs[4 + parts : 4 + 2 * parts]
    states_ref, ctx_ref = refs[-2:]

    def body(*o_refs):
        states = back(x_ref[...], gated_refs, o_refs)
        states_ref[...] = states
        context = jnp.dot(share_ref[...], states, preferred_element_type=F32).astype(BF16)
        summed = jnp.dot(context, w_ref[...], preferred_element_type=F32)
        ctx_ref[...] = silu(summed + bias_ref[...].astype(F32)).astype(BF16)

    by_phase(body, o_other, o_own)


def section_flops(rows, width, local_cols):
    return 2 * rows * (width * 4 * local_cols + 2 * rows * local_cols)


def fetch_rows_padded(owners, item_row, table, width):
    dp_count = lax.axis_size("dp")
    row_total = item_row.shape[0]
    capacity = max(2, 7 * row_total // (4 * dp_count))
    hits = (owners[:, None] == jnp.arange(dp_count, dtype=jnp.int32)[None, :]).astype(jnp.int32)
    rank = jnp.sum((jnp.cumsum(hits, axis=0) - 1) * hits, axis=1)
    slot = owners * capacity + rank
    requests = jnp.full((dp_count * capacity,), -1, jnp.int32).at[slot].set(item_row)
    asked = swap(requests.reshape(dp_count, capacity), "dp")
    part = lax.dynamic_slice_in_dim(table, lax.axis_index("mp") * width, width, 1)
    found = jnp.take(part, jnp.maximum(asked, 0), axis=0)
    return swap(found, "dp").reshape(dp_count * capacity, width)[slot]


def on_device(
    item_owner, item_row, segments, neighbors, table, gains, w_in, w_out, w_ctx, ctx_bias
):
    dp_count, mp_count = lax.axis_size("dp"), lax.axis_size("mp")
    table_rows, width = table.shape
    batches, rows = segments.shape[1], segments.shape[2]
    imps = neighbors.shape[2]
    local_cols = w_out.shape[1]
    part = width // mp_count

    w_own = jnp.transpose(w_in[0], (1, 0, 2)) * gains[0][None, :, None]
    relayed = mp_count == 4
    direct = range(1, 3 if relayed else mp_count)
    pieces = [w_out[0]] + [exchange(w_out[0], "mp", k) for k in direct]
    places = [(k, 0) for k in range(len(pieces))]
    corner = [(0, 0), (0, local_cols // 2)]
    neigh = jnp.transpose(neighbors[0], (0, 2, 1))
    bias = ctx_bias.reshape(1, -1)
    mask, share = prepare(segments, neigh)

    if is_pow2(dp_count) and dp_count <= 8:
        wanted = jnp.concatenate([item_owner.reshape(-1, LANES), item_row.reshape(-1, LANES)])
        asked = ask_around(wanted)
        w_own = hold(w_own, asked[1:2])
        w_other = exchange(w_own, "phase", 1)
        late = fetch(asked[-1:], batches, table, part, [])
        found = fetch(asked[:-1], batches, table, part, late) + late

        piece = gather_in(found, [], [w_other])
    else:
        piece = fetch_rows_padded(item_owner[:, 0], item_row, table, part)
        piece = lax.dynamic_index_in_dim(
            piece.reshape(batches, rows, part), lax.axis_index("phase"), 0, keepdims=False
        )
        w_other = exchange(w_own, "phase", 1)
    x_pieces = spread(piece, "mp")

    x_shape = jax.ShapeDtypeStruct((rows, width), BF16)
    gated_shape = jax.ShapeDtypeStruct((rows, local_cols), BF16)
    front_flops = section_flops(rows, width, local_cols)
    back_flops = 2 * rows * width * local_cols * mp_count

    gated, x0, o_own = pl.pallas_call(
        functools.partial(first_kernel, mp_count, places),
        out_shape=[
            gated_shape,
            x_shape,
            jax.ShapeDtypeStruct((len(pieces), local_cols, width), BF16),
        ],
        in_specs=[VMEM] * mp_count + [HBM] * len(places) + [VMEM] * 3,
        out_specs=[VMEM] * 2 + [HBM],
        scratch_shapes=[pltpu.SemaphoreType.DMA((len(places),))],
        compiler_params=params(),
        cost_estimate=pl.CostEstimate(
            flops=1 * front_flops, bytes_accessed=8 * width * local_cols, transcendentals=0
        ),
        name="section0_front",
    )(*x_pieces, *pieces, mask, w_own, w_other)
    o_own = [o_own]
    if relayed:
        o_own.append(stack(relay(*pieces[1:], [piece]), corner, 1, []))
    o_other = [exchange(block, "phase", 1) for block in o_own]

    arrived = spread(gated, "mp")
    arrived[-1] = hold(arrived[-1], arrived[1:-1], 32 * front_flops)
    gated, x1 = pl.pallas_call(
        functools.partial(middle_kernel, mp_count, len(o_own)),
        out_shape=[gated_shape, x_shape],
        in_specs=[VMEM] * (mp_count + 4 + 2 * len(o_own)),
        out_specs=[VMEM] * 2,
        compiler_params=params(),
        cost_estimate=pl.CostEstimate(
            flops=front_flops + back_flops,
            bytes_accessed=(8 + 2 * mp_count) * width * local_cols,
            transcendentals=0,
        ),
        name="section0_back_section1_front",
    )(*arrived, x0, mask, w_own, w_other, *o_own, *o_other)

    states, ctx = pl.pallas_call(
        functools.partial(last_kernel, mp_count, len(o_own)),
        out_shape=[x_shape, jax.ShapeDtypeStruct((imps, w_ctx.shape[1]), BF16)],
        in_specs=[VMEM] * (mp_count + 4 + 2 * len(o_own)),
        out_specs=[VMEM] * 2,
        compiler_params=params(),
        cost_estimate=pl.CostEstimate(
            flops=back_flops + 2 * imps * width * (rows + w_ctx.shape[1]),
            bytes_accessed=2 * mp_count * width * local_cols,
            transcendentals=0,
        ),
        name="section1_back_context",
    )(*spread(gated, "mp"), x1, share, w_ctx, bias, *o_own, *o_other)

    return (
        states.reshape(1, 1, rows, width),
        ctx.reshape(1, 1, imps, w_ctx.shape[1]),
    )


def solution(mesh):
    in_specs = (
        P("dp", None),
        P("dp"),
        P("dp", None, None),
        P("dp", None, None, None),
        P("dp", None),
        P("phase", None),
        P("phase", None, None, "mp"),
        P("phase", "mp", None),
        P(None, "mp"),
        P("mp"),
    )
    out_specs = (P("dp", "phase", None, None), P("dp", "phase", None, "mp"))
    return jax.shard_map(
        on_device, mesh=mesh, in_specs=in_specs, out_specs=out_specs, check_vma=False
    )
```

```python
import functools

import jax
import jax.numpy as jnp
from jax import lax
from jax.experimental import pallas as pl
from jax.experimental.pallas import tpu as pltpu
from jax.sharding import PartitionSpec as P

HD = 128
NBR = 8
LANES = 128
EPS = 1e-06
VMEM_LIMIT = 20 * 1024 * 1024
VMEM = pl.BlockSpec(memory_space=pltpu.VMEM)
HBM = pl.BlockSpec(memory_space=pltpu.HBM)
F32 = jnp.float32
BF16 = jnp.bfloat16


def params():
    return pltpu.CompilerParams(vmem_limit_bytes=VMEM_LIMIT)


def is_pow2(n):
    return n & (n - 1) == 0


def source_of(me, k, n):
    return me ^ k if is_pow2(n) else lax.rem(me + n - k, n)


def exchange(value, axis, k):
    n = lax.axis_size(axis)
    pairs = [(i, i ^ k if is_pow2(n) else (i + k) % n) for i in range(n)]
    return lax.ppermute(value, axis, pairs)


def spread(value, axis):
    return [value] + [exchange(value, axis, k) for k in range(1, lax.axis_size(axis))]


def swap(blocks, axis):
    return lax.all_to_all(blocks, axis, split_axis=0, concat_axis=0, tiled=True)


def columns_of(row, count):
    return jnp.transpose(jnp.broadcast_to(row, (count, row.shape[1])))


def silu(x):
    return x * jax.nn.sigmoid(x)


def fetch_kernel(steps, batches, *refs):
    asked_refs, table_ref = refs[:steps], refs[steps]
    out_refs, width = refs[-steps:], refs[-1].shape[1]
    me = lax.axis_index("dp")
    phase = lax.axis_index("phase")
    hots = []
    for asked_ref in asked_refs:
        half = asked_ref.shape[0] // 2
        per = half // batches
        cols = []
        for n in range(per):
            at = phase * per + n
            mine = asked_ref[pl.ds(at, 1), :] == me
            row = jnp.where(mine, asked_ref[pl.ds(half + at, 1), :], -1)
            cols.append(columns_of(row, LANES))
        cols = jnp.concatenate(cols)
        lane = lax.broadcasted_iota(jnp.int32, cols.shape, 1)
        hots.append(
            jnp.concatenate(
                [
                    jnp.where(cols == lane + c, 1.0, 0.0).astype(BF16)
                    for c in range(0, table_ref.shape[0], LANES)
                ],
                axis=1,
            )
        )
    held = table_ref[:, pl.ds(pl.multiple_of(lax.axis_index("mp") * width, width), width)]
    for hot, out_ref in zip(hots, out_refs):
        out_ref[...] = jnp.dot(hot, held, preferred_element_type=F32).astype(BF16)


def fetch(asked, batches, table, width, after):
    steps, rows = len(asked), asked[0].size // (2 * batches)
    return pl.pallas_call(
        functools.partial(fetch_kernel, steps, batches),
        out_shape=[jax.ShapeDtypeStruct((rows, width), BF16)] * steps,
        in_specs=[VMEM] * (steps + 1) + [HBM] * len(after),
        out_specs=[VMEM] * steps,
        compiler_params=params(),
        cost_estimate=pl.CostEstimate(
            flops=2 * steps * rows * width * table.shape[0],
            bytes_accessed=2 * width * table.shape[0],
            transcendentals=0,
        ),
        name="fetch",
    )(*asked, table, *after)


def merge_kernel(a_ref, b_ref, *refs):
    refs[-1][...] = a_ref[...] + b_ref[...]


def merge(a, b, after):
    return pl.pallas_call(
        merge_kernel,
        out_shape=jax.ShapeDtypeStruct(a.shape, BF16),
        in_specs=[VMEM] * 2 + [HBM] * len(after),
        out_specs=VMEM,
        compiler_params=params(),
        name="merge",
    )(a, b, *after)


def hold_kernel(*refs):
    pass


def hold(value, after, flops=0):
    return pl.pallas_call(
        hold_kernel,
        out_shape=jax.ShapeDtypeStruct(value.shape, value.dtype),
        in_specs=[HBM] * (1 + len(after)),
        out_specs=HBM,
        input_output_aliases={0: 0},
        compiler_params=params(),
        cost_estimate=pl.CostEstimate(flops=flops, bytes_accessed=0, transcendentals=0),
        name="hold",
    )(value, *after)


def cut_kernel(near_ref, far_ref, *refs):
    low_ref, high_ref, sems = refs[-3:]
    half = low_ref.shape[0]
    copies = [
        pltpu.make_async_copy(far_ref.at[pl.ds(0, half), :], low_ref, sems.at[0]),
        pltpu.make_async_copy(near_ref.at[pl.ds(half, half), :], high_ref, sems.at[1]),
    ]
    for copy in copies:
        copy.start()
    for copy in copies:
        copy.wait()


def relay(near, far, after):
    half = jax.ShapeDtypeStruct((near.shape[0] // 2,) + near.shape[1:], near.dtype)
    low, high = pl.pallas_call(
        cut_kernel,
        out_shape=[half] * 2,
        in_specs=[HBM] * (2 + len(after)),
        out_specs=[HBM] * 2,
        scratch_shapes=[pltpu.SemaphoreType.DMA((2,))],
        compiler_params=params(),
        name="cut",
    )(near, far, *after)
    return [exchange(low, "mp", 1), exchange(high, "mp", 2)]


def ask_around(wanted):
    asked, step = [wanted], 1
    while step < lax.axis_size("dp"):
        got = exchange(jnp.concatenate(asked), "dp", step)
        asked = asked + jnp.split(got, step)
        step = 2 * step
    return asked


def gather_in(blocks, first, last):
    blocks, step = dict(enumerate(blocks)), 1
    while step < lax.axis_size("dp"):
        at_end = 2 * step == lax.axis_size("dp")
        for k in sorted((k for k in blocks if k & step), reverse=True):
            got = exchange(blocks.pop(k), "dp", step)
            after = last if at_end else first
            blocks[k ^ step] = merge(blocks[k ^ step], got, after)
            first = [blocks[k ^ step]]
        step = 2 * step
    return blocks[0]


def prepare_kernel(seg_ref, neigh_ref, mask_ref, share_ref):
    phase, rows, imps = lax.axis_index("phase"), mask_ref.shape[0], share_ref.shape[0]
    seg = seg_ref[0, pl.ds(phase, 1), :]
    at_row = lax.broadcasted_iota(jnp.int32, (rows, rows), 0)
    at_col = lax.broadcasted_iota(jnp.int32, (rows, rows), 1)
    allowed = (at_col <= at_row) & (columns_of(seg, rows) == seg)
    mask_ref[...] = jnp.where(allowed, 1.0 / rows, 0.0)
    near = neigh_ref[phase]
    row = lax.broadcasted_iota(jnp.int32, (rows, imps), 0)
    share = jnp.zeros((rows, imps), F32)
    for n in range(NBR):
        share = share + jnp.where(near[n : n + 1, :] == row, 1.0 / NBR, 0.0)
    share_ref[...] = jnp.transpose(share).astype(BF16)


def prepare(segments, neigh):
    rows, imps = segments.shape[2], neigh.shape[2]
    return pl.pallas_call(
        prepare_kernel,
        out_shape=[
            jax.ShapeDtypeStruct((rows, rows), F32),
            jax.ShapeDtypeStruct((imps, rows), BF16),
        ],
        in_specs=[VMEM] * 2,
        out_specs=[VMEM] * 2,
        compiler_params=params(),
        cost_estimate=pl.CostEstimate(
            flops=16 * rows * imps, bytes_accessed=8 * rows * rows, transcendentals=0
        ),
        name="prepare",
    )(segments, neigh)


def by_phase(body, zero, one):
    phase = lax.axis_index("phase")
    pl.when(phase == 0)(functools.partial(body, *zero))
    pl.when(phase != 0)(functools.partial(body, *one))


def front(x, mask_ref, w_ref, gated_ref):
    local_cols = w_ref.shape[2]
    xf = x.astype(F32)
    inv = lax.rsqrt(jnp.mean(xf * xf, axis=-1, keepdims=True) + EPS)
    proj = []
    for g in range(4):
        raw = jnp.dot(x, w_ref[g], preferred_element_type=F32)
        proj.append(silu(raw * inv).astype(BF16))
    gates, values, queries, keys = proj
    mask = mask_ref[...]
    for h in range(0, local_cols, HD):
        head = slice(h, h + HD)
        scores = lax.dot_general(
            queries[:, head], keys[:, head], (((1,), (1,)), ((), ())), preferred_element_type=F32
        ) * HD ** (-0.5)
        weights = (silu(scores) * mask).astype(BF16)
        mixed = jnp.dot(weights, values[:, head], preferred_element_type=F32)
        mixed = mixed * lax.rsqrt(jnp.mean(mixed * mixed, axis=-1, keepdims=True) + EPS)
        gated_ref[:, head] = (mixed * gates[:, head].astype(F32)).astype(BF16)


def back(x, gated_refs, o_refs):
    total, at = x.astype(F32), 0
    for o_ref in o_refs:
        steps, cols, width = o_ref.shape
        gated = jnp.concatenate([ref[...] for ref in gated_refs[at : at + steps]], axis=1)
        weights = o_ref[...].reshape(steps * cols, width)
        total = total + jnp.dot(gated, weights, preferred_element_type=F32)
        at += steps
    return total.astype(BF16)


def stack_copies(pieces, places, stack_ref, sems):
    copies = []
    for n, (k, row) in enumerate(places):
        at = stack_ref.at[k, pl.ds(row, pieces[n].shape[0]), :]
        copies.append(pltpu.make_async_copy(pieces[n], at, sems.at[n]))
    return copies


def stack_kernel(places, *refs):
    copies = stack_copies(refs[: len(places)], places, refs[-2], refs[-1])
    for copy in copies:
        copy.start()
    for copy in copies:
        copy.wait()


def stack(pieces, places, count, after):
    rows, width = sum(piece.shape[0] for piece in pieces) // count, pieces[0].shape[1]
    return pl.pallas_call(
        functools.partial(stack_kernel, places),
        out_shape=jax.ShapeDtypeStruct((count, rows, width), BF16),
        in_specs=[HBM] * (len(pieces) + len(after)),
        out_specs=HBM,
        scratch_shapes=[pltpu.SemaphoreType.DMA((len(places),))],
        compiler_params=params(),
        name="stack",
    )(*pieces, *after)


def first_kernel(steps, places, *refs):
    x_refs, pieces, refs = refs[:steps], refs[steps : steps + len(places)], refs[steps + len(places) :]
    mask_ref, w_own, w_other, gated_ref, x_ref, stack_ref, sems = refs
    copies = stack_copies(pieces, places, stack_ref, sems)
    for copy in copies:
        copy.start()
    width = x_refs[0].shape[1]
    for k, piece in enumerate(x_refs):
        at = pl.multiple_of(source_of(lax.axis_index("mp"), k, steps) * width, width)
        x_ref[:, pl.ds(at, width)] = piece[...]

    def body(w_ref):
        front(x_ref[...], mask_ref, w_ref, gated_ref)

    by_phase(body, [w_own], [w_other])
    for copy in copies:
        copy.wait()


def middle_kernel(steps, parts, *refs):
    gated_refs, refs = refs[:steps], refs[steps:]
    x_ref, mask_ref, w_own, w_other = refs[:4]
    o_own, o_other = refs[4 : 4 + parts], refs[4 + parts : 4 + 2 * parts]
    gated_ref, x1_ref = refs[-2:]

    def body(w_ref, *o_refs):
        x1 = back(x_ref[...], gated_refs, o_refs)
        x1_ref[...] = x1
        front(x1, mask_ref, w_ref, gated_ref)

    by_phase(body, (w_other, *o_own), (w_own, *o_other))


def last_kernel(steps, parts, *refs):
    gated_refs, refs = refs[:steps], refs[steps:]
    x_ref, share_ref, w_ref, bias_ref = refs[:4]
    o_own, o_other = refs[4 : 4 + parts], refs[4 + parts : 4 + 2 * parts]
    out_ref, ctx_ref, states_ref, sem = refs[-4:]
    copy = pltpu.make_async_copy(states_ref, out_ref, sem)

    def body(*o_refs):
        states_ref[...] = back(x_ref[...], gated_refs, o_refs)

    by_phase(body, o_other, o_own)
    copy.start()
    context = jnp.dot(share_ref[...], states_ref[...], preferred_element_type=F32).astype(BF16)
    summed = jnp.dot(context, w_ref[...], preferred_element_type=F32)
    ctx_ref[...] = silu(summed + bias_ref[...].astype(F32)).astype(BF16)
    copy.wait()


def section_flops(rows, width, local_cols):
    return 2 * rows * (width * 4 * local_cols + 2 * rows * local_cols)


def fetch_rows_padded(owners, item_row, table, width):
    dp_count = lax.axis_size("dp")
    row_total = item_row.shape[0]
    capacity = max(2, 7 * row_total // (4 * dp_count))
    hits = (owners[:, None] == jnp.arange(dp_count, dtype=jnp.int32)[None, :]).astype(jnp.int32)
    rank = jnp.sum((jnp.cumsum(hits, axis=0) - 1) * hits, axis=1)
    slot = owners * capacity + rank
    requests = jnp.full((dp_count * capacity,), -1, jnp.int32).at[slot].set(item_row)
    asked = swap(requests.reshape(dp_count, capacity), "dp")
    part = lax.dynamic_slice_in_dim(table, lax.axis_index("mp") * width, width, 1)
    found = jnp.take(part, jnp.maximum(asked, 0), axis=0)
    return swap(found, "dp").reshape(dp_count * capacity, width)[slot]


def on_device(
    item_owner, item_row, segments, neighbors, table, gains, w_in, w_out, w_ctx, ctx_bias
):
    dp_count, mp_count = lax.axis_size("dp"), lax.axis_size("mp")
    table_rows, width = table.shape
    batches, rows = segments.shape[1], segments.shape[2]
    imps = neighbors.shape[2]
    local_cols = w_out.shape[1]
    part = width // mp_count

    w_own = jnp.transpose(w_in[0], (1, 0, 2)) * gains[0][None, :, None]
    relayed = mp_count == 4
    direct = range(1, 3 if relayed else mp_count)
    pieces = [w_out[0]] + [exchange(w_out[0], "mp", k) for k in direct]
    places = [(k, 0) for k in range(len(pieces))]
    corner = [(0, 0), (0, local_cols // 2)]
    neigh = jnp.transpose(neighbors[0], (0, 2, 1))
    bias = ctx_bias.reshape(1, -1)
    mask, share = prepare(segments, neigh)

    if is_pow2(dp_count) and dp_count <= 8:
        wanted = jnp.concatenate([item_owner.reshape(-1, LANES), item_row.reshape(-1, LANES)])
        asked = ask_around(wanted)
        w_own = hold(w_own, asked[1:2])
        w_other = exchange(w_own, "phase", 1)
        late = fetch(asked[-1:], batches, table, part, [])
        found = fetch(asked[:-1], batches, table, part, late) + late

        piece = gather_in(found, [], [w_other])
    else:
        piece = fetch_rows_padded(item_owner[:, 0], item_row, table, part)
        piece = lax.dynamic_index_in_dim(
            piece.reshape(batches, rows, part), lax.axis_index("phase"), 0, keepdims=False
        )
        w_other = exchange(w_own, "phase", 1)
    x_pieces = spread(piece, "mp")

    x_shape = jax.ShapeDtypeStruct((rows, width), BF16)
    gated_shape = jax.ShapeDtypeStruct((rows, local_cols), BF16)
    front_flops = section_flops(rows, width, local_cols)
    back_flops = 2 * rows * width * local_cols * mp_count

    gated, x0, o_own = pl.pallas_call(
        functools.partial(first_kernel, mp_count, places),
        out_shape=[
            gated_shape,
            x_shape,
            jax.ShapeDtypeStruct((len(pieces), local_cols, width), BF16),
        ],
        in_specs=[VMEM] * mp_count + [HBM] * len(places) + [VMEM] * 3,
        out_specs=[VMEM] * 2 + [HBM],
        scratch_shapes=[pltpu.SemaphoreType.DMA((len(places),))],
        compiler_params=params(),
        cost_estimate=pl.CostEstimate(
            flops=1 * front_flops, bytes_accessed=8 * width * local_cols, transcendentals=0
        ),
        name="section0_front",
    )(*x_pieces, *pieces, mask, w_own, w_other)
    o_own = [o_own]
    if relayed:
        o_own.append(stack(relay(*pieces[1:], [piece]), corner, 1, []))
    o_other = [exchange(block, "phase", 1) for block in o_own]

    arrived = spread(gated, "mp")
    arrived[-1] = hold(arrived[-1], arrived[1:-1], 32 * front_flops)
    gated, x1 = pl.pallas_call(
        functools.partial(middle_kernel, mp_count, len(o_own)),
        out_shape=[gated_shape, x_shape],
        in_specs=[VMEM] * (mp_count + 4 + 2 * len(o_own)),
        out_specs=[VMEM] * 2,
        compiler_params=params(),
        cost_estimate=pl.CostEstimate(
            flops=front_flops + back_flops,
            bytes_accessed=(8 + 2 * mp_count) * width * local_cols,
            transcendentals=0,
        ),
        name="section0_back_section1_front",
    )(*arrived, x0, mask, w_own, w_other, *o_own, *o_other)

    states, ctx = pl.pallas_call(
        functools.partial(last_kernel, mp_count, len(o_own)),
        out_shape=[x_shape, jax.ShapeDtypeStruct((imps, w_ctx.shape[1]), BF16)],
        in_specs=[VMEM] * (mp_count + 4 + 2 * len(o_own)),
        out_specs=[HBM, VMEM],
        scratch_shapes=[pltpu.VMEM((rows, width), BF16), pltpu.SemaphoreType.DMA],
        compiler_params=params(),
        cost_estimate=pl.CostEstimate(
            flops=back_flops + 2 * imps * width * (rows + w_ctx.shape[1]),
            bytes_accessed=2 * mp_count * width * local_cols,
            transcendentals=0,
        ),
        name="section1_back_context",
    )(*spread(gated, "mp"), x1, share, w_ctx, bias, *o_own, *o_other)

    return (
        states.reshape(1, 1, rows, width),
        ctx.reshape(1, 1, imps, w_ctx.shape[1]),
    )


def solution(mesh):
    in_specs = (
        P("dp", None),
        P("dp"),
        P("dp", None, None),
        P("dp", None, None, None),
        P("dp", None),
        P("phase", None),
        P("phase", None, None, "mp"),
        P("phase", "mp", None),
        P(None, "mp"),
        P("mp"),
    )
    out_specs = (P("dp", "phase", None, None), P("dp", "phase", None, "mp"))
    return jax.shard_map(
        on_device, mesh=mesh, in_specs=in_specs, out_specs=out_specs, check_vma=False
    )
```

```python
import functools

import jax
import jax.numpy as jnp
from jax import lax
from jax.experimental import pallas as pl
from jax.experimental.pallas import tpu as pltpu
from jax.sharding import PartitionSpec as P

HD = 128
NBR = 8
LANES = 128
EPS = 1e-06
VMEM_LIMIT = 20 * 1024 * 1024
VMEM = pl.BlockSpec(memory_space=pltpu.VMEM)
HBM = pl.BlockSpec(memory_space=pltpu.HBM)
F32 = jnp.float32
BF16 = jnp.bfloat16


def params():
    return pltpu.CompilerParams(vmem_limit_bytes=VMEM_LIMIT)


def is_pow2(n):
    return n & (n - 1) == 0


def source_of(me, k, n):
    return me ^ k if is_pow2(n) else lax.rem(me + n - k, n)


def exchange(value, axis, k):
    n = lax.axis_size(axis)
    pairs = [(i, i ^ k if is_pow2(n) else (i + k) % n) for i in range(n)]
    return lax.ppermute(value, axis, pairs)


def spread(value, axis):
    return [value] + [exchange(value, axis, k) for k in range(1, lax.axis_size(axis))]


def swap(blocks, axis):
    return lax.all_to_all(blocks, axis, split_axis=0, concat_axis=0, tiled=True)


def columns_of(row, count):
    return jnp.transpose(jnp.broadcast_to(row, (count, row.shape[1])))


def silu(x):
    return x * jax.nn.sigmoid(x)


def fetch_kernel(steps, batches, *refs):
    asked_refs, table_ref = refs[:steps], refs[steps]
    out_refs, width = refs[-steps:], refs[-1].shape[1]
    me = lax.axis_index("dp")
    phase = lax.axis_index("phase")
    hots = []
    for asked_ref in asked_refs:
        half = asked_ref.shape[0] // 2
        per = half // batches
        cols = []
        for n in range(per):
            at = phase * per + n
            mine = asked_ref[pl.ds(at, 1), :] == me
            row = jnp.where(mine, asked_ref[pl.ds(half + at, 1), :], -1)
            cols.append(columns_of(row, LANES))
        cols = jnp.concatenate(cols)
        lane = lax.broadcasted_iota(jnp.int32, cols.shape, 1)
        hots.append(
            jnp.concatenate(
                [
                    jnp.where(cols == lane + c, 1.0, 0.0).astype(BF16)
                    for c in range(0, table_ref.shape[0], LANES)
                ],
                axis=1,
            )
        )
    held = table_ref[:, pl.ds(pl.multiple_of(lax.axis_index("mp") * width, width), width)]
    for hot, out_ref in zip(hots, out_refs):
        out_ref[...] = jnp.dot(hot, held, preferred_element_type=F32).astype(BF16)


def fetch(asked, batches, table, width, after):
    steps, rows = len(asked), asked[0].size // (2 * batches)
    return pl.pallas_call(
        functools.partial(fetch_kernel, steps, batches),
        out_shape=[jax.ShapeDtypeStruct((rows, width), BF16)] * steps,
        in_specs=[VMEM] * (steps + 1) + [HBM] * len(after),
        out_specs=[VMEM] * steps,
        compiler_params=params(),
        cost_estimate=pl.CostEstimate(
            flops=2 * steps * rows * width * table.shape[0],
            bytes_accessed=2 * width * table.shape[0],
            transcendentals=0,
        ),
        name="fetch",
    )(*asked, table, *after)


def merge_kernel(a_ref, b_ref, *refs):
    refs[-1][...] = a_ref[...] + b_ref[...]


def merge(a, b, after):
    return pl.pallas_call(
        merge_kernel,
        out_shape=jax.ShapeDtypeStruct(a.shape, BF16),
        in_specs=[VMEM] * 2 + [HBM] * len(after),
        out_specs=VMEM,
        compiler_params=params(),
        name="merge",
    )(a, b, *after)


def hold_kernel(*refs):
    pass


def hold(value, after, flops=0):
    return pl.pallas_call(
        hold_kernel,
        out_shape=jax.ShapeDtypeStruct(value.shape, value.dtype),
        in_specs=[HBM] * (1 + len(after)),
        out_specs=HBM,
        input_output_aliases={0: 0},
        compiler_params=params(),
        cost_estimate=pl.CostEstimate(flops=flops, bytes_accessed=0, transcendentals=0),
        name="hold",
    )(value, *after)


def cut_kernel(near_ref, far_ref, *refs):
    low_ref, high_ref, sems = refs[-3:]
    half = low_ref.shape[0]
    copies = [
        pltpu.make_async_copy(far_ref.at[pl.ds(0, half), :], low_ref, sems.at[0]),
        pltpu.make_async_copy(near_ref.at[pl.ds(half, half), :], high_ref, sems.at[1]),
    ]
    for copy in copies:
        copy.start()
    for copy in copies:
        copy.wait()


def relay(near, far, after):
    half = jax.ShapeDtypeStruct((near.shape[0] // 2,) + near.shape[1:], near.dtype)
    low, high = pl.pallas_call(
        cut_kernel,
        out_shape=[half] * 2,
        in_specs=[HBM] * (2 + len(after)),
        out_specs=[HBM] * 2,
        scratch_shapes=[pltpu.SemaphoreType.DMA((2,))],
        compiler_params=params(),
        name="cut",
    )(near, far, *after)
    return [exchange(low, "mp", 1), exchange(high, "mp", 2)]


def ask_around(wanted):
    asked, step = [wanted], 1
    while step < lax.axis_size("dp"):
        got = exchange(jnp.concatenate(asked), "dp", step)
        asked = asked + jnp.split(got, step)
        step = 2 * step
    return asked


def gather_in(blocks, first, last):
    blocks, step = dict(enumerate(blocks)), 1
    while step < lax.axis_size("dp"):
        at_end = 2 * step == lax.axis_size("dp")
        for k in sorted((k for k in blocks if k & step), reverse=True):
            got = exchange(blocks.pop(k), "dp", step)
            after = last if at_end else first
            blocks[k ^ step] = merge(blocks[k ^ step], got, after)
            first = [blocks[k ^ step]]
        step = 2 * step
    return blocks[0]


def prepare_kernel(seg_ref, neigh_ref, mask_ref, share_ref):
    phase, rows, imps = lax.axis_index("phase"), mask_ref.shape[0], share_ref.shape[0]
    seg = seg_ref[0, pl.ds(phase, 1), :]
    at_row = lax.broadcasted_iota(jnp.int32, (rows, rows), 0)
    at_col = lax.broadcasted_iota(jnp.int32, (rows, rows), 1)
    allowed = (at_col <= at_row) & (columns_of(seg, rows) == seg)
    mask_ref[...] = jnp.where(allowed, 1.0 / rows, 0.0)
    near = neigh_ref[phase]
    row = lax.broadcasted_iota(jnp.int32, (rows, imps), 0)
    share = jnp.zeros((rows, imps), F32)
    for n in range(NBR):
        share = share + jnp.where(near[n : n + 1, :] == row, 1.0 / NBR, 0.0)
    share_ref[...] = jnp.transpose(share).astype(BF16)


def prepare(segments, neigh):
    rows, imps = segments.shape[2], neigh.shape[2]
    return pl.pallas_call(
        prepare_kernel,
        out_shape=[
            jax.ShapeDtypeStruct((rows, rows), F32),
            jax.ShapeDtypeStruct((imps, rows), BF16),
        ],
        in_specs=[VMEM] * 2,
        out_specs=[VMEM] * 2,
        compiler_params=params(),
        cost_estimate=pl.CostEstimate(
            flops=16 * rows * imps, bytes_accessed=8 * rows * rows, transcendentals=0
        ),
        name="prepare",
    )(segments, neigh)


def by_phase(body, zero, one):
    phase = lax.axis_index("phase")
    pl.when(phase == 0)(functools.partial(body, *zero))
    pl.when(phase != 0)(functools.partial(body, *one))


def front(x, mask_ref, w_ref, gated_ref):
    local_cols = w_ref.shape[2]
    xf = x.astype(F32)
    inv = lax.rsqrt(jnp.mean(xf * xf, axis=-1, keepdims=True) + EPS)
    proj = []
    for g in range(4):
        raw = jnp.dot(x, w_ref[g], preferred_element_type=F32)
        proj.append(silu(raw * inv).astype(BF16))
    gates, values, queries, keys = proj
    mask = mask_ref[...]
    for h in range(0, local_cols, HD):
        head = slice(h, h + HD)
        scores = lax.dot_general(
            queries[:, head], keys[:, head], (((1,), (1,)), ((), ())), preferred_element_type=F32
        ) * HD ** (-0.5)
        weights = (silu(scores) * mask).astype(BF16)
        mixed = jnp.dot(weights, values[:, head], preferred_element_type=F32)
        mixed = mixed * lax.rsqrt(jnp.mean(mixed * mixed, axis=-1, keepdims=True) + EPS)
        gated_ref[:, head] = (mixed * gates[:, head].astype(F32)).astype(BF16)


def back(x, gated_refs, o_refs):
    total, at = x.astype(F32), 0
    for o_ref in o_refs:
        steps, cols, width = o_ref.shape
        gated = jnp.concatenate([ref[...] for ref in gated_refs[at : at + steps]], axis=1)
        weights = o_ref[...].reshape(steps * cols, width)
        total = total + jnp.dot(gated, weights, preferred_element_type=F32)
        at += steps
    return total.astype(BF16)


def stack_copies(pieces, places, stack_ref, sems):
    copies = []
    for n, (k, row) in enumerate(places):
        at = stack_ref.at[k, pl.ds(row, pieces[n].shape[0]), :]
        copies.append(pltpu.make_async_copy(pieces[n], at, sems.at[n]))
    return copies


def stack_kernel(places, *refs):
    copies = stack_copies(refs[: len(places)], places, refs[-2], refs[-1])
    for copy in copies:
        copy.start()
    for copy in copies:
        copy.wait()


def stack(pieces, places, count, after):
    rows, width = sum(piece.shape[0] for piece in pieces) // count, pieces[0].shape[1]
    return pl.pallas_call(
        functools.partial(stack_kernel, places),
        out_shape=jax.ShapeDtypeStruct((count, rows, width), BF16),
        in_specs=[HBM] * (len(pieces) + len(after)),
        out_specs=HBM,
        scratch_shapes=[pltpu.SemaphoreType.DMA((len(places),))],
        compiler_params=params(),
        name="stack",
    )(*pieces, *after)


def first_kernel(steps, places, *refs):
    x_refs, pieces, refs = refs[:steps], refs[steps : steps + len(places)], refs[steps + len(places) :]
    mask_ref, w_own, w_other, gated_ref, x_ref, stack_ref, sems = refs
    copies = stack_copies(pieces, places, stack_ref, sems)
    for copy in copies:
        copy.start()
    width = x_refs[0].shape[1]
    for k, piece in enumerate(x_refs):
        at = pl.multiple_of(source_of(lax.axis_index("mp"), k, steps) * width, width)
        x_ref[:, pl.ds(at, width)] = piece[...]

    def body(w_ref):
        front(x_ref[...], mask_ref, w_ref, gated_ref)

    by_phase(body, [w_own], [w_other])
    for copy in copies:
        copy.wait()


def middle_kernel(steps, parts, *refs):
    gated_refs, refs = refs[:steps], refs[steps:]
    x_ref, mask_ref, w_own, w_other = refs[:4]
    o_own, o_other = refs[4 : 4 + parts], refs[4 + parts : 4 + 2 * parts]
    gated_ref, x1_ref = refs[-2:]

    def body(w_ref, *o_refs):
        x1 = back(x_ref[...], gated_refs, o_refs)
        x1_ref[...] = x1
        front(x1, mask_ref, w_ref, gated_ref)

    by_phase(body, (w_other, *o_own), (w_own, *o_other))


def last_kernel(steps, parts, *refs):
    gated_refs, refs = refs[:steps], refs[steps:]
    x_ref, share_ref, w_ref, bias_ref = refs[:4]
    o_own, o_other = refs[4 : 4 + parts], refs[4 + parts : 4 + 2 * parts]
    states_ref, ctx_ref = refs[-2:]

    def body(*o_refs):
        states = back(x_ref[...], gated_refs, o_refs)
        states_ref[...] = states
        context = jnp.dot(share_ref[...], states, preferred_element_type=F32).astype(BF16)
        summed = jnp.dot(context, w_ref[...], preferred_element_type=F32)
        ctx_ref[...] = silu(summed + bias_ref[...].astype(F32)).astype(BF16)

    by_phase(body, o_other, o_own)


def section_flops(rows, width, local_cols):
    return 2 * rows * (width * 4 * local_cols + 2 * rows * local_cols)


def fetch_rows_padded(owners, item_row, table, width):
    dp_count = lax.axis_size("dp")
    row_total = item_row.shape[0]
    capacity = max(2, 7 * row_total // (4 * dp_count))
    hits = (owners[:, None] == jnp.arange(dp_count, dtype=jnp.int32)[None, :]).astype(jnp.int32)
    rank = jnp.sum((jnp.cumsum(hits, axis=0) - 1) * hits, axis=1)
    slot = owners * capacity + rank
    requests = jnp.full((dp_count * capacity,), -1, jnp.int32).at[slot].set(item_row)
    asked = swap(requests.reshape(dp_count, capacity), "dp")
    part = lax.dynamic_slice_in_dim(table, lax.axis_index("mp") * width, width, 1)
    found = jnp.take(part, jnp.maximum(asked, 0), axis=0)
    return swap(found, "dp").reshape(dp_count * capacity, width)[slot]


def on_device(
    item_owner, item_row, segments, neighbors, table, gains, w_in, w_out, w_ctx, ctx_bias
):
    dp_count, mp_count = lax.axis_size("dp"), lax.axis_size("mp")
    table_rows, width = table.shape
    batches, rows = segments.shape[1], segments.shape[2]
    imps = neighbors.shape[2]
    local_cols = w_out.shape[1]
    part = width // mp_count

    w_own = jnp.transpose(w_in[0], (1, 0, 2)) * gains[0][None, :, None]
    relayed = mp_count == 4
    direct = range(1, 3 if relayed else mp_count)
    pieces = [w_out[0]] + [exchange(w_out[0], "mp", k) for k in direct]
    places = [(k, 0) for k in range(len(pieces))]
    corner = [(0, 0), (0, local_cols // 2)]
    neigh = jnp.transpose(neighbors[0], (0, 2, 1))
    bias = ctx_bias.reshape(1, -1)
    mask, share = prepare(segments, neigh)

    if is_pow2(dp_count) and dp_count <= 8:
        wanted = jnp.concatenate([item_owner.reshape(-1, LANES), item_row.reshape(-1, LANES)])
        asked = ask_around(wanted)
        w_own = hold(w_own, asked[1:2])
        w_other = exchange(w_own, "phase", 1)
        late = fetch(asked[-1:], batches, table, part, [])
        found = fetch(asked[:-1], batches, table, part, late) + late

        piece = gather_in(found, [], [w_other])
    else:
        piece = fetch_rows_padded(item_owner[:, 0], item_row, table, part)
        piece = lax.dynamic_index_in_dim(
            piece.reshape(batches, rows, part), lax.axis_index("phase"), 0, keepdims=False
        )
        w_other = exchange(w_own, "phase", 1)
    x_pieces = spread(piece, "mp")

    x_shape = jax.ShapeDtypeStruct((rows, width), BF16)
    gated_shape = jax.ShapeDtypeStruct((rows, local_cols), BF16)
    front_flops = section_flops(rows, width, local_cols)
    back_flops = 2 * rows * width * local_cols * mp_count

    gated, x0, o_own = pl.pallas_call(
        functools.partial(first_kernel, mp_count, places),
        out_shape=[
            gated_shape,
            x_shape,
            jax.ShapeDtypeStruct((len(pieces), local_cols, width), BF16),
        ],
        in_specs=[VMEM] * mp_count + [HBM] * len(places) + [VMEM] * 3,
        out_specs=[VMEM] * 2 + [HBM],
        scratch_shapes=[pltpu.SemaphoreType.DMA((len(places),))],
        compiler_params=params(),
        cost_estimate=pl.CostEstimate(
            flops=1 * front_flops, bytes_accessed=8 * width * local_cols, transcendentals=0
        ),
        name="section0_front",
    )(*x_pieces, *pieces, mask, w_own, w_other)
    o_own = [o_own]
    if relayed:
        o_own.append(stack(relay(*pieces[1:], x_pieces[1:2]), corner, 1, []))
    o_other = [exchange(block, "phase", 1) for block in o_own]

    arrived = spread(gated, "mp")
    arrived[-1] = hold(arrived[-1], arrived[1:-1], 32 * front_flops)
    gated, x1 = pl.pallas_call(
        functools.partial(middle_kernel, mp_count, len(o_own)),
        out_shape=[gated_shape, x_shape],
        in_specs=[VMEM] * (mp_count + 4 + 2 * len(o_own)),
        out_specs=[VMEM] * 2,
        compiler_params=params(),
        cost_estimate=pl.CostEstimate(
            flops=front_flops + back_flops,
            bytes_accessed=(8 + 2 * mp_count) * width * local_cols,
            transcendentals=0,
        ),
        name="section0_back_section1_front",
    )(*arrived, x0, mask, w_own, w_other, *o_own, *o_other)

    states, ctx = pl.pallas_call(
        functools.partial(last_kernel, mp_count, len(o_own)),
        out_shape=[x_shape, jax.ShapeDtypeStruct((imps, w_ctx.shape[1]), BF16)],
        in_specs=[VMEM] * (mp_count + 4 + 2 * len(o_own)),
        out_specs=[VMEM] * 2,
        compiler_params=params(),
        cost_estimate=pl.CostEstimate(
            flops=back_flops + 2 * imps * width * (rows + w_ctx.shape[1]),
            bytes_accessed=2 * mp_count * width * local_cols,
            transcendentals=0,
        ),
        name="section1_back_context",
    )(*spread(gated, "mp"), x1, share, w_ctx, bias, *o_own, *o_other)

    return (
        states.reshape(1, 1, rows, width),
        ctx.reshape(1, 1, imps, w_ctx.shape[1]),
    )


def solution(mesh):
    in_specs = (
        P("dp", None),
        P("dp"),
        P("dp", None, None),
        P("dp", None, None, None),
        P("dp", None),
        P("phase", None),
        P("phase", None, None, "mp"),
        P("phase", "mp", None),
        P(None, "mp"),
        P("mp"),
    )
    out_specs = (P("dp", "phase", None, None), P("dp", "phase", None, "mp"))
    return jax.shard_map(
        on_device, mesh=mesh, in_specs=in_specs, out_specs=out_specs, check_vma=False
    )
```
